32 devices in a mesh: grp: 8 (over z, x), crm: 4 (over y, core).
Axes of the slice: x: 2, y: 2, z: 4, core: 2. Of those that a mesh axis runs over, the one named last changes fastest.
Arguments:
- crm_state: float32 [1152, 3, 3712], P(('grp', 'crm')), may hold values from -6 to 6
- forcing: float32 [768, 2, 72], P(('grp', 'crm')), may hold values from -6 to 6
- target: int32 [768], P(('grp', 'crm')), may hold values from 0 to 3, as said below
- cost_class: int32 [768], P(('grp', 'crm')), may hold values from 1 to 3
- level_map: float32 [58, 72], replicated, may hold values from 0 to 0.4, as said below
- remap_index: int32 [768, 4], P(('grp', 'crm')), may hold values from 0 to 71, as said below
- remap_weight: float32 [768, 4], P(('grp', 'crm')), may hold values from 0.2 to 1
Outputs:
- new_state: float32 [1152, 3, 3712], P(('grp', 'crm'))
- cloud_water: float32 [768, 3712], P(('grp', 'crm'))
- physics_tendency: float32 [768, 2, 72], P(('grp', 'crm'))
The draws below stay inside these ranges and needn't reach their ends.
Inputs may be any that keep to these rules, and one draw needn't show every extreme that they name: `target`: of one owner device's columns at most 9 name the same worker; in every group one worker receives exactly 9 columns from each of the group's 4 owners. `remap_index`: entry 0 names a column of the block before the cell's own, entry 1 one of its own block (offset 24), entry 2 one of the block after (offset 2 * 24), entry 3 any of the three. `level_map`: zero except within two GCM levels of the level nearest to each model level.
All inputs are finite; a program needn't handle non-finite values.
Results may differ from the reference program's by a relative error of at most 0.0003.
Values sent between devices are 32-bit elements; how exact they have to be, the bound alone decides.
No kernel may reach another device: no remote copies, remote signals or barrier semaphores. Data moves between devices by JAX's collectives and lax.ppermute only.
A program may use at most 64 MiB of HBM per device.

```python
import math
import jax
import jax.numpy as jnp
from jax import lax

NX = 64
NZ = 58
LEV = 72
COL_DEV = 24
CLASSES = 3
SUB = 4
NB = 4
CAP = 9
SLOTS_DEV = 36
CELLS = 3712
COLUMNS = 768
SLOTS = 1152
N_CRM = 4


def draw_target(key, part):
    key = jax.random.fold_in(key, 11)
    device_count = COLUMNS // COL_DEV
    group_count = device_count // N_CRM
    pool_size = N_CRM * CAP
    key_hot, key_order, key_shuffle = jax.random.split(key, 3)
    hot_worker = jax.random.randint(key_hot, (group_count,), 0, N_CRM)
    hot_device = jnp.repeat(hot_worker, N_CRM)
    pool = jnp.repeat(jnp.arange(N_CRM), CAP)
    spread = jnp.arange(pool_size)
    scores = jax.random.randint(key_order, (device_count, pool_size), 0, 1 << 16) * pool_size + spread[None, :]
    scores = jnp.where(pool[None, :] == hot_device[:, None], spread[None, :] - pool_size, scores)
    order = jnp.argsort(scores, axis=1)
    chosen = pool[order][:, :COL_DEV]
    shuffle_scores = jax.random.randint(key_shuffle, (device_count, COL_DEV), 0, 1 << 16) * COL_DEV + jnp.arange(COL_DEV)[None, :]
    shuffled = jnp.take_along_axis(chosen, jnp.argsort(shuffle_scores, axis=1), axis=1)
    return shuffled.reshape(-1).astype(jnp.int32)


def draw_remap_index(key, part):
    key = jax.random.fold_in(key, 23)
    keys = jax.random.split(key, 4)
    first = jax.random.randint(keys[0], (COLUMNS,), 0, COL_DEV)
    second = jax.random.randint(keys[1], (COLUMNS,), COL_DEV, 2 * COL_DEV)
    third = jax.random.randint(keys[2], (COLUMNS,), 2 * COL_DEV, 3 * COL_DEV)
    fourth = jax.random.randint(keys[3], (COLUMNS,), 0, 3 * COL_DEV)
    return jnp.stack([first, second, third, fourth], axis=1).astype(jnp.int32)


def draw_level_map(key, part):
    key = jax.random.fold_in(key, 37)
    model_level = jnp.arange(NZ)[:, None]
    gcm_level = jnp.arange(LEV)[None, :]
    nearest = (model_level * LEV + LEV // 2) // NZ
    near = jnp.abs(gcm_level - nearest) <= 2
    values = jax.random.uniform(key, (NZ, LEV), jnp.float32, 0.1, 0.4)
    return jnp.where(near, values, 0.0).astype(jnp.float32)


def set_ends(array, rng, low, top_value):
    longest = array.shape.index(max(array.shape))
    spots = []
    for shift in (0, 1):
        where = [jax.random.randint(jax.random.fold_in(rng, axis), (), 0, length) for axis, length in enumerate(array.shape)]
        where[longest] = (where[longest] + shift) % array.shape[longest]
        spots.append(tuple(where))
    return array.at[spots[0]].set(low).at[spots[1]].set(top_value)


def block_levels(rng, shape, shards, smallest, high):
    loudness = 1.0
    for dim, parts in shards:
        heights = jax.random.uniform(jax.random.fold_in(jax.random.fold_in(rng, 6), dim), (parts,), jnp.float32, smallest / len(shards), high / len(shards))
        loudness = loudness * jnp.repeat(jnp.exp(heights), shape[dim] // parts).reshape((-1,) + (1,) * (len(shape) - 1 - dim))
    return loudness


def scatter_about(key, dims, width, limit, cuts=(), held_as=jnp.bfloat16):
    level = block_levels(key, dims, cuts, -0.22, 0.18) if cuts else 1.0
    entries = jax.random.normal(key, dims, jnp.float32) * width * level
    return jnp.minimum(jnp.maximum(entries, -limit), limit).astype(held_as)


def setup_inputs(seed: int = 0) -> dict:
    arg_keys = jax.random.split(jax.random.key(seed), 8)
    crm_state = scatter_about(arg_keys[0], (SLOTS, 3, CELLS), 1.0, 6.0, ((0, 32),), jnp.float32)
    forcing = scatter_about(arg_keys[1], (COLUMNS, 2, LEV), 1.0, 6.0, ((0, 32),), jnp.float32)
    target = draw_target(jax.random.fold_in(arg_keys[7], 71), 0)
    cost_class = set_ends(jax.random.randint(arg_keys[3], (COLUMNS,), 1, CLASSES + 1), jax.random.fold_in(arg_keys[3], 1), 1, CLASSES).astype(jnp.int32)
    level_map = draw_level_map(jax.random.fold_in(arg_keys[7], 71), 0)
    remap_index = draw_remap_index(jax.random.fold_in(arg_keys[7], 71), 0)
    remap_weight = jnp.clip(jnp.exp(math.log(1.0) - 1.609438 * jax.random.uniform(arg_keys[6], (COLUMNS, NB), jnp.float32) ** block_levels(arg_keys[6], (COLUMNS, NB), ((0, 32),), -0.2, 0.2)), 0.2, 1.0)
    return dict(crm_state=crm_state, forcing=forcing, target=target, cost_class=cost_class, level_map=level_map, remap_index=remap_index, remap_weight=remap_weight)


DIFFUSE_HORIZ = 0.2
DIFFUSE_VERT = 0.1
CONDENSE_RATE = 3.0
LINEAR_DRAG = 0.1
MOIST_BUOYANCY = 0.6


def saturation(level_count):
    levels_idx = jnp.arange(level_count).astype(jnp.float32)
    return 1.0 - 2.0 * (levels_idx + 0.5) / level_count


def vertical_terms(field):
    zeros_row = jnp.zeros_like(field[..., :1, :])
    above = jnp.concatenate([field[..., 1:, :], zeros_row], axis=-2)
    below = jnp.concatenate([zeros_row, field[..., :-1, :]], axis=-2)
    return 0.5 * (above - below), above + below - 2.0 * field


def horizontal_lap(field):
    return jnp.roll(field, 1, -1) + jnp.roll(field, -1, -1) - 2.0 * field


def substep(current, crm_forcing, step_size, saturated):
    theta_field = current[:, 0]
    moist = current[:, 1]
    vertical = current[:, 2]
    step_grid = step_size[:, None, None]
    buoyancy = theta_field + MOIST_BUOYANCY * moist
    condensed = CONDENSE_RATE * jnp.maximum(moist - saturated[:, None], 0.0)
    theta_grad, theta_lapz = vertical_terms(theta_field)
    moist_grad, moist_lapz = vertical_terms(moist)
    vert_grad, vert_lapz = vertical_terms(vertical)
    new_theta = theta_field + step_grid * (-vertical * theta_grad + DIFFUSE_HORIZ * horizontal_lap(theta_field)
                                           + DIFFUSE_VERT * theta_lapz + crm_forcing[:, 0, :, None] + condensed)
    new_moist = moist + step_grid * (-vertical * moist_grad + DIFFUSE_HORIZ * horizontal_lap(moist)
                                     + DIFFUSE_VERT * moist_lapz + crm_forcing[:, 1, :, None] - condensed)
    pushed = vertical + step_grid * (buoyancy - jnp.mean(buoyancy, -1, keepdims=True)
                                     + DIFFUSE_HORIZ * horizontal_lap(vertical) + DIFFUSE_VERT * vert_lapz
                                     - LINEAR_DRAG * vertical)
    new_vertical = pushed - jnp.mean(pushed, -1, keepdims=True)
    return jnp.stack([new_theta, new_moist, new_vertical], axis=1)


def run_models(start, crm_forcing, class_value, total_steps):
    saturated = saturation(start.shape[2])
    steps_here = class_value * SUB
    step_size = 1.0 / jnp.maximum(steps_here, 1.0)

    def advance(index_step, current):
        moved = substep(current, crm_forcing, step_size, saturated)
        live = (index_step.astype(jnp.float32) < steps_here)[:, None, None, None]
        return jnp.where(live, moved, current)

    return lax.fori_loop(0, total_steps, advance, start)


def model_outputs(start, finish):
    saturated = saturation(start.shape[2])
    tendency = jnp.mean(finish[:, :2] - start[:, :2], axis=-1)
    condensate = jnp.maximum(finish[:, 1] - saturated[:, None], 0.0)
    return tendency, condensate.reshape(start.shape[0], -1)


def reference(crm_state, forcing, target, cost_class, level_map, remap_index, remap_weight):
    device_count = COLUMNS // COL_DEV
    group_count = device_count // N_CRM
    owned = target.reshape(device_count, COL_DEV)
    onehot = (owned[:, :, None] == jnp.arange(N_CRM).astype(jnp.int32)[None, None, :]).astype(jnp.int32)
    before = jnp.cumsum(onehot, axis=1) - onehot
    slot_rank = jnp.sum(before * onehot, axis=2)
    owner_ids = jnp.arange(device_count).astype(jnp.int32)[:, None]
    group_ids = owner_ids // N_CRM
    position = owner_ids % N_CRM
    slot = ((group_ids * N_CRM + owned) * SLOTS_DEV + position * CAP + slot_rank).reshape(-1).astype(jnp.int32)
    crm_forcing = jnp.einsum('kj,cvj->cvk', level_map, forcing, precision=lax.Precision.HIGHEST)

    def one_block(pieces):
        slots_here, forcing_here, class_here = pieces
        start = crm_state[slots_here].reshape(-1, 3, NZ, NX)
        finish = run_models(start, forcing_here, class_here.astype(jnp.float32), CLASSES * SUB)
        tendency, condensate = model_outputs(start, finish)
        return finish.reshape(-1, 3, CELLS), tendency, condensate

    finals, tendencies, condensates = lax.map(one_block, (slot.reshape(group_count, -1),
                                                          crm_forcing.reshape(group_count, -1, 2, NZ),
                                                          cost_class.reshape(group_count, -1)))
    new_state = crm_state.at[slot].set(finals.reshape(-1, 3, CELLS))
    gcm_tendency = jnp.einsum('kj,cvk->cvj', level_map, tendencies.reshape(COLUMNS, 2, NZ),
                              precision=lax.Precision.HIGHEST)
    block_ids = (jnp.arange(COLUMNS).astype(jnp.int32) // COL_DEV)[:, None]
    source = ((block_ids + remap_index // COL_DEV - 1) % device_count) * COL_DEV + remap_index % COL_DEV
    picked = gcm_tendency[source.astype(jnp.int32)]
    weighted = jnp.sum(remap_weight[:, :, None, None] * picked, axis=1)
    physics_tendency = weighted / jnp.sum(remap_weight, axis=1)[:, None, None]
    return new_state, condensates.reshape(COLUMNS, CELLS), physics_tendency
```

```python
import functools

import jax
import jax.numpy as jnp
from jax import lax
from jax.experimental import pallas as pl
from jax.experimental.pallas import tpu as pltpu
from jax.sharding import PartitionSpec as P

CLASSES = 3
SUB = 4
DIFFUSE_HORIZ = 0.2
DIFFUSE_VERT = 0.1
CONDENSE_RATE = 3.0
LINEAR_DRAG = 0.1
MOIST_BUOYANCY = 0.6
HIGHEST = lax.Precision.HIGHEST
F32 = jnp.float32
LANES = 128
ROWS = 8
PHASES = 4
MIB = 1 << 20


def iota(shape, axis):
    return lax.broadcasted_iota(jnp.int32, shape, axis)


def dot_t(lhs, rhs):
    return lax.dot_general(lhs, rhs, (((0,), (0,)), ((), ())), precision=HIGHEST, preferred_element_type=F32)


def dot(lhs, rhs):
    return jnp.dot(lhs, rhs, precision=HIGHEST, preferred_element_type=F32)


def all_rows(x):
    x = x + pltpu.roll(x, 4, 0)
    x = x + pltpu.roll(x, 2, 0)
    return x + pltpu.roll(x, 1, 0)


def lanes_of(levels):
    base = 2 * levels
    return base, base + 1, base + 2, base + 3


def pack_kernel(capacity, workers, target, cost, forcing, level_map, rows, counts):
    levels, gcm = level_map.shape
    columns = forcing.shape[0]
    lane_class, lane_slot, lane_column, lane_owner = lanes_of(levels)
    me = lax.axis_index("crm")
    for worker in range(workers):
        counts[worker] = 0
    sub = iota((columns, LANES), 0)
    lane = iota((columns, LANES), 1)
    classes = jnp.zeros((columns, LANES), F32)
    slots = jnp.zeros((columns, LANES), F32)
    for column in range(columns):
        worker = target[column]
        rank = counts[worker]
        counts[worker] = rank + 1
        slot = (worker * workers + me) * capacity + rank
        classes = jnp.where(sub == column, cost[column].astype(F32), classes)
        slots = jnp.where(sub == column, slot.astype(F32), slots)
    spread_row = iota((levels, LANES), 0)
    spread_lane = iota((levels, LANES), 1)
    mapped = jnp.zeros((columns, LANES), F32)
    for variable in range(2):
        place = (spread_lane == spread_row + variable * levels).astype(F32)
        mapped = mapped + dot(forcing[:, variable, :], dot_t(level_map[...], place))
    meta = jnp.where(lane == lane_class, classes, 0.0)
    meta = jnp.where(lane == lane_slot, slots, meta)
    meta = jnp.where(lane == lane_column, (sub + 1).astype(F32), meta)
    meta = jnp.where(lane == lane_owner, me.astype(F32), meta)
    rows[...] = jnp.where(lane < lane_class, mapped, meta)


def pack(target, cost, forcing, level_map, workers, capacity):
    columns = forcing.shape[0]
    return pl.pallas_call(
        functools.partial(pack_kernel, capacity, workers),
        out_shape=jax.ShapeDtypeStruct((columns, LANES), F32),
        in_specs=[pl.BlockSpec(memory_space=pltpu.SMEM)] * 2 + [pl.BlockSpec(memory_space=pltpu.VMEM)] * 2,
        out_specs=pl.BlockSpec(memory_space=pltpu.VMEM),
        scratch_shapes=[pltpu.SMEM((workers,), jnp.int32)],
        name="pack_forcing",
    )(target, cost, forcing, level_map)


def model_kernel(workers, slots, levels, width, *refs):
    row_refs = refs[:workers]
    x_hbm = refs[workers]
    y_hbm, t_ref = refs[workers + 1 : workers + 3]
    cloud_hbm = refs[workers + 3 : 2 * workers + 3]
    (xs, cl, nat, s0, s1, saved, coef, rows_s, meta_v, meta_s, sem_meta, sem_in, sem_out, sem_cloud) = refs[2 * workers + 3 :]
    groups = xs.shape[1] // ROWS
    padded = groups * ROWS
    capacity = slots // workers
    tiles = levels * width // LANES
    residues = width // ROWS
    lane_class, lane_slot, lane_column, lane_owner = lanes_of(levels)
    me = lax.axis_index("crm")

    rows = jnp.concatenate([ref[...] for ref in row_refs], axis=0)
    lane_c = iota(rows.shape, 1)
    local = rows[:, lane_slot : lane_slot + 1] - (me * slots).astype(F32)
    member = (local == lane_c.astype(F32)) & (lane_c < slots)
    class_row = jnp.sum(jnp.where(member, rows[:, lane_class : lane_class + 1], 0.0), axis=0, keepdims=True)
    sub_p = iota((padded, LANES), 0)
    lane_p = iota((padded, LANES), 1)
    key_row = class_row * LANES + (LANES - 1 - iota((1, LANES), 1)).astype(F32)
    key_col = jnp.sum(jnp.where(sub_p == lane_p, key_row, 0.0), axis=1, keepdims=True)
    class_col = jnp.sum(jnp.where(sub_p == lane_p, class_row, 0.0), axis=1, keepdims=True)
    ahead_row = ((key_col > key_row) & (sub_p < slots)).astype(F32)
    place_row = jnp.sum(ahead_row, axis=0, keepdims=True)
    ahead_col = ((key_row > key_col) & (lane_p < slots)).astype(F32)
    place_col = jnp.sum(ahead_col, axis=1, keepdims=True)
    here = (place_col == lane_p.astype(F32)) & (sub_p < slots)
    order = jnp.sum(jnp.where(here, sub_p.astype(F32), 0.0), axis=0, keepdims=True)
    class_sorted = jnp.sum(jnp.where(here, class_col, 0.0), axis=0, keepdims=True)
    sub_m = iota((ROWS, LANES), 0)
    lane_m = iota((ROWS, LANES), 1)
    meta_v[...] = jnp.where(sub_m == 0, order, jnp.where(sub_m == 1, class_sorted, 0.0)).astype(jnp.int32)
    fetch = pltpu.make_async_copy(meta_v, meta_s, sem_meta)
    fetch.start()
    place_of = jnp.sum(jnp.where(member, place_row + 1.0, 0.0), axis=1, keepdims=True) - 1.0
    rows_s[...] = dot_t((place_of == lane_c.astype(F32)).astype(F32), rows)[:padded]
    fetch.wait()

    def load(index, carry):
        slot = meta_s[0, index]
        pltpu.make_async_copy(x_hbm.at[:, pl.ds(slot, 1), :], xs.at[:, pl.ds(index, 1), :], sem_in.at[index]).start()
        return carry

    lax.fori_loop(0, slots, load, 0)

    model_of = lax.rem(lane_m, ROWS)
    step_of = lane_m // ROWS
    own = model_of == sub_m

    def coef_index(name, phase=0):
        names = ("a", "bx", "c0", "c1", "aw", "ac")
        return names.index(name) if name in names else len(names) + ("fh", "fq", "fs").index(name) * PHASES + phase

    def at(field, phase, residue):
        return (field * PHASES + phase) * residues + residue

    def substep(src, dst):
        def self_at(field, phase, residue):
            return src[at(field, phase, residue)]

        def above(field, phase, residue):
            if phase < PHASES - 1:
                return src[at(field, phase + 1, residue)]
            return pltpu.roll(src[at(field, 0, residue)], LANES - ROWS, 1)

        def below(field, phase, residue):
            if phase > 0:
                return src[at(field, phase - 1, residue)]
            return pltpu.roll(src[at(field, PHASES - 1, residue)], ROWS, 1)

        a, bx, aw, ac = (coef[coef_index(name)] for name in ("a", "bx", "aw", "ac"))
        for phase in range(PHASES):
            c1 = coef[coef_index("c0" if phase < 2 else "c1")]
            fh, fq, fs = (coef[coef_index(name, phase)] for name in ("fh", "fq", "fs"))
            first = [self_at(field, phase, 0) for field in range(3)]
            left = [pltpu.roll(self_at(field, phase, residues - 1), 1, 0) for field in range(3)]
            here = first
            pushed = []
            for residue in range(residues):
                if residue < residues - 1:
                    right = [self_at(field, phase, residue + 1) for field in range(3)]
                else:
                    right = [pltpu.roll(first[field], ROWS - 1, 0) for field in range(3)]
                heat, moist, wind = here
                up_coef = c1 - wind
                down_coef = c1 + wind
                new_heat = (a * heat + fh) + bx * (left[0] + right[0])
                new_heat = new_heat + (up_coef * above(0, phase, residue) + down_coef * below(0, phase, residue))
                new_moist = jnp.minimum(a * moist + fq, ac * moist + fs) + bx * (left[1] + right[1])
                new_moist = new_moist + (up_coef * above(1, phase, residue) + down_coef * below(1, phase, residue))
                new_wind = (aw * wind + (heat - moist)) + bx * (left[2] + right[2])
                new_wind = new_wind + c1 * (above(2, phase, residue) + below(2, phase, residue))
                dst[at(0, phase, residue)] = new_heat
                dst[at(1, phase, residue)] = new_moist
                pushed.append(new_wind)
                left, here = here, right
            total = pushed
            while len(total) > 1:
                total = [sum(total[i : i + 2]) for i in range(0, len(total), 2)]
            mean = all_rows(total[0]) * (1.0 / width)
            for residue in range(residues):
                dst[at(2, phase, residue)] = pushed[residue] - mean

    def run_group(group, carry):
        base = pl.multiple_of(group * ROWS, ROWS)
        units = meta_s[1, base]
        mixed = meta_s[1, base + ROWS - 1] != units

        def wait_in(member_index, inner):
            index = base + member_index

            @pl.when(index < slots)
            def _():
                pltpu.make_async_copy(x_hbm.at[:, pl.ds(0, 1), :], xs.at[:, pl.ds(index, 1), :], sem_in.at[index]).wait()

            return inner

        lax.fori_loop(0, ROWS, wait_in, 0)

        @pl.when(units > 0)
        def _():
            mine = rows_s[pl.ds(base, ROWS), :]
            class_m = mine[:, lane_class : lane_class + 1]
            class_l = all_rows(jnp.where(own, class_m, 0.0))
            steps = jnp.maximum(class_l * SUB, 1.0)
            dt = 1.0 / steps
            scale = 0.5 * dt * dt
            moist_weight = 1.0 - MOIST_BUOYANCY
            diffuse = 1.0 - 2.0 * (DIFFUSE_HORIZ + DIFFUSE_VERT) * dt
            coef[coef_index("a")] = diffuse
            coef[coef_index("bx")] = DIFFUSE_HORIZ * dt
            inside = [(PHASES * step_of + phase) < levels for phase in range(PHASES)]
            coef[coef_index("c0")] = jnp.where(inside[1], DIFFUSE_VERT * dt, 0.0)
            coef[coef_index("c1")] = jnp.where(inside[3], DIFFUSE_VERT * dt, 0.0)
            coef[coef_index("aw")] = diffuse - LINEAR_DRAG * dt
            coef[coef_index("ac")] = diffuse - CONDENSE_RATE * dt
            for phase in range(PHASES):
                level = PHASES * step_of + phase
                pick = jnp.minimum(level, levels - 1)
                keep = own & inside[phase]
                force = [
                    all_rows(jnp.where(keep, jnp.take_along_axis(mine, pick + variable * levels, axis=1), 0.0))
                    for variable in range(2)
                ]
                saturated = jnp.where(inside[phase], 1.0 - 2.0 * (level.astype(F32) + 0.5) / levels, 0.0)
                fq = (moist_weight * scale * dt) * force[1]
                coef[coef_index("fh", phase)] = (scale * dt) * (force[0] + force[1])
                coef[coef_index("fq", phase)] = fq
                coef[coef_index("fs", phase)] = fq + (CONDENSE_RATE * moist_weight) * dt * scale * saturated

            zero = jnp.zeros((ROWS, LANES), F32)
            for field in range(3):
                for half in range(2):
                    parts = []
                    for step in range(LANES // ROWS):
                        tile = 2 * step + half
                        parts.append(xs[field, pl.ds(base, ROWS), tile * LANES : (tile + 1) * LANES] if tile < tiles else zero)
                    start = (field * PHASES + 2 * half) * width
                    nat[start : start + LANES, :] = jnp.concatenate(parts, axis=0).T

            def natural(field, phase, residue):
                return pl.ds((field * PHASES + phase) * width + residue, ROWS, stride=residues)

            moist_scale = moist_weight * scale
            wind_scale = 0.5 * dt
            for phase in range(PHASES):
                for residue in range(residues):
                    theta, moist, wind = (nat[natural(field, phase, residue), :] for field in range(3))
                    s0[at(0, phase, residue)] = scale * (theta + moist)
                    s0[at(1, phase, residue)] = moist_scale * moist
                    s0[at(2, phase, residue)] = wind_scale * wind

            def unit(index, inner):
                for _ in range(SUB // 2):
                    substep(s0, s1)
                    substep(s1, s0)

                @pl.when(mixed & (index + 1 < units))
                def _():
                    done = class_l == (index + 1).astype(F32)
                    for entry in range(3 * PHASES * residues):
                        saved[entry] = jnp.where(done, s0[entry], saved[entry])

                return inner

            lax.fori_loop(0, units, unit, 0)

            last = class_l == units.astype(F32)
            inv_scale = 2.0 * steps * steps
            inv_moist = inv_scale * (1.0 / moist_weight)
            inv_wind = 2.0 * steps
            change = []
            for phase in range(PHASES):
                sums = [jnp.zeros((ROWS, LANES), F32)] * 2
                for residue in range(residues):
                    heat, moist, wind = (
                        jnp.where(last, s0[at(field, phase, residue)], saved[at(field, phase, residue)]) for field in range(3)
                    )
                    moist = inv_moist * moist
                    theta = inv_scale * heat - moist
                    for variable, value in enumerate((theta, moist)):
                        sums[variable] = sums[variable] + (value - nat[natural(variable, phase, residue), :])
                    for field, value in enumerate((theta, moist, inv_wind * wind)):
                        nat[natural(field, phase, residue), :] = value
                change.append([all_rows(value) * (1.0 / width) for value in sums])

            active = class_m > 0.0
            second = lane_m >= levels
            level = jnp.where(second, lane_m - levels, lane_m)
            pick = jnp.minimum(level // PHASES * ROWS + sub_m, LANES - 1)
            which = lax.rem(level, PHASES)
            tendency = jnp.zeros((ROWS, LANES), F32)
            for phase in range(PHASES):
                found = [jnp.take_along_axis(change[phase][variable], pick, axis=1) for variable in range(2)]
                tendency = jnp.where(which == phase, jnp.where(second, found[1], found[0]), tendency)
            t_ref[pl.ds(base, ROWS), :] = jnp.where((lane_m < lane_class) & active, tendency, jnp.where(lane_m < lane_class, 0.0, mine))

            for field in range(3):
                for half in range(2):
                    start = (field * PHASES + 2 * half) * width
                    back = nat[start : start + LANES, :].T
                    for step in range(LANES // ROWS):
                        tile = 2 * step + half
                        if tile >= tiles:
                            continue
                        spot = (field, pl.ds(base, ROWS), slice(tile * LANES, (tile + 1) * LANES))
                        value = back[step * ROWS : (step + 1) * ROWS]
                        xs[spot] = jnp.where(active, value, xs[spot])
                        if field == 1:
                            level = (LANES // width) * tile + lane_m // width
                            saturated = 1.0 - 2.0 * (level.astype(F32) + 0.5) / levels
                            cl[pl.ds(base, ROWS), tile * LANES : (tile + 1) * LANES] = jnp.maximum(value - saturated, 0.0)

        @pl.when(units <= 0)
        def _():
            t_ref[pl.ds(base, ROWS), :] = jnp.zeros((ROWS, LANES), F32)

        def store(member_index, inner):
            index = base + member_index

            @pl.when(index < slots)
            def _():
                slot = meta_s[0, index]
                pltpu.make_async_copy(xs.at[:, pl.ds(index, 1), :], y_hbm.at[:, pl.ds(slot, 1), :], sem_out.at[index]).start()

                @pl.when(meta_s[1, index] > 0)
                def _():
                    owner = lax.div(slot, capacity)
                    rank = slot - owner * capacity
                    for distance in range(workers):

                        @pl.when(owner == (me ^ distance))
                        def _():
                            pltpu.make_async_copy(
                                cl.at[pl.ds(index, 1), :], cloud_hbm[distance].at[pl.ds(rank, 1), :], sem_cloud.at[index]
                            ).start()

            return inner

        lax.fori_loop(0, ROWS, store, 0)
        return carry

    lax.fori_loop(0, groups, run_group, 0)

    def finish(index, carry):
        pltpu.make_async_copy(xs.at[:, pl.ds(index, 1), :], y_hbm.at[:, pl.ds(0, 1), :], sem_out.at[index]).wait()

        @pl.when(meta_s[1, index] > 0)
        def _():
            pltpu.make_async_copy(cl.at[pl.ds(index, 1), :], cloud_hbm[0].at[pl.ds(0, 1), :], sem_cloud.at[index]).wait()

        return carry

    lax.fori_loop(0, slots, finish, 0)


def run_models(row_blocks, state, levels):
    workers = len(row_blocks)
    _, slots, cells = state.shape
    capacity = slots // workers
    width = cells // levels
    groups = -(-slots // ROWS)
    padded = groups * ROWS
    vmem = pl.BlockSpec(memory_space=pltpu.VMEM)
    hbm = pl.BlockSpec(memory_space=pl.ANY)
    entries = 3 * PHASES * (width // ROWS)
    outs = pl.pallas_call(
        functools.partial(model_kernel, workers, slots, levels, width),
        out_shape=[jax.ShapeDtypeStruct(state.shape, F32), jax.ShapeDtypeStruct((padded, LANES), F32)]
        + [jax.ShapeDtypeStruct((capacity, cells), F32)] * workers,
        in_specs=[vmem] * workers + [hbm],
        out_specs=[hbm, vmem] + [hbm] * workers,
        scratch_shapes=[
            pltpu.VMEM((3, padded, cells), F32),
            pltpu.VMEM((padded, cells), F32),
            pltpu.VMEM((3 * PHASES * width, LANES), F32),
            pltpu.VMEM((entries, ROWS, LANES), F32),
            pltpu.VMEM((entries, ROWS, LANES), F32),
            pltpu.VMEM((entries, ROWS, LANES), F32),
            pltpu.VMEM((6 + 3 * PHASES, ROWS, LANES), F32),
            pltpu.VMEM((padded, LANES), F32),
            pltpu.VMEM((ROWS, LANES), jnp.int32),
            pltpu.SMEM((ROWS, LANES), jnp.int32),
            pltpu.SemaphoreType.DMA,
            pltpu.SemaphoreType.DMA((slots,)),
            pltpu.SemaphoreType.DMA((slots,)),
            pltpu.SemaphoreType.DMA((slots,)),
        ],
        compiler_params=pltpu.CompilerParams(vmem_limit_bytes=24 * MIB),
        name="cloud_models",
    )(*row_blocks, state)
    return outs[0], outs[1], outs[2:]


def edge_kernel(levels, columns, workers, *refs):
    t_refs, out = refs[:workers], refs[workers]
    _, _, lane_column, lane_owner = lanes_of(levels)
    me = lax.axis_index("crm")
    wanted = jnp.where(me == 0, workers - 1, 0).astype(F32)
    rows = jnp.concatenate([ref[...] for ref in t_refs], axis=0)
    lane = iota(rows.shape, 1).astype(F32)
    owner = rows[:, lane_owner : lane_owner + 1]
    column = rows[:, lane_column : lane_column + 1]
    select = ((owner == wanted) & (column == lane + 1.0)).astype(F32)
    out[...] = dot_t(select, rows)[:columns]


def physics_kernel(levels, columns, workers, *refs):
    t_refs = refs[:workers]
    edge, index, weight, level_map, out = refs[workers:]
    _, _, lane_column, lane_owner = lanes_of(levels)
    sources = index.shape[0]
    me = lax.axis_index("crm")
    rows = jnp.concatenate([ref[...] for ref in t_refs], axis=0)
    owner = rows[:, lane_owner : lane_owner + 1]
    column = rows[:, lane_column : lane_column + 1]
    block = owner - me.astype(F32) + 1.0
    named = (column > 0.0) & (block >= 0.0) & (block <= 2.0)
    ident = jnp.where(named, block * columns + column - 1.0, -1.0)
    edge_sub = iota((columns, 1), 0)
    edge_block = jnp.where(me == 0, 0, jnp.where(me == workers - 1, 2, -3))
    edge_ident = (edge_block * columns + edge_sub).astype(F32)
    index_rows = index[...].astype(F32)
    weight_rows = weight[...]
    total = jnp.sum(weight_rows, axis=0, keepdims=True)
    inner = jnp.zeros((rows.shape[0], columns), F32)
    outer = jnp.zeros((columns, columns), F32)
    for source in range(sources):
        wanted = index_rows[source : source + 1]
        share = weight_rows[source : source + 1] / total
        inner = inner + jnp.where(ident == wanted, share, 0.0)
        outer = outer + jnp.where(edge_ident == wanted, share, 0.0)
    edge_rows = jnp.where(edge_block >= 0, edge[...], 0.0)
    mixed = dot_t(inner, rows) + dot_t(outer, edge_rows)
    spread_row = iota((levels, LANES), 0)
    spread_lane = iota((levels, LANES), 1)
    for variable in range(2):
        place = (spread_lane == spread_row + variable * levels).astype(F32)
        out[:, variable, :] = dot(mixed, dot_t(place, level_map[...]))


def cloud_kernel(columns, workers, *refs):
    target = refs[0]
    received = refs[1 : workers + 1]
    out, counts, sem = refs[workers + 1 :]
    me = lax.axis_index("crm")
    for worker in range(workers):
        counts[worker] = 0

    def start(column, carry):
        worker = target[column]
        rank = counts[worker]
        counts[worker] = rank + 1
        for distance in range(workers):

            @pl.when(worker == (me ^ distance))
            def _():
                pltpu.make_async_copy(
                    received[distance].at[pl.ds(rank, 1), :], out.at[pl.ds(column, 1), :], sem.at[column]
                ).start()

        return carry

    lax.fori_loop(0, columns, start, 0)

    def finish(column, carry):
        pltpu.make_async_copy(received[0].at[pl.ds(0, 1), :], out.at[pl.ds(column, 1), :], sem.at[column]).wait()
        return carry

    lax.fori_loop(0, columns, finish, 0)


def exchange(blocks, axis):
    size = lax.axis_size(axis)
    out = [blocks[0]]
    for distance in range(1, size):
        out.append(lax.ppermute(blocks[distance], axis, [(i, i ^ distance) for i in range(size)]))
    return out


def body(crm_state, forcing, target, cost_class, level_map, remap_index, remap_weight):
    workers = lax.axis_size("crm")
    groups = lax.axis_size("grp")
    columns = forcing.shape[0]
    slots, _, cells = crm_state.shape
    capacity = slots // workers
    levels, gcm = level_map.shape
    vmem = pl.BlockSpec(memory_space=pltpu.VMEM)
    hbm = pl.BlockSpec(memory_space=pl.ANY)

    rows = pack(target, cost_class, forcing, level_map, workers, capacity)
    row_blocks = exchange([rows] * workers, "crm")
    state, tendency, clouds = run_models(row_blocks, crm_state.transpose(1, 0, 2), levels)
    tendencies = exchange([tendency] * workers, "crm")

    edge = pl.pallas_call(
        functools.partial(edge_kernel, levels, columns, workers),
        out_shape=jax.ShapeDtypeStruct((columns, LANES), F32),
        in_specs=[vmem] * workers,
        out_specs=vmem,
        name="edge_columns",
    )(*tendencies)
    pairs = []
    for group in range(groups):
        after = (group + 1) % groups
        pairs.append((group * workers, after * workers))
        pairs.append((after * workers + workers - 1, group * workers + workers - 1))
    edge = lax.ppermute(edge, ("grp", "crm"), pairs)
    clouds = exchange(clouds, "crm")
    cloud_water = pl.pallas_call(
        functools.partial(cloud_kernel, columns, workers),
        out_shape=jax.ShapeDtypeStruct((columns, cells), F32),
        in_specs=[pl.BlockSpec(memory_space=pltpu.SMEM)] + [hbm] * workers,
        out_specs=hbm,
        scratch_shapes=[pltpu.SMEM((workers,), jnp.int32), pltpu.SemaphoreType.DMA((columns,))],
        name="cloud_rows",
    )(target, *clouds)
    physics = pl.pallas_call(
        functools.partial(physics_kernel, levels, columns, workers),
        out_shape=jax.ShapeDtypeStruct((columns, 2, gcm), F32),
        in_specs=[vmem] * (workers + 4),
        out_specs=vmem,
        name="physics_cells",
    )(*tendencies, edge, remap_index.T, remap_weight.T, level_map)
    return state.transpose(1, 0, 2), cloud_water, physics


def solution(mesh):
    wide = P(("grp", "crm"), None, None)
    flat = P(("grp", "crm"), None)
    line = P(("grp", "crm"))
    in_specs = (wide, wide, line, line, P(), flat, flat)
    out_specs = (wide, flat, wide)
    return jax.shard_map(body, mesh=mesh, in_specs=in_specs, out_specs=out_specs, check_vma=False)
```

```python
import functools

import jax
import jax.numpy as jnp
from jax import lax
from jax.experimental import pallas as pl
from jax.experimental.pallas import tpu as pltpu
from jax.sharding import PartitionSpec as P

CLASSES = 3
SUB = 4
DIFFUSE_HORIZ = 0.2
DIFFUSE_VERT = 0.1
CONDENSE_RATE = 3.0
LINEAR_DRAG = 0.1
MOIST_BUOYANCY = 0.6
HIGHEST = lax.Precision.HIGHEST
F32 = jnp.float32
LANES = 128
ROWS = 8
PHASES = 4
MIB = 1 << 20


def iota(shape, axis):
    return lax.broadcasted_iota(jnp.int32, shape, axis)


def dot_t(lhs, rhs):
    return lax.dot_general(lhs, rhs, (((0,), (0,)), ((), ())), precision=HIGHEST, preferred_element_type=F32)


def dot(lhs, rhs):
    return jnp.dot(lhs, rhs, precision=HIGHEST, preferred_element_type=F32)


def all_rows(x):
    x = x + pltpu.roll(x, 4, 0)
    x = x + pltpu.roll(x, 2, 0)
    return x + pltpu.roll(x, 1, 0)


def lanes_of(levels):
    base = 2 * levels
    return base, base + 1, base + 2, base + 3


def pack_kernel(capacity, workers, target, cost, forcing, level_map, rows, counts):
    levels, gcm = level_map.shape
    columns = forcing.shape[0]
    lane_class, lane_slot, lane_column, lane_owner = lanes_of(levels)
    me = lax.axis_index("crm")
    for worker in range(workers):
        counts[worker] = 0
    sub = iota((columns, LANES), 0)
    lane = iota((columns, LANES), 1)
    classes = jnp.zeros((columns, LANES), F32)
    slots = jnp.zeros((columns, LANES), F32)
    for column in range(columns):
        worker = target[column]
        rank = counts[worker]
        counts[worker] = rank + 1
        slot = (worker * workers + me) * capacity + rank
        classes = jnp.where(sub == column, cost[column].astype(F32), classes)
        slots = jnp.where(sub == column, slot.astype(F32), slots)
    spread_row = iota((levels, LANES), 0)
    spread_lane = iota((levels, LANES), 1)
    mapped = jnp.zeros((columns, LANES), F32)
    for variable in range(2):
        place = (spread_lane == spread_row + variable * levels).astype(F32)
        mapped = mapped + dot(forcing[:, variable, :], dot_t(level_map[...], place))
    meta = jnp.where(lane == lane_class, classes, 0.0)
    meta = jnp.where(lane == lane_slot, slots, meta)
    meta = jnp.where(lane == lane_column, (sub + 1).astype(F32), meta)
    meta = jnp.where(lane == lane_owner, me.astype(F32), meta)
    rows[...] = jnp.where(lane < lane_class, mapped, meta)


def pack(target, cost, forcing, level_map, workers, capacity):
    columns = forcing.shape[0]
    return pl.pallas_call(
        functools.partial(pack_kernel, capacity, workers),
        out_shape=jax.ShapeDtypeStruct((columns, LANES), F32),
        in_specs=[pl.BlockSpec(memory_space=pltpu.SMEM)] * 2 + [pl.BlockSpec(memory_space=pltpu.VMEM)] * 2,
        out_specs=pl.BlockSpec(memory_space=pltpu.VMEM),
        scratch_shapes=[pltpu.SMEM((workers,), jnp.int32)],
        compiler_params=pltpu.CompilerParams(vmem_limit_bytes=8 * MIB),
        name="pack_forcing",
    )(target, cost, forcing, level_map)


def model_kernel(workers, slots, levels, width, *refs):
    row_refs = refs[:workers]
    x_hbm = refs[workers]
    y_hbm, t_ref = refs[workers + 1 : workers + 3]
    cloud_hbm = refs[workers + 3 : 2 * workers + 3]
    (xs, cl, nat, s0, s1, saved, coef, rows_s, meta_v, meta_s, sem_meta, sem_in, sem_out, sem_cloud) = refs[2 * workers + 3 :]
    groups = xs.shape[1] // ROWS
    padded = groups * ROWS
    capacity = slots // workers
    tiles = levels * width // LANES
    residues = width // ROWS
    lane_class, lane_slot, lane_column, lane_owner = lanes_of(levels)
    me = lax.axis_index("crm")

    rows = jnp.concatenate([ref[...] for ref in row_refs], axis=0)
    lane_c = iota(rows.shape, 1)
    local = rows[:, lane_slot : lane_slot + 1] - (me * slots).astype(F32)
    member = (local == lane_c.astype(F32)) & (lane_c < slots)
    class_row = jnp.sum(jnp.where(member, rows[:, lane_class : lane_class + 1], 0.0), axis=0, keepdims=True)
    sub_p = iota((padded, LANES), 0)
    lane_p = iota((padded, LANES), 1)
    key_row = class_row * LANES + (LANES - 1 - iota((1, LANES), 1)).astype(F32)
    key_col = jnp.sum(jnp.where(sub_p == lane_p, key_row, 0.0), axis=1, keepdims=True)
    class_col = jnp.sum(jnp.where(sub_p == lane_p, class_row, 0.0), axis=1, keepdims=True)
    ahead_row = ((key_col > key_row) & (sub_p < slots)).astype(F32)
    place_row = jnp.sum(ahead_row, axis=0, keepdims=True)
    ahead_col = ((key_row > key_col) & (lane_p < slots)).astype(F32)
    place_col = jnp.sum(ahead_col, axis=1, keepdims=True)
    here = (place_col == lane_p.astype(F32)) & (sub_p < slots)
    order = jnp.sum(jnp.where(here, sub_p.astype(F32), 0.0), axis=0, keepdims=True)
    class_sorted = jnp.sum(jnp.where(here, class_col, 0.0), axis=0, keepdims=True)
    sub_m = iota((ROWS, LANES), 0)
    lane_m = iota((ROWS, LANES), 1)
    owner_row = jnp.floor((order + 0.5) * (1.0 / capacity))
    rank_row = order - owner_row * capacity
    away_row = owner_row.astype(jnp.int32) ^ me
    table = jnp.where(sub_m == 0, order, jnp.where(sub_m == 1, class_sorted, rank_row)).astype(jnp.int32)
    meta_v[...] = jnp.where(sub_m == 2, away_row, table)
    fetch = pltpu.make_async_copy(meta_v, meta_s, sem_meta)
    fetch.start()
    place_of = jnp.sum(jnp.where(member, place_row + 1.0, 0.0), axis=1, keepdims=True) - 1.0
    rows_s[...] = dot_t((place_of == lane_c.astype(F32)).astype(F32), rows)[:padded]
    fetch.wait()

    def load(index, carry):
        slot = meta_s[0, index]
        group = lax.shift_right_logical(index, 3)
        pltpu.make_async_copy(x_hbm.at[:, pl.ds(slot, 1), :], xs.at[:, pl.ds(index, 1), :], sem_in.at[group]).start()
        return carry

    lax.fori_loop(0, padded, load, 0, unroll=4)

    model_of = lax.rem(lane_m, ROWS)
    step_of = lane_m // ROWS
    own = model_of == sub_m

    def coef_index(name, phase=0):
        names = ("a", "bx", "c0", "c1", "aw", "ac")
        return names.index(name) if name in names else len(names) + ("fh", "fq", "fs").index(name) * PHASES + phase

    def at(field, phase, residue):
        return (field * PHASES + phase) * residues + residue

    def substep(src, dst):
        def self_at(field, phase, residue):
            return src[at(field, phase, residue)]

        def above(field, phase, residue):
            if phase < PHASES - 1:
                return src[at(field, phase + 1, residue)]
            return pltpu.roll(src[at(field, 0, residue)], LANES - ROWS, 1)

        def below(field, phase, residue):
            if phase > 0:
                return src[at(field, phase - 1, residue)]
            return pltpu.roll(src[at(field, PHASES - 1, residue)], ROWS, 1)

        a, bx, aw, ac = (coef[coef_index(name)] for name in ("a", "bx", "aw", "ac"))
        for phase in range(PHASES):
            c1 = coef[coef_index("c0" if phase < 2 else "c1")]
            fh, fq, fs = (coef[coef_index(name, phase)] for name in ("fh", "fq", "fs"))
            first = [self_at(field, phase, 0) for field in range(3)]
            left = [pltpu.roll(self_at(field, phase, residues - 1), 1, 0) for field in range(3)]
            here = first
            pushed = []
            for residue in range(residues):
                if residue < residues - 1:
                    right = [self_at(field, phase, residue + 1) for field in range(3)]
                else:
                    right = [pltpu.roll(first[field], ROWS - 1, 0) for field in range(3)]
                heat, moist, wind = here
                up_coef = c1 - wind
                down_coef = c1 + wind
                new_heat = (a * heat + fh) + bx * (left[0] + right[0])
                new_heat = new_heat + (up_coef * above(0, phase, residue) + down_coef * below(0, phase, residue))
                new_moist = jnp.minimum(a * moist + fq, ac * moist + fs) + bx * (left[1] + right[1])
                new_moist = new_moist + (up_coef * above(1, phase, residue) + down_coef * below(1, phase, residue))
                new_wind = (aw * wind + (heat - moist)) + bx * (left[2] + right[2])
                new_wind = new_wind + c1 * (above(2, phase, residue) + below(2, phase, residue))
                dst[at(0, phase, residue)] = new_heat
                dst[at(1, phase, residue)] = new_moist
                pushed.append(new_wind)
                left, here = here, right
            total = pushed
            while len(total) > 1:
                total = [sum(total[i : i + 2]) for i in range(0, len(total), 2)]
            mean = all_rows(total[0]) * (1.0 / width)
            for residue in range(residues):
                dst[at(2, phase, residue)] = pushed[residue] - mean

    def run_group(group, carry):
        base = pl.multiple_of(group * ROWS, ROWS)
        units = meta_s[1, base]
        mixed = meta_s[1, base + ROWS - 1] != units

        here = xs.at[:, pl.ds(base, ROWS), :]
        pltpu.make_async_copy(here, here, sem_in.at[group]).wait()

        @pl.when(units > 0)
        def _():
            mine = rows_s[pl.ds(base, ROWS), :]
            class_m = mine[:, lane_class : lane_class + 1]
            class_l = all_rows(jnp.where(own, class_m, 0.0))
            steps = jnp.maximum(class_l * SUB, 1.0)
            dt = 1.0 / steps
            scale = 0.5 * dt * dt
            moist_weight = 1.0 - MOIST_BUOYANCY
            diffuse = 1.0 - 2.0 * (DIFFUSE_HORIZ + DIFFUSE_VERT) * dt
            coef[coef_index("a")] = diffuse
            coef[coef_index("bx")] = DIFFUSE_HORIZ * dt
            inside = [(PHASES * step_of + phase) < levels for phase in range(PHASES)]
            coef[coef_index("c0")] = jnp.where(inside[1], DIFFUSE_VERT * dt, 0.0)
            coef[coef_index("c1")] = jnp.where(inside[3], DIFFUSE_VERT * dt, 0.0)
            coef[coef_index("aw")] = diffuse - LINEAR_DRAG * dt
            coef[coef_index("ac")] = diffuse - CONDENSE_RATE * dt
            for phase in range(PHASES):
                level = PHASES * step_of + phase
                pick = jnp.minimum(level, levels - 1)
                keep = own & inside[phase]
                force = [
                    all_rows(jnp.where(keep, jnp.take_along_axis(mine, pick + variable * levels, axis=1), 0.0))
                    for variable in range(2)
                ]
                saturated = jnp.where(inside[phase], 1.0 - 2.0 * (level.astype(F32) + 0.5) / levels, 0.0)
                fq = (moist_weight * scale * dt) * force[1]
                coef[coef_index("fh", phase)] = (scale * dt) * (force[0] + force[1])
                coef[coef_index("fq", phase)] = fq
                coef[coef_index("fs", phase)] = fq + (CONDENSE_RATE * moist_weight) * dt * scale * saturated

            zero = jnp.zeros((ROWS, LANES), F32)
            for field in range(3):
                for half in range(2):
                    parts = []
                    for step in range(LANES // ROWS):
                        tile = 2 * step + half
                        parts.append(xs[field, pl.ds(base, ROWS), tile * LANES : (tile + 1) * LANES] if tile < tiles else zero)
                    start = (field * PHASES + 2 * half) * width
                    nat[start : start + LANES, :] = jnp.concatenate(parts, axis=0).T

            def natural(field, phase, residue):
                return pl.ds((field * PHASES + phase) * width + residue, ROWS, stride=residues)

            moist_scale = moist_weight * scale
            wind_scale = 0.5 * dt
            for phase in range(PHASES):
                for residue in range(residues):
                    theta, moist, wind = (nat[natural(field, phase, residue), :] for field in range(3))
                    s0[at(0, phase, residue)] = scale * (theta + moist)
                    s0[at(1, phase, residue)] = moist_scale * moist
                    s0[at(2, phase, residue)] = wind_scale * wind

            def unit(index, inner):
                for _ in range(SUB // 2):
                    substep(s0, s1)
                    substep(s1, s0)

                @pl.when(mixed & (index + 1 < units))
                def _():
                    done = class_l == (index + 1).astype(F32)
                    for entry in range(3 * PHASES * residues):
                        saved[entry] = jnp.where(done, s0[entry], saved[entry])

                return inner

            lax.fori_loop(0, units, unit, 0)

            last = class_l == units.astype(F32)
            inv_scale = 2.0 * steps * steps
            inv_moist = inv_scale * (1.0 / moist_weight)
            inv_wind = 2.0 * steps
            change = []
            for phase in range(PHASES):
                sums = [jnp.zeros((ROWS, LANES), F32)] * 2
                for residue in range(residues):
                    heat, moist, wind = (
                        jnp.where(last, s0[at(field, phase, residue)], saved[at(field, phase, residue)]) for field in range(3)
                    )
                    moist = inv_moist * moist
                    theta = inv_scale * heat - moist
                    for variable, value in enumerate((theta, moist)):
                        sums[variable] = sums[variable] + (value - nat[natural(variable, phase, residue), :])
                    for field, value in enumerate((theta, moist, inv_wind * wind)):
                        nat[natural(field, phase, residue), :] = value
                change.append([all_rows(value) * (1.0 / width) for value in sums])

            active = class_m > 0.0
            second = lane_m >= levels
            level = jnp.where(second, lane_m - levels, lane_m)
            pick = jnp.minimum(level // PHASES * ROWS + sub_m, LANES - 1)
            which = lax.rem(level, PHASES)
            tendency = jnp.zeros((ROWS, LANES), F32)
            for phase in range(PHASES):
                found = [jnp.take_along_axis(change[phase][variable], pick, axis=1) for variable in range(2)]
                tendency = jnp.where(which == phase, jnp.where(second, found[1], found[0]), tendency)
            t_ref[pl.ds(base, ROWS), :] = jnp.where((lane_m < lane_class) & active, tendency, jnp.where(lane_m < lane_class, 0.0, mine))

            for field in range(3):
                for half in range(2):
                    start = (field * PHASES + 2 * half) * width
                    back = nat[start : start + LANES, :].T
                    for step in range(LANES // ROWS):
                        tile = 2 * step + half
                        if tile >= tiles:
                            continue
                        spot = (field, pl.ds(base, ROWS), slice(tile * LANES, (tile + 1) * LANES))
                        value = back[step * ROWS : (step + 1) * ROWS]
                        xs[spot] = jnp.where(active, value, xs[spot])
                        if field == 1:
                            level = (LANES // width) * tile + lane_m // width
                            saturated = 1.0 - 2.0 * (level.astype(F32) + 0.5) / levels
                            cl[pl.ds(base, ROWS), tile * LANES : (tile + 1) * LANES] = jnp.maximum(value - saturated, 0.0)

        @pl.when(units <= 0)
        def _():
            t_ref[pl.ds(base, ROWS), :] = jnp.zeros((ROWS, LANES), F32)

        def store(member):
            index = base + member
            slot = meta_s[0, index]
            rank = meta_s[3, index]
            away = meta_s[2, index]
            pltpu.make_async_copy(xs.at[:, pl.ds(index, 1), :], y_hbm.at[:, pl.ds(slot, 1), :], sem_out.at[index]).start()
            for distance in range(workers):

                @pl.when(away == distance)
                def _():
                    pltpu.make_async_copy(
                        cl.at[pl.ds(index, 1), :], cloud_hbm[distance].at[pl.ds(rank, 1), :], sem_cloud.at[index]
                    ).start()

        for member in range(ROWS):
            if member < (slots - 1) % ROWS + 1:
                store(member)
            else:
                pl.when(group < groups - 1)(functools.partial(store, member))
        return carry

    lax.fori_loop(0, groups, run_group, 0)

    for index in range(slots):
        pltpu.make_async_copy(xs.at[:, pl.ds(index, 1), :], y_hbm.at[:, pl.ds(0, 1), :], sem_out.at[index]).wait()
        pltpu.make_async_copy(cl.at[pl.ds(index, 1), :], cloud_hbm[0].at[pl.ds(0, 1), :], sem_cloud.at[index]).wait()


def run_models(row_blocks, state, levels):
    workers = len(row_blocks)
    _, slots, cells = state.shape
    capacity = slots // workers
    width = cells // levels
    groups = -(-slots // ROWS)
    padded = groups * ROWS
    vmem = pl.BlockSpec(memory_space=pltpu.VMEM)
    hbm = pl.BlockSpec(memory_space=pl.ANY)
    entries = 3 * PHASES * (width // ROWS)
    outs = pl.pallas_call(
        functools.partial(model_kernel, workers, slots, levels, width),
        out_shape=[jax.ShapeDtypeStruct(state.shape, F32), jax.ShapeDtypeStruct((padded, LANES), F32)]
        + [jax.ShapeDtypeStruct((capacity, cells), F32)] * workers,
        in_specs=[vmem] * workers + [hbm],
        out_specs=[hbm, vmem] + [hbm] * workers,
        scratch_shapes=[
            pltpu.VMEM((3, padded, cells), F32),
            pltpu.VMEM((padded, cells), F32),
            pltpu.VMEM((3 * PHASES * width, LANES), F32),
            pltpu.VMEM((entries, ROWS, LANES), F32),
            pltpu.VMEM((entries, ROWS, LANES), F32),
            pltpu.VMEM((entries, ROWS, LANES), F32),
            pltpu.VMEM((6 + 3 * PHASES, ROWS, LANES), F32),
            pltpu.VMEM((padded, LANES), F32),
            pltpu.VMEM((ROWS, LANES), jnp.int32),
            pltpu.SMEM((ROWS, LANES), jnp.int32),
            pltpu.SemaphoreType.DMA,
            pltpu.SemaphoreType.DMA((groups,)),
            pltpu.SemaphoreType.DMA((slots,)),
            pltpu.SemaphoreType.DMA((slots,)),
        ],
        compiler_params=pltpu.CompilerParams(vmem_limit_bytes=24 * MIB),
        name="cloud_models",
    )(*row_blocks, state)
    return outs[0], outs[1], outs[2:]


def edge_kernel(levels, columns, workers, *refs):
    t_refs, out = refs[:workers], refs[workers]
    _, _, lane_column, lane_owner = lanes_of(levels)
    me = lax.axis_index("crm")
    wanted = jnp.where(me == 0, workers - 1, 0).astype(F32)
    rows = jnp.concatenate([ref[...] for ref in t_refs], axis=0)
    lane = iota(rows.shape, 1).astype(F32)
    owner = rows[:, lane_owner : lane_owner + 1]
    column = rows[:, lane_column : lane_column + 1]
    select = ((owner == wanted) & (column == lane + 1.0)).astype(F32)
    out[...] = dot_t(select, rows)[:columns]


def physics_kernel(levels, columns, workers, *refs):
    t_refs = refs[:workers]
    edge, index, weight, level_map, out = refs[workers:]
    _, _, lane_column, lane_owner = lanes_of(levels)
    sources = index.shape[0]
    me = lax.axis_index("crm")
    rows = jnp.concatenate([ref[...] for ref in t_refs], axis=0)
    owner = rows[:, lane_owner : lane_owner + 1]
    column = rows[:, lane_column : lane_column + 1]
    block = owner - me.astype(F32) + 1.0
    named = (column > 0.0) & (block >= 0.0) & (block <= 2.0)
    ident = jnp.where(named, block * columns + column - 1.0, -1.0)
    edge_sub = iota((columns, 1), 0)
    edge_block = jnp.where(me == 0, 0, jnp.where(me == workers - 1, 2, -3))
    edge_ident = (edge_block * columns + edge_sub).astype(F32)
    index_rows = index[...].astype(F32)
    weight_rows = weight[...]
    total = jnp.sum(weight_rows, axis=0, keepdims=True)
    inner = jnp.zeros((rows.shape[0], columns), F32)
    outer = jnp.zeros((columns, columns), F32)
    for source in range(sources):
        wanted = index_rows[source : source + 1]
        share = weight_rows[source : source + 1] / total
        inner = inner + jnp.where(ident == wanted, share, 0.0)
        outer = outer + jnp.where(edge_ident == wanted, share, 0.0)
    edge_rows = jnp.where(edge_block >= 0, edge[...], 0.0)
    mixed = dot_t(inner, rows) + dot_t(outer, edge_rows)
    spread_row = iota((levels, LANES), 0)
    spread_lane = iota((levels, LANES), 1)
    for variable in range(2):
        place = (spread_lane == spread_row + variable * levels).astype(F32)
        out[:, variable, :] = dot(mixed, dot_t(place, level_map[...]))


def cloud_kernel(columns, workers, *refs):
    target = refs[0]
    received = refs[1 : workers + 1]
    out, counts, sem = refs[workers + 1 :]
    me = lax.axis_index("crm")
    for worker in range(workers):
        counts[worker] = 0

    def start(column, carry):
        worker = target[column]
        rank = counts[worker]
        counts[worker] = rank + 1
        for distance in range(workers):

            @pl.when(worker == (me ^ distance))
            def _():
                pltpu.make_async_copy(
                    received[distance].at[pl.ds(rank, 1), :], out.at[pl.ds(column, 1), :], sem.at[column]
                ).start()

        return carry

    lax.fori_loop(0, columns, start, 0)

    def finish(column, carry):
        pltpu.make_async_copy(received[0].at[pl.ds(0, 1), :], out.at[pl.ds(column, 1), :], sem.at[column]).wait()
        return carry

    lax.fori_loop(0, columns, finish, 0)


def exchange(blocks, axis):
    size = lax.axis_size(axis)
    out = [blocks[0]]
    for distance in range(1, size):
        out.append(lax.ppermute(blocks[distance], axis, [(i, i ^ distance) for i in range(size)]))
    return out


def body(crm_state, forcing, target, cost_class, level_map, remap_index, remap_weight):
    workers = lax.axis_size("crm")
    groups = lax.axis_size("grp")
    columns = forcing.shape[0]
    slots, _, cells = crm_state.shape
    capacity = slots // workers
    levels, gcm = level_map.shape
    vmem = pl.BlockSpec(memory_space=pltpu.VMEM)
    hbm = pl.BlockSpec(memory_space=pl.ANY)

    rows = pack(target, cost_class, forcing, level_map, workers, capacity)
    row_blocks = exchange([rows] * workers, "crm")
    state, tendency, clouds = run_models(row_blocks, crm_state.transpose(1, 0, 2), levels)
    tendencies = exchange([tendency] * workers, "crm")
    clouds, tendencies = lax.optimization_barrier((clouds, tendencies))

    edge = pl.pallas_call(
        functools.partial(edge_kernel, levels, columns, workers),
        out_shape=jax.ShapeDtypeStruct((columns, LANES), F32),
        in_specs=[vmem] * workers,
        out_specs=vmem,
        compiler_params=pltpu.CompilerParams(vmem_limit_bytes=8 * MIB),
        name="edge_columns",
    )(*tendencies)
    pairs = []
    for group in range(groups):
        after = (group + 1) % groups
        pairs.append((group * workers, after * workers))
        pairs.append((after * workers + workers - 1, group * workers + workers - 1))
    edge = lax.ppermute(edge, ("grp", "crm"), pairs)
    clouds = exchange(clouds, "crm")
    cloud_water = pl.pallas_call(
        functools.partial(cloud_kernel, columns, workers),
        out_shape=jax.ShapeDtypeStruct((columns, cells), F32),
        in_specs=[pl.BlockSpec(memory_space=pltpu.SMEM)] + [hbm] * workers,
        out_specs=hbm,
        scratch_shapes=[pltpu.SMEM((workers,), jnp.int32), pltpu.SemaphoreType.DMA((columns,))],
        compiler_params=pltpu.CompilerParams(vmem_limit_bytes=8 * MIB),
        name="cloud_rows",
    )(target, *clouds)
    physics = pl.pallas_call(
        functools.partial(physics_kernel, levels, columns, workers),
        out_shape=jax.ShapeDtypeStruct((columns, 2, gcm), F32),
        in_specs=[vmem] * (workers + 4),
        out_specs=vmem,
        compiler_params=pltpu.CompilerParams(vmem_limit_bytes=8 * MIB),
        name="physics_cells",
    )(*tendencies, edge, remap_index.T, remap_weight.T, level_map)
    return state.transpose(1, 0, 2), cloud_water, physics


def solution(mesh):
    wide = P(("grp", "crm"), None, None)
    flat = P(("grp", "crm"), None)
    line = P(("grp", "crm"))
    in_specs = (wide, wide, line, line, P(), flat, flat)
    out_specs = (wide, flat, wide)
    return jax.shard_map(body, mesh=mesh, in_specs=in_specs, out_specs=out_specs, check_vma=False)
```

```python
import functools

import jax
import jax.numpy as jnp
from jax import lax
from jax.experimental import pallas as pl
from jax.experimental.pallas import tpu as pltpu
from jax.sharding import PartitionSpec as P

CLASSES = 3
SUB = 4
DIFFUSE_HORIZ = 0.2
DIFFUSE_VERT = 0.1
CONDENSE_RATE = 3.0
LINEAR_DRAG = 0.1
MOIST_BUOYANCY = 0.6
HIGHEST = lax.Precision.HIGHEST
F32 = jnp.float32
LANES = 128
ROWS = 8
PHASES = 4
MIB = 1 << 20


def iota(shape, axis):
    return lax.broadcasted_iota(jnp.int32, shape, axis)


def dot_t(lhs, rhs):
    return lax.dot_general(lhs, rhs, (((0,), (0,)), ((), ())), precision=HIGHEST, preferred_element_type=F32)


def dot(lhs, rhs):
    return jnp.dot(lhs, rhs, precision=HIGHEST, preferred_element_type=F32)


def all_rows(x):
    x = x + pltpu.roll(x, 4, 0)
    x = x + pltpu.roll(x, 2, 0)
    return x + pltpu.roll(x, 1, 0)


def lanes_of(levels):
    base = 2 * levels
    return base, base + 1, base + 2, base + 3


def pack_kernel(capacity, workers, target_hbm, cost_hbm, forcing_hbm, level_hbm, rows, target, cost, forcing, level_map, counts, sems):
    pairs = ((target_hbm, target), (cost_hbm, cost), (forcing_hbm, forcing), (level_hbm, level_map))
    copies = [pltpu.make_async_copy(source, place, sems.at[i]) for i, (source, place) in enumerate(pairs)]
    for copy in copies:
        copy.start()
    for copy in copies:
        copy.wait()
    levels, gcm = level_map.shape
    columns = forcing.shape[0]
    lane_class, lane_slot, lane_column, lane_owner = lanes_of(levels)
    me = lax.axis_index("crm")
    for worker in range(workers):
        counts[worker] = 0
    sub = iota((columns, LANES), 0)
    lane = iota((columns, LANES), 1)
    classes = jnp.zeros((columns, LANES), F32)
    slots = jnp.zeros((columns, LANES), F32)
    for column in range(columns):
        worker = target[column]
        rank = counts[worker]
        counts[worker] = rank + 1
        slot = (worker * workers + me) * capacity + rank
        classes = jnp.where(sub == column, cost[column].astype(F32), classes)
        slots = jnp.where(sub == column, slot.astype(F32), slots)
    spread_row = iota((levels, LANES), 0)
    spread_lane = iota((levels, LANES), 1)
    mapped = jnp.zeros((columns, LANES), F32)
    for variable in range(2):
        place = (spread_lane == spread_row + variable * levels).astype(F32)
        mapped = mapped + dot(forcing[:, variable, :], dot_t(level_map[...], place))
    meta = jnp.where(lane == lane_class, classes, 0.0)
    meta = jnp.where(lane == lane_slot, slots, meta)
    meta = jnp.where(lane == lane_column, (sub + 1).astype(F32), meta)
    meta = jnp.where(lane == lane_owner, me.astype(F32), meta)
    rows[...] = jnp.where(lane < lane_class, mapped, meta)


def pack(target, cost, forcing, level_map, workers, capacity):
    columns = forcing.shape[0]
    return pl.pallas_call(
        functools.partial(pack_kernel, capacity, workers),
        out_shape=jax.ShapeDtypeStruct((columns, LANES), F32),
        in_specs=[pl.BlockSpec(memory_space=pltpu.HBM)] * 4,
        out_specs=pl.BlockSpec(memory_space=pltpu.VMEM),
        scratch_shapes=[
            pltpu.SMEM(target.shape, jnp.int32),
            pltpu.SMEM(cost.shape, jnp.int32),
            pltpu.VMEM(forcing.shape, F32),
            pltpu.VMEM(level_map.shape, F32),
            pltpu.SMEM((workers,), jnp.int32),
            pltpu.SemaphoreType.DMA((4,)),
        ],
        compiler_params=pltpu.CompilerParams(vmem_limit_bytes=8 * MIB),
        name="pack_forcing",
    )(target, cost, forcing, level_map)


def model_kernel(workers, slots, levels, width, *refs):
    row_refs = refs[:workers]
    x_hbm, fin, xs, t_ref, meta_v, nat, s1, saved, coef, rows_s, meta_s, sem_meta, sem_in = refs[workers:]
    groups = xs.shape[1] // ROWS
    padded = groups * ROWS
    capacity = slots // workers
    tiles = levels * width // LANES
    residues = width // ROWS
    lane_class, lane_slot, lane_column, lane_owner = lanes_of(levels)
    me = lax.axis_index("crm")

    rows = jnp.concatenate([ref[...] for ref in row_refs], axis=0)
    lane_c = iota(rows.shape, 1)
    local = rows[:, lane_slot : lane_slot + 1] - (me * slots).astype(F32)
    member = (local == lane_c.astype(F32)) & (lane_c < slots)
    class_row = jnp.sum(jnp.where(member, rows[:, lane_class : lane_class + 1], 0.0), axis=0, keepdims=True)
    sub_p = iota((padded, LANES), 0)
    lane_p = iota((padded, LANES), 1)
    key_row = class_row * LANES + (LANES - 1 - iota((1, LANES), 1)).astype(F32)
    key_col = jnp.sum(jnp.where(sub_p == lane_p, key_row, 0.0), axis=1, keepdims=True)
    class_col = jnp.sum(jnp.where(sub_p == lane_p, class_row, 0.0), axis=1, keepdims=True)
    ahead_row = ((key_col > key_row) & (sub_p < slots)).astype(F32)
    place_row = jnp.sum(ahead_row, axis=0, keepdims=True)
    ahead_col = ((key_row > key_col) & (lane_p < slots)).astype(F32)
    place_col = jnp.sum(ahead_col, axis=1, keepdims=True)
    here = (place_col == lane_p.astype(F32)) & (sub_p < slots)
    order = jnp.sum(jnp.where(here, sub_p.astype(F32), 0.0), axis=0, keepdims=True)
    class_sorted = jnp.sum(jnp.where(here, class_col, 0.0), axis=0, keepdims=True)
    sub_m = iota((ROWS, LANES), 0)
    lane_m = iota((ROWS, LANES), 1)
    owner_row = jnp.floor((order + 0.5) * (1.0 / capacity))
    rank_row = order - owner_row * capacity
    away_row = owner_row.astype(jnp.int32) ^ me
    table = jnp.where(sub_m == 0, order, jnp.where(sub_m == 1, class_sorted, rank_row)).astype(jnp.int32)
    meta_v[...] = jnp.where(sub_m == 2, away_row, table)
    fetch = pltpu.make_async_copy(meta_v, meta_s, sem_meta)
    fetch.start()
    place_of = jnp.sum(jnp.where(member, place_row + 1.0, 0.0), axis=1, keepdims=True) - 1.0
    rows_s[...] = dot_t((place_of == lane_c.astype(F32)).astype(F32), rows)[:padded]
    fetch.wait()

    def load(index, carry):
        slot = meta_s[0, index]
        pltpu.make_async_copy(x_hbm.at[:, pl.ds(slot, 1), :], xs.at[:, pl.ds(index, 1), :], sem_in.at[index]).start()
        return carry

    lax.fori_loop(0, padded, load, 0, unroll=4)

    model_of = lax.rem(lane_m, ROWS)
    step_of = lane_m // ROWS
    own = model_of == sub_m

    def coef_index(name, phase=0):
        names = ("a", "bx", "c0", "c1", "aw", "ac")
        return names.index(name) if name in names else len(names) + ("fh", "fq", "fs").index(name) * PHASES + phase

    def at(field, phase, residue):
        return (field * PHASES + phase) * residues + residue

    def substep(src, dst):
        def self_at(field, phase, residue):
            return src[at(field, phase, residue)]

        def above(field, phase, residue):
            if phase < PHASES - 1:
                return src[at(field, phase + 1, residue)]
            return pltpu.roll(src[at(field, 0, residue)], LANES - ROWS, 1)

        def below(field, phase, residue):
            if phase > 0:
                return src[at(field, phase - 1, residue)]
            return pltpu.roll(src[at(field, PHASES - 1, residue)], ROWS, 1)

        a, bx, aw, ac = (coef[coef_index(name)] for name in ("a", "bx", "aw", "ac"))
        for phase in range(PHASES):
            c1 = coef[coef_index("c0" if phase < 2 else "c1")]
            fh, fq, fs = (coef[coef_index(name, phase)] for name in ("fh", "fq", "fs"))
            def around(field, residue):
                if residue > 0:
                    left = self_at(field, phase, residue - 1)
                else:
                    left = pltpu.roll(self_at(field, phase, residues - 1), 1, 0)
                if residue < residues - 1:
                    return left + self_at(field, phase, residue + 1)
                return left + pltpu.roll(self_at(field, phase, 0), ROWS - 1, 0)

            pushed = []
            for residue in range(residues):
                wind = self_at(2, phase, residue)
                new_wind = (aw * wind + (self_at(0, phase, residue) - self_at(1, phase, residue))) + bx * around(2, residue)
                pushed.append(new_wind + c1 * (above(2, phase, residue) + below(2, phase, residue)))
            total = pushed
            while len(total) > 1:
                total = [sum(total[i : i + 2]) for i in range(0, len(total), 2)]
            mean = all_rows(total[0]) * (1.0 / width)
            for residue in range(residues):
                dst[at(2, phase, residue)] = pushed[residue] - mean
            for residue in range(residues):
                heat, moist, wind = (self_at(field, phase, residue) for field in range(3))
                up_coef = c1 - wind
                down_coef = c1 + wind
                new_heat = (a * heat + fh) + bx * around(0, residue)
                dst[at(0, phase, residue)] = new_heat + (
                    up_coef * above(0, phase, residue) + down_coef * below(0, phase, residue)
                )
                new_moist = jnp.minimum(a * moist + fq, ac * moist + fs) + bx * around(1, residue)
                dst[at(1, phase, residue)] = new_moist + (
                    up_coef * above(1, phase, residue) + down_coef * below(1, phase, residue)
                )

    def run_group(group, carry):
        base = pl.multiple_of(group * ROWS, ROWS)
        units = meta_s[1, base]
        mixed = meta_s[1, base + ROWS - 1] != units

        for member in range(ROWS):
            index = base + member
            pltpu.make_async_copy(x_hbm.at[:, pl.ds(0, 1), :], xs.at[:, pl.ds(index, 1), :], sem_in.at[index]).wait()

        s0 = fin.at[group]

        @pl.when(units > 0)
        def _():
            mine = rows_s[pl.ds(base, ROWS), :]
            class_m = mine[:, lane_class : lane_class + 1]
            class_l = all_rows(jnp.where(own, class_m, 0.0))
            steps = jnp.maximum(class_l * SUB, 1.0)
            dt = 1.0 / steps
            scale = 0.5 * dt * dt
            moist_weight = 1.0 - MOIST_BUOYANCY
            diffuse = 1.0 - 2.0 * (DIFFUSE_HORIZ + DIFFUSE_VERT) * dt
            coef[coef_index("a")] = diffuse
            coef[coef_index("bx")] = DIFFUSE_HORIZ * dt
            inside = [(PHASES * step_of + phase) < levels for phase in range(PHASES)]
            coef[coef_index("c0")] = jnp.where(inside[1], DIFFUSE_VERT * dt, 0.0)
            coef[coef_index("c1")] = jnp.where(inside[3], DIFFUSE_VERT * dt, 0.0)
            coef[coef_index("aw")] = diffuse - LINEAR_DRAG * dt
            coef[coef_index("ac")] = diffuse - CONDENSE_RATE * dt
            for phase in range(PHASES):
                level = PHASES * step_of + phase
                pick = jnp.minimum(level, levels - 1)
                keep = own & inside[phase]
                force = [
                    all_rows(jnp.where(keep, jnp.take_along_axis(mine, pick + variable * levels, axis=1), 0.0))
                    for variable in range(2)
                ]
                saturated = jnp.where(inside[phase], 1.0 - 2.0 * (level.astype(F32) + 0.5) / levels, 0.0)
                fq = (moist_weight * scale * dt) * force[1]
                coef[coef_index("fh", phase)] = (scale * dt) * (force[0] + force[1])
                coef[coef_index("fq", phase)] = fq
                coef[coef_index("fs", phase)] = fq + (CONDENSE_RATE * moist_weight) * dt * scale * saturated

            zero = jnp.zeros((ROWS, LANES), F32)
            for field in range(3):
                for half in range(2):
                    parts = []
                    for step in range(LANES // ROWS):
                        tile = 2 * step + half
                        parts.append(xs[field, pl.ds(base, ROWS), tile * LANES : (tile + 1) * LANES] if tile < tiles else zero)
                    start = (field * PHASES + 2 * half) * width
                    nat[start : start + LANES, :] = jnp.concatenate(parts, axis=0).T

            def natural(field, phase, residue):
                return pl.ds((field * PHASES + phase) * width + residue, ROWS, stride=residues)

            moist_scale = moist_weight * scale
            wind_scale = 0.5 * dt
            before = []
            for phase in range(PHASES):
                sums = [jnp.zeros((ROWS, LANES), F32)] * 2
                for residue in range(residues):
                    theta, moist, wind = (nat[natural(field, phase, residue), :] for field in range(3))
                    scaled = (scale * (theta + moist), moist_scale * moist, wind_scale * wind)
                    for field in range(3):
                        s0[at(field, phase, residue)] = scaled[field]
                    sums = [sums[variable] + scaled[variable] for variable in range(2)]
                before.append(sums)

            def unit(index, inner):
                for _ in range(SUB // 2):
                    substep(s0, s1)
                    substep(s1, s0)

                done = class_l == (index + 1).astype(F32)

                def keep(chunk, kept):
                    for residue in range(residues):
                        entry = chunk * residues + residue
                        saved[entry] = jnp.where(done, s0[entry], saved[entry])
                    return kept

                lax.fori_loop(0, jnp.where(mixed & (index + 1 < units), 3 * PHASES, 0), keep, 0)
                return inner

            lax.fori_loop(0, units, unit, 0)

            last = class_l == units.astype(F32)

            def restore(chunk, kept):
                for residue in range(residues):
                    entry = chunk * residues + residue
                    s0[entry] = jnp.where(last, s0[entry], saved[entry])
                return kept

            lax.fori_loop(0, jnp.where(mixed, 3 * PHASES, 0), restore, 0)
            heat_share = (2.0 / width) * steps * steps
            moist_share = heat_share * (1.0 / moist_weight)
            change = []
            for phase in range(PHASES):
                sums = [-value for value in before[phase]]
                for residue in range(residues):
                    sums = [sums[variable] + s0[at(variable, phase, residue)] for variable in range(2)]
                moist = moist_share * all_rows(sums[1])
                change.append((heat_share * all_rows(sums[0]) - moist, moist))

            active = class_m > 0.0
            second = lane_m >= levels
            level = jnp.where(second, lane_m - levels, lane_m)
            pick = jnp.minimum(level // PHASES * ROWS + sub_m, LANES - 1)
            which = lax.rem(level, PHASES)
            tendency = jnp.zeros((ROWS, LANES), F32)
            for phase in range(PHASES):
                found = [jnp.take_along_axis(change[phase][variable], pick, axis=1) for variable in range(2)]
                tendency = jnp.where(which == phase, jnp.where(second, found[1], found[0]), tendency)
            t_ref[pl.ds(base, ROWS), :] = jnp.where((lane_m < lane_class) & active, tendency, jnp.where(lane_m < lane_class, 0.0, mine))

        @pl.when(units <= 0)
        def _():
            t_ref[pl.ds(base, ROWS), :] = jnp.zeros((ROWS, LANES), F32)

        return carry

    lax.fori_loop(0, groups, run_group, 0)


def turned(fin, nat, group, field, width):
    residues = width // ROWS
    tiles = {}
    for half in range(2):
        for pair in range(2):
            phase = 2 * half + pair
            for residue in range(residues):
                spot = pl.ds(phase * width + residue, ROWS, stride=residues)
                nat[spot, :] = fin[group, (field * PHASES + phase) * residues + residue]
        back = nat[2 * half * width : 2 * half * width + LANES, :].T
        for step in range(LANES // ROWS):
            tiles[2 * step + half] = back[step * ROWS : (step + 1) * ROWS]
    return tiles


def weights_of(t_ref, base, lane_class):
    class_m = t_ref[pl.ds(base, ROWS), lane_class : lane_class + 1]
    steps = jnp.broadcast_to(jnp.maximum(class_m * SUB, 1.0), (ROWS, LANES))
    heat = 2.0 * steps * steps
    return class_m > 0.0, heat, heat * (1.0 / (1.0 - MOIST_BUOYANCY)), 2.0 * steps


def cloud_kernel(workers, slots, levels, width, meta, fin, t_ref, water, *refs):
    outs = refs[:workers]
    cl, nat, sems = refs[workers:]
    groups = fin.shape[0]
    tiles = levels * width // LANES
    lane_m = iota((ROWS, LANES), 1)
    lane_class = lanes_of(levels)[0]

    def run_group(group, carry):
        base = pl.multiple_of(group * ROWS, ROWS)

        @pl.when(meta[1, base] > 0)
        def _():
            _, _, moist_weight, _ = weights_of(t_ref, base, lane_class)
            parts = turned(fin, nat, group, 1, width)
            for tile in range(tiles):
                value = moist_weight * parts[tile]
                level = (LANES // width) * tile + lane_m // width
                saturated = 1.0 - 2.0 * (level.astype(F32) + 0.5) / levels
                spot = (pl.ds(base, ROWS), slice(tile * LANES, (tile + 1) * LANES))
                water[spot] = value
                cl[spot] = jnp.maximum(value - saturated, 0.0)

            def send(member, inner):
                index = base + member
                rank = meta[3, index]
                away = meta[2, index]
                for distance in range(workers):

                    @pl.when((away == distance) & (meta[1, index] > 0))
                    def _():
                        pltpu.make_async_copy(
                            cl.at[pl.ds(index, 1), :], outs[distance].at[pl.ds(rank, 1), :], sems.at[index]
                        ).start()

                return inner

            lax.fori_loop(0, ROWS, send, 0)

        return carry

    lax.fori_loop(0, groups, run_group, 0)

    def finish(index, carry):
        @pl.when(meta[1, index] > 0)
        def _():
            pltpu.make_async_copy(cl.at[pl.ds(index, 1), :], outs[0].at[pl.ds(0, 1), :], sems.at[index]).wait()

        return carry

    lax.fori_loop(0, slots, finish, 0)


def state_kernel(slots, levels, width, meta, fin, t_ref, water, xs, y_hbm, ys, nat, sems):
    groups = fin.shape[0]
    tiles = levels * width // LANES
    lane_class = lanes_of(levels)[0]

    def run_group(group, carry):
        base = pl.multiple_of(group * ROWS, ROWS)

        @pl.when(meta[1, base] > 0)
        def _():
            active, heat_weight, _, wind_weight = weights_of(t_ref, base, lane_class)
            heats = turned(fin, nat, group, 0, width)
            winds = turned(fin, nat, group, 2, width)
            for tile in range(tiles):
                lanes = slice(tile * LANES, (tile + 1) * LANES)
                moist = water[pl.ds(base, ROWS), lanes]
                values = (heat_weight * heats[tile] - moist, moist, wind_weight * winds[tile])
                for field in range(3):
                    spot = (field, pl.ds(base, ROWS), lanes)
                    ys[spot] = jnp.where(active, values[field], xs[spot])

        def store(source, member, inner):
            index = base + member

            @pl.when(index < slots)
            def _():
                pltpu.make_async_copy(
                    source.at[:, pl.ds(index, 1), :], y_hbm.at[:, pl.ds(meta[0, index], 1), :], sems.at[index]
                ).start()

            return inner

        @pl.when(meta[1, base] > 0)
        def _():
            lax.fori_loop(0, ROWS, functools.partial(store, ys), 0)

        @pl.when(meta[1, base] <= 0)
        def _():
            lax.fori_loop(0, ROWS, functools.partial(store, xs), 0)

        return carry

    lax.fori_loop(0, groups, run_group, 0)
    for index in range(slots):
        pltpu.make_async_copy(ys.at[:, pl.ds(index, 1), :], y_hbm.at[:, pl.ds(0, 1), :], sems.at[index]).wait()


def small(name, mib=8):
    return dict(compiler_params=pltpu.CompilerParams(vmem_limit_bytes=mib * MIB), name=name)


def run_models(row_blocks, state, levels):
    workers = len(row_blocks)
    _, slots, cells = state.shape
    width = cells // levels
    groups = -(-slots // ROWS)
    padded = groups * ROWS
    vmem = pl.BlockSpec(memory_space=pltpu.VMEM)
    entries = 3 * PHASES * (width // ROWS)
    return pl.pallas_call(
        functools.partial(model_kernel, workers, slots, levels, width),
        out_shape=[
            jax.ShapeDtypeStruct((groups, entries, ROWS, LANES), F32),
            jax.ShapeDtypeStruct((3, padded, cells), F32),
            jax.ShapeDtypeStruct((padded, LANES), F32),
            jax.ShapeDtypeStruct((ROWS, LANES), jnp.int32),
        ],
        in_specs=[vmem] * workers + [pl.BlockSpec(memory_space=pl.ANY)],
        out_specs=[vmem] * 4,
        scratch_shapes=[
            pltpu.VMEM((3 * PHASES * width, LANES), F32),
            pltpu.VMEM((entries, ROWS, LANES), F32),
            pltpu.VMEM((entries, ROWS, LANES), F32),
            pltpu.VMEM((6 + 3 * PHASES, ROWS, LANES), F32),
            pltpu.VMEM((padded, LANES), F32),
            pltpu.SMEM((ROWS, LANES), jnp.int32),
            pltpu.SemaphoreType.DMA,
            pltpu.SemaphoreType.DMA((padded,)),
        ],
        **small("cloud_models", 12),
    )(*row_blocks, state)


def condensate(workers, slots, levels, meta, fin, tendency):
    groups = fin.shape[0]
    padded = groups * ROWS
    width = fin.shape[1] // (3 * PHASES) * ROWS
    cells = levels * width
    vmem = pl.BlockSpec(memory_space=pltpu.VMEM)
    hbm = pl.BlockSpec(memory_space=pl.ANY)
    outs = pl.pallas_call(
        functools.partial(cloud_kernel, workers, slots, levels, width),
        out_shape=[jax.ShapeDtypeStruct((padded, cells), F32)]
        + [jax.ShapeDtypeStruct((slots // workers, cells), F32)] * workers,
        in_specs=[pl.BlockSpec(memory_space=pltpu.SMEM), vmem, vmem],
        out_specs=[vmem] + [hbm] * workers,
        scratch_shapes=[
            pltpu.VMEM((padded, cells), F32),
            pltpu.VMEM((PHASES * width, LANES), F32),
            pltpu.SemaphoreType.DMA((slots,)),
        ],
        **small("condensate"),
    )(meta, fin, tendency)
    return outs[0], outs[1:]


def state_rows(slots, levels, meta, fin, tendency, water, start):
    width = fin.shape[1] // (3 * PHASES) * ROWS
    fields, padded, cells = start.shape
    vmem = pl.BlockSpec(memory_space=pltpu.VMEM)
    return pl.pallas_call(
        functools.partial(state_kernel, slots, levels, width),
        out_shape=jax.ShapeDtypeStruct((fields, slots, cells), F32),
        in_specs=[pl.BlockSpec(memory_space=pltpu.SMEM)] + [vmem] * 4,
        out_specs=pl.BlockSpec(memory_space=pl.ANY),
        scratch_shapes=[
            pltpu.VMEM((fields, padded, cells), F32),
            pltpu.VMEM((PHASES * width, LANES), F32),
            pltpu.SemaphoreType.DMA((slots,)),
        ],
        **small("state_rows"),
    )(meta, fin, tendency, water, start)


def edge_kernel(levels, columns, workers, *refs):
    t_refs, out = refs[:workers], refs[workers]
    _, _, lane_column, lane_owner = lanes_of(levels)
    me = lax.axis_index("crm")
    wanted = jnp.where(me == 0, workers - 1, 0).astype(F32)
    rows = jnp.concatenate([ref[...] for ref in t_refs], axis=0)
    lane = iota(rows.shape, 1).astype(F32)
    owner = rows[:, lane_owner : lane_owner + 1]
    column = rows[:, lane_column : lane_column + 1]
    select = ((owner == wanted) & (column == lane + 1.0)).astype(F32)
    out[...] = dot_t(select, rows)[:columns]


def share_rows(index, weight):
    rows = weight[...]
    total = jnp.sum(rows, axis=0, keepdims=True)
    return index[...].astype(F32), rows / total


def inner_kernel(levels, columns, workers, *refs):
    t_refs = refs[:workers]
    index, weight, level_map, inner, maps = refs[workers:]
    _, _, lane_column, lane_owner = lanes_of(levels)
    me = lax.axis_index("crm")
    rows = jnp.concatenate([ref[...] for ref in t_refs], axis=0)
    owner = rows[:, lane_owner : lane_owner + 1]
    column = rows[:, lane_column : lane_column + 1]
    block = owner - me.astype(F32) + 1.0
    named = (column > 0.0) & (block >= 0.0) & (block <= 2.0)
    ident = jnp.where(named, block * columns + column - 1.0, -1.0)
    wanted, share = share_rows(index, weight)
    mix = jnp.zeros((rows.shape[0], columns), F32)
    for source in range(index.shape[0]):
        mix = mix + jnp.where(ident == wanted[source : source + 1], share[source : source + 1], 0.0)
    inner[...] = dot_t(mix, rows)
    spread_row = iota((levels, LANES), 0)
    spread_lane = iota((levels, LANES), 1)
    for variable in range(2):
        place = (spread_lane == spread_row + variable * levels).astype(F32)
        maps[variable] = dot_t(place, level_map[...])


def physics_kernel(columns, workers, inner, maps, edge, index, weight, out):
    me = lax.axis_index("crm")
    edge_sub = iota((columns, 1), 0)
    edge_block = jnp.where(me == 0, 0, jnp.where(me == workers - 1, 2, -3))
    ident = (edge_block * columns + edge_sub).astype(F32)
    wanted, share = share_rows(index, weight)
    mix = jnp.zeros((columns, columns), F32)
    for source in range(index.shape[0]):
        mix = mix + jnp.where(ident == wanted[source : source + 1], share[source : source + 1], 0.0)
    mixed = inner[...] + dot_t(mix, jnp.where(edge_block >= 0, edge[...], 0.0))
    for variable in range(2):
        out[:, variable, :] = dot(mixed, maps[variable])


def gather_kernel(columns, workers, *refs):
    target = refs[0]
    received = refs[1 : workers + 1]
    out, counts, sem = refs[workers + 1 :]
    me = lax.axis_index("crm")
    for worker in range(workers):
        counts[worker] = 0

    def start(column, carry):
        worker = target[column]
        rank = counts[worker]
        counts[worker] = rank + 1
        for distance in range(workers):

            @pl.when(worker == (me ^ distance))
            def _():
                pltpu.make_async_copy(
                    received[distance].at[pl.ds(rank, 1), :], out.at[pl.ds(column, 1), :], sem.at[column]
                ).start()

        return carry

    lax.fori_loop(0, columns, start, 0)

    def finish(column, carry):
        pltpu.make_async_copy(received[0].at[pl.ds(0, 1), :], out.at[pl.ds(column, 1), :], sem.at[column]).wait()
        return carry

    lax.fori_loop(0, columns, finish, 0)


def exchange(blocks, axis):
    size = lax.axis_size(axis)
    out = [blocks[0]]
    for distance in range(1, size):
        out.append(lax.ppermute(blocks[distance], axis, [(i, i ^ distance) for i in range(size)]))
    return out


def body(crm_state, forcing, target, cost_class, level_map, remap_index, remap_weight):
    workers = lax.axis_size("crm")
    groups = lax.axis_size("grp")
    columns = forcing.shape[0]
    slots, _, cells = crm_state.shape
    capacity = slots // workers
    levels, gcm = level_map.shape
    vmem = pl.BlockSpec(memory_space=pltpu.VMEM)
    hbm = pl.BlockSpec(memory_space=pl.ANY)

    rows = pack(target, cost_class, forcing, level_map, workers, capacity)
    row_blocks = exchange([rows] * workers, "crm")
    fin, start, tendency, meta = run_models(row_blocks, pltpu.with_memory_space_constraint(crm_state.transpose(1, 0, 2), pltpu.HBM), levels)
    tendencies = exchange([tendency] * workers, "crm")
    water, clouds = condensate(workers, slots, levels, meta, fin, tendency)
    clouds = exchange(clouds, "crm")

    edge = pl.pallas_call(
        functools.partial(edge_kernel, levels, columns, workers),
        out_shape=jax.ShapeDtypeStruct((columns, LANES), F32),
        in_specs=[vmem] * workers,
        out_specs=vmem,
        **small("edge_columns"),
    )(*tendencies)
    pairs = []
    for group in range(groups):
        after = (group + 1) % groups
        pairs.append((group * workers, after * workers))
        pairs.append((after * workers + workers - 1, group * workers + workers - 1))
    edge, meta, tendencies = lax.optimization_barrier((edge, meta, tendencies))
    edge = lax.ppermute(edge, ("grp", "crm"), pairs)
    inner, maps = pl.pallas_call(
        functools.partial(inner_kernel, levels, columns, workers),
        out_shape=[jax.ShapeDtypeStruct((columns, LANES), F32), jax.ShapeDtypeStruct((2, LANES, gcm), F32)],
        in_specs=[vmem] * (workers + 3),
        out_specs=[vmem] * 2,
        **small("inner_blocks"),
    )(*tendencies, remap_index.T, remap_weight.T, level_map)
    state = state_rows(slots, levels, meta, fin, tendency, water, start)
    cloud_water = pl.pallas_call(
        functools.partial(gather_kernel, columns, workers),
        out_shape=jax.ShapeDtypeStruct((columns, cells), F32),
        in_specs=[pl.BlockSpec(memory_space=pltpu.SMEM)] + [hbm] * workers,
        out_specs=hbm,
        scratch_shapes=[pltpu.SMEM((workers,), jnp.int32), pltpu.SemaphoreType.DMA((columns,))],
        **small("cloud_rows"),
    )(target, *clouds)
    physics = pl.pallas_call(
        functools.partial(physics_kernel, columns, workers),
        out_shape=jax.ShapeDtypeStruct((columns, 2, gcm), F32),
        in_specs=[vmem] * 5,
        out_specs=vmem,
        **small("physics_cells"),
    )(inner, maps, edge, remap_index.T, remap_weight.T)
    return state.transpose(1, 0, 2), cloud_water, physics


def solution(mesh):
    wide = P(("grp", "crm"), None, None)
    flat = P(("grp", "crm"), None)
    line = P(("grp", "crm"))
    in_specs = (wide, wide, line, line, P(), flat, flat)
    out_specs = (wide, flat, wide)
    return jax.shard_map(body, mesh=mesh, in_specs=in_specs, out_specs=out_specs, check_vma=False)
```

```python
import functools

import jax
import jax.numpy as jnp
from jax import lax
from jax.experimental import pallas as pl
from jax.experimental.pallas import tpu as pltpu
from jax.sharding import PartitionSpec as P

CLASSES = 3
SUB = 4
DIFFUSE_HORIZ = 0.2
DIFFUSE_VERT = 0.1
CONDENSE_RATE = 3.0
LINEAR_DRAG = 0.1
MOIST_BUOYANCY = 0.6
HIGHEST = lax.Precision.HIGHEST
F32 = jnp.float32
LANES = 128
ROWS = 8
PHASES = 4
MIB = 1 << 20


def in_hbm(x):
    return pltpu.with_memory_space_constraint(x, pltpu.HBM)


def iota(shape, axis):
    return lax.broadcasted_iota(jnp.int32, shape, axis)


def dot_t(lhs, rhs):
    return lax.dot_general(lhs, rhs, (((0,), (0,)), ((), ())), precision=HIGHEST, preferred_element_type=F32)


def dot(lhs, rhs):
    return jnp.dot(lhs, rhs, precision=HIGHEST, preferred_element_type=F32)


def all_rows(x):
    x = x + pltpu.roll(x, 4, 0)
    x = x + pltpu.roll(x, 2, 0)
    return x + pltpu.roll(x, 1, 0)


def lanes_of(levels):
    base = 2 * levels
    return base, base + 1, base + 2, base + 3


def pack_kernel(capacity, workers, target_hbm, cost_hbm, forcing_hbm, level_hbm, rows, target, cost, forcing, level_map, counts, sems):
    pairs = ((target_hbm, target), (cost_hbm, cost), (forcing_hbm, forcing), (level_hbm, level_map))
    copies = [pltpu.make_async_copy(source, place, sems.at[i]) for i, (source, place) in enumerate(pairs)]
    for copy in copies:
        copy.start()
    for copy in copies:
        copy.wait()
    levels, gcm = level_map.shape
    columns = forcing.shape[0]
    lane_class, lane_slot, lane_column, lane_owner = lanes_of(levels)
    me = lax.axis_index("crm")
    for worker in range(workers):
        counts[worker] = 0
    sub = iota((columns, LANES), 0)
    lane = iota((columns, LANES), 1)
    classes = jnp.zeros((columns, LANES), F32)
    slots = jnp.zeros((columns, LANES), F32)
    for column in range(columns):
        worker = target[column]
        rank = counts[worker]
        counts[worker] = rank + 1
        slot = (worker * workers + me) * capacity + rank
        classes = jnp.where(sub == column, cost[column].astype(F32), classes)
        slots = jnp.where(sub == column, slot.astype(F32), slots)
    spread_row = iota((levels, LANES), 0)
    spread_lane = iota((levels, LANES), 1)
    mapped = jnp.zeros((columns, LANES), F32)
    for variable in range(2):
        place = (spread_lane == spread_row + variable * levels).astype(F32)
        mapped = mapped + dot(forcing[:, variable, :], dot_t(level_map[...], place))
    meta = jnp.where(lane == lane_class, classes, 0.0)
    meta = jnp.where(lane == lane_slot, slots, meta)
    meta = jnp.where(lane == lane_column, (sub + 1).astype(F32), meta)
    meta = jnp.where(lane == lane_owner, me.astype(F32), meta)
    rows[...] = jnp.where(lane < lane_class, mapped, meta)


def pack(target, cost, forcing, level_map, workers, capacity):
    columns = forcing.shape[0]
    return pl.pallas_call(
        functools.partial(pack_kernel, capacity, workers),
        out_shape=jax.ShapeDtypeStruct((columns, LANES), F32),
        in_specs=[pl.BlockSpec(memory_space=pl.ANY)] * 4,
        out_specs=pl.BlockSpec(memory_space=pltpu.VMEM),
        scratch_shapes=[
            pltpu.SMEM(target.shape, jnp.int32),
            pltpu.SMEM(cost.shape, jnp.int32),
            pltpu.VMEM(forcing.shape, F32),
            pltpu.VMEM(level_map.shape, F32),
            pltpu.SMEM((workers,), jnp.int32),
            pltpu.SemaphoreType.DMA((4,)),
        ],
        compiler_params=pltpu.CompilerParams(vmem_limit_bytes=8 * MIB),
        name="pack_forcing",
    )(*(in_hbm(x) for x in (target, cost, forcing, level_map)))


def model_kernel(workers, slots, levels, width, *refs):
    row_refs = refs[:workers]
    x_hbm, fin, xs, t_ref, meta_v, nat, s1, saved, coef, rows_s, meta_s, sem_meta, sem_in = refs[workers:]
    groups = xs.shape[1] // ROWS
    padded = groups * ROWS
    capacity = slots // workers
    tiles = levels * width // LANES
    residues = width // ROWS
    lane_class, lane_slot, lane_column, lane_owner = lanes_of(levels)
    me = lax.axis_index("crm")

    rows = jnp.concatenate([ref[...] for ref in row_refs], axis=0)
    lane_c = iota(rows.shape, 1)
    local = rows[:, lane_slot : lane_slot + 1] - (me * slots).astype(F32)
    member = (local == lane_c.astype(F32)) & (lane_c < slots)
    class_row = jnp.sum(jnp.where(member, rows[:, lane_class : lane_class + 1], 0.0), axis=0, keepdims=True)
    sub_p = iota((padded, LANES), 0)
    lane_p = iota((padded, LANES), 1)
    key_row = class_row * LANES + (LANES - 1 - iota((1, LANES), 1)).astype(F32)
    key_col = jnp.sum(jnp.where(sub_p == lane_p, key_row, 0.0), axis=1, keepdims=True)
    class_col = jnp.sum(jnp.where(sub_p == lane_p, class_row, 0.0), axis=1, keepdims=True)
    ahead_row = ((key_col > key_row) & (sub_p < slots)).astype(F32)
    place_row = jnp.sum(ahead_row, axis=0, keepdims=True)
    ahead_col = ((key_row > key_col) & (lane_p < slots)).astype(F32)
    place_col = jnp.sum(ahead_col, axis=1, keepdims=True)
    here = (place_col == lane_p.astype(F32)) & (sub_p < slots)
    order = jnp.sum(jnp.where(here, sub_p.astype(F32), 0.0), axis=0, keepdims=True)
    class_sorted = jnp.sum(jnp.where(here, class_col, 0.0), axis=0, keepdims=True)
    sub_m = iota((ROWS, LANES), 0)
    lane_m = iota((ROWS, LANES), 1)
    owner_row = jnp.floor((order + 0.5) * (1.0 / capacity))
    rank_row = order - owner_row * capacity
    away_row = owner_row.astype(jnp.int32) ^ me
    table = jnp.where(sub_m == 0, order, jnp.where(sub_m == 1, class_sorted, rank_row)).astype(jnp.int32)
    table = jnp.where(sub_m == 2, away_row, table)
    meta_v[...] = jnp.where(sub_m == 4, place_row.astype(jnp.int32), table)
    fetch = pltpu.make_async_copy(meta_v, meta_s, sem_meta)
    fetch.start()
    place_of = jnp.sum(jnp.where(member, place_row + 1.0, 0.0), axis=1, keepdims=True) - 1.0
    rows_s[...] = dot_t((place_of == lane_c.astype(F32)).astype(F32), rows)[:padded]
    fetch.wait()

    def load(index, carry):
        slot = meta_s[0, index]
        pltpu.make_async_copy(x_hbm.at[:, pl.ds(slot, 1), :], xs.at[:, pl.ds(index, 1), :], sem_in.at[index]).start()
        return carry

    lax.fori_loop(0, padded, load, 0, unroll=4)

    model_of = lax.rem(lane_m, ROWS)
    step_of = lane_m // ROWS
    own = model_of == sub_m

    def coef_index(name, phase=0):
        names = ("a", "bx", "c0", "c1", "aw", "ac")
        return names.index(name) if name in names else len(names) + ("fh", "fq", "fs").index(name) * PHASES + phase

    def at(field, phase, residue):
        return (field * PHASES + phase) * residues + residue

    def substep(src, dst):
        def self_at(field, phase, residue):
            return src[at(field, phase, residue)]

        def above(field, phase, residue):
            if phase < PHASES - 1:
                return src[at(field, phase + 1, residue)]
            return pltpu.roll(src[at(field, 0, residue)], LANES - ROWS, 1)

        def below(field, phase, residue):
            if phase > 0:
                return src[at(field, phase - 1, residue)]
            return pltpu.roll(src[at(field, PHASES - 1, residue)], ROWS, 1)

        a, bx, aw, ac = (coef[coef_index(name)] for name in ("a", "bx", "aw", "ac"))
        for phase in range(PHASES):
            c1 = coef[coef_index("c0" if phase < 2 else "c1")]
            fh, fq, fs = (coef[coef_index(name, phase)] for name in ("fh", "fq", "fs"))
            def around(field, residue):
                if residue > 0:
                    left = self_at(field, phase, residue - 1)
                else:
                    left = pltpu.roll(self_at(field, phase, residues - 1), 1, 0)
                if residue < residues - 1:
                    return left + self_at(field, phase, residue + 1)
                return left + pltpu.roll(self_at(field, phase, 0), ROWS - 1, 0)

            pushed = []
            for residue in range(residues):
                wind = self_at(2, phase, residue)
                new_wind = (aw * wind + (self_at(0, phase, residue) - self_at(1, phase, residue))) + bx * around(2, residue)
                pushed.append(new_wind + c1 * (above(2, phase, residue) + below(2, phase, residue)))
            total = pushed
            while len(total) > 1:
                total = [sum(total[i : i + 2]) for i in range(0, len(total), 2)]
            mean = all_rows(total[0]) * (1.0 / width)
            for residue in range(residues):
                dst[at(2, phase, residue)] = pushed[residue] - mean
            for residue in range(residues):
                heat, moist, wind = (self_at(field, phase, residue) for field in range(3))
                up_coef = c1 - wind
                down_coef = c1 + wind
                new_heat = (a * heat + fh) + bx * around(0, residue)
                dst[at(0, phase, residue)] = new_heat + (
                    up_coef * above(0, phase, residue) + down_coef * below(0, phase, residue)
                )
                new_moist = jnp.minimum(a * moist + fq, ac * moist + fs) + bx * around(1, residue)
                dst[at(1, phase, residue)] = new_moist + (
                    up_coef * above(1, phase, residue) + down_coef * below(1, phase, residue)
                )

    def run_group(group, carry):
        base = pl.multiple_of(group * ROWS, ROWS)
        units = meta_s[1, base]
        mixed = meta_s[1, base + ROWS - 1] != units

        for member in range(ROWS):
            index = base + member
            pltpu.make_async_copy(x_hbm.at[:, pl.ds(0, 1), :], xs.at[:, pl.ds(index, 1), :], sem_in.at[index]).wait()

        s0 = fin.at[group]

        @pl.when(units > 0)
        def _():
            mine = rows_s[pl.ds(base, ROWS), :]
            class_m = mine[:, lane_class : lane_class + 1]
            class_l = all_rows(jnp.where(own, class_m, 0.0))
            steps = jnp.maximum(class_l * SUB, 1.0)
            dt = 1.0 / steps
            scale = 0.5 * dt * dt
            moist_weight = 1.0 - MOIST_BUOYANCY
            diffuse = 1.0 - 2.0 * (DIFFUSE_HORIZ + DIFFUSE_VERT) * dt
            coef[coef_index("a")] = diffuse
            coef[coef_index("bx")] = DIFFUSE_HORIZ * dt
            inside = [(PHASES * step_of + phase) < levels for phase in range(PHASES)]
            coef[coef_index("c0")] = jnp.where(inside[1], DIFFUSE_VERT * dt, 0.0)
            coef[coef_index("c1")] = jnp.where(inside[3], DIFFUSE_VERT * dt, 0.0)
            coef[coef_index("aw")] = diffuse - LINEAR_DRAG * dt
            coef[coef_index("ac")] = diffuse - CONDENSE_RATE * dt
            for phase in range(PHASES):
                level = PHASES * step_of + phase
                pick = jnp.minimum(level, levels - 1)
                keep = own & inside[phase]
                force = [
                    all_rows(jnp.where(keep, jnp.take_along_axis(mine, pick + variable * levels, axis=1), 0.0))
                    for variable in range(2)
                ]
                saturated = jnp.where(inside[phase], 1.0 - 2.0 * (level.astype(F32) + 0.5) / levels, 0.0)
                fq = (moist_weight * scale * dt) * force[1]
                coef[coef_index("fh", phase)] = (scale * dt) * (force[0] + force[1])
                coef[coef_index("fq", phase)] = fq
                coef[coef_index("fs", phase)] = fq + (CONDENSE_RATE * moist_weight) * dt * scale * saturated

            zero = jnp.zeros((ROWS, LANES), F32)
            for field in range(3):
                for half in range(2):
                    parts = []
                    for step in range(LANES // ROWS):
                        tile = 2 * step + half
                        parts.append(xs[field, pl.ds(base, ROWS), tile * LANES : (tile + 1) * LANES] if tile < tiles else zero)
                    start = (field * PHASES + 2 * half) * width
                    nat[start : start + LANES, :] = jnp.concatenate(parts, axis=0).T

            def natural(field, phase, residue):
                return pl.ds((field * PHASES + phase) * width + residue, ROWS, stride=residues)

            moist_scale = moist_weight * scale
            wind_scale = 0.5 * dt
            before = []
            for phase in range(PHASES):
                sums = [jnp.zeros((ROWS, LANES), F32)] * 2
                for residue in range(residues):
                    theta, moist, wind = (nat[natural(field, phase, residue), :] for field in range(3))
                    scaled = (scale * (theta + moist), moist_scale * moist, wind_scale * wind)
                    for field in range(3):
                        s0[at(field, phase, residue)] = scaled[field]
                    sums = [sums[variable] + scaled[variable] for variable in range(2)]
                before.append(sums)

            def unit(index, inner):
                for _ in range(SUB // 2):
                    substep(s0, s1)
                    substep(s1, s0)

                done = class_l == (index + 1).astype(F32)

                def keep(chunk, kept):
                    for residue in range(residues):
                        entry = chunk * residues + residue
                        saved[entry] = jnp.where(done, s0[entry], saved[entry])
                    return kept

                lax.fori_loop(0, jnp.where(mixed & (index + 1 < units), 3 * PHASES, 0), keep, 0)
                return inner

            lax.fori_loop(0, units, unit, 0)

            last = class_l == units.astype(F32)

            def restore(chunk, kept):
                for residue in range(residues):
                    entry = chunk * residues + residue
                    s0[entry] = jnp.where(last, s0[entry], saved[entry])
                return kept

            lax.fori_loop(0, jnp.where(mixed, 3 * PHASES, 0), restore, 0)
            heat_share = (2.0 / width) * steps * steps
            moist_share = heat_share * (1.0 / moist_weight)
            change = []
            for phase in range(PHASES):
                sums = [-value for value in before[phase]]
                for residue in range(residues):
                    sums = [sums[variable] + s0[at(variable, phase, residue)] for variable in range(2)]
                moist = moist_share * all_rows(sums[1])
                change.append((heat_share * all_rows(sums[0]) - moist, moist))

            active = class_m > 0.0
            second = lane_m >= levels
            level = jnp.where(second, lane_m - levels, lane_m)
            pick = jnp.minimum(level // PHASES * ROWS + sub_m, LANES - 1)
            which = lax.rem(level, PHASES)
            tendency = jnp.zeros((ROWS, LANES), F32)
            for phase in range(PHASES):
                found = [jnp.take_along_axis(change[phase][variable], pick, axis=1) for variable in range(2)]
                tendency = jnp.where(which == phase, jnp.where(second, found[1], found[0]), tendency)
            t_ref[pl.ds(base, ROWS), :] = jnp.where((lane_m < lane_class) & active, tendency, jnp.where(lane_m < lane_class, 0.0, mine))

        @pl.when(units <= 0)
        def _():
            t_ref[pl.ds(base, ROWS), :] = jnp.zeros((ROWS, LANES), F32)

        return carry

    lax.fori_loop(0, groups, run_group, 0)


def turned(fin, nat, group, field, width):
    residues = width // ROWS
    tiles = {}
    for half in range(2):
        for pair in range(2):
            phase = 2 * half + pair
            for residue in range(residues):
                spot = pl.ds(phase * width + residue, ROWS, stride=residues)
                nat[spot, :] = fin[group, (field * PHASES + phase) * residues + residue]
        back = nat[2 * half * width : 2 * half * width + LANES, :].T
        for step in range(LANES // ROWS):
            tiles[2 * step + half] = back[step * ROWS : (step + 1) * ROWS]
    return tiles


def weights_of(t_ref, base, lane_class):
    class_m = t_ref[pl.ds(base, ROWS), lane_class : lane_class + 1]
    steps = jnp.broadcast_to(jnp.maximum(class_m * SUB, 1.0), (ROWS, LANES))
    heat = 2.0 * steps * steps
    return class_m > 0.0, heat, heat * (1.0 / (1.0 - MOIST_BUOYANCY)), 2.0 * steps


def cloud_kernel(levels, width, meta, fin, t_ref, water, cl, nat):
    groups = fin.shape[0]
    tiles = levels * width // LANES
    block = -(-tiles // ROWS) * ROWS
    lane_m = iota((ROWS, LANES), 1)
    lane_class = lanes_of(levels)[0]

    def run_group(group, carry):
        base = pl.multiple_of(group * ROWS, ROWS)

        @pl.when(meta[1, base] > 0)
        def _():
            _, _, moist_weight, _ = weights_of(t_ref, base, lane_class)
            parts = turned(fin, nat, group, 1, width)
            for tile in range(tiles):
                value = moist_weight * parts[tile]
                level = (LANES // width) * tile + lane_m // width
                saturated = 1.0 - 2.0 * (level.astype(F32) + 0.5) / levels
                water[pl.ds(base, ROWS), tile * LANES : (tile + 1) * LANES] = value
                cl[pl.ds(base * block + tile, ROWS, stride=block), :] = jnp.maximum(value - saturated, 0.0)

        return carry

    lax.fori_loop(0, groups, run_group, 0)


def send_kernel(workers, capacity, meta, cl, *outs):
    block = outs[0].shape[0] // capacity
    me = lax.axis_index("crm")
    for distance in range(workers):
        first = (me ^ distance) * capacity
        for rank in range(capacity):
            source = pl.multiple_of(meta[4, first + rank] * block, ROWS)
            outs[distance][rank * block : (rank + 1) * block, :] = cl[pl.ds(source, block), :]


def state_kernel(slots, levels, width, meta, fin, t_ref, water, xs, y_hbm, ys, nat, sems):
    groups = fin.shape[0]
    tiles = levels * width // LANES
    lane_class = lanes_of(levels)[0]

    def run_group(group, carry):
        base = pl.multiple_of(group * ROWS, ROWS)

        @pl.when(meta[1, base] > 0)
        def _():
            active, heat_weight, _, wind_weight = weights_of(t_ref, base, lane_class)
            heats = turned(fin, nat, group, 0, width)
            winds = turned(fin, nat, group, 2, width)
            for tile in range(tiles):
                lanes = slice(tile * LANES, (tile + 1) * LANES)
                moist = water[pl.ds(base, ROWS), lanes]
                values = (heat_weight * heats[tile] - moist, moist, wind_weight * winds[tile])
                for field in range(3):
                    spot = (field, pl.ds(base, ROWS), lanes)
                    ys[spot] = jnp.where(active, values[field], xs[spot])

        def store(source, member, inner):
            index = base + member

            @pl.when(index < slots)
            def _():
                pltpu.make_async_copy(
                    source.at[:, pl.ds(index, 1), :], y_hbm.at[:, pl.ds(meta[0, index], 1), :], sems.at[index]
                ).start()

            return inner

        @pl.when(meta[1, base] > 0)
        def _():
            lax.fori_loop(0, ROWS, functools.partial(store, ys), 0)

        @pl.when(meta[1, base] <= 0)
        def _():
            lax.fori_loop(0, ROWS, functools.partial(store, xs), 0)

        return carry

    lax.fori_loop(0, groups, run_group, 0)
    for index in range(slots):
        pltpu.make_async_copy(ys.at[:, pl.ds(index, 1), :], y_hbm.at[:, pl.ds(0, 1), :], sems.at[index]).wait()


def small(name, mib=8, moved=1 << 20):
    cost = pl.CostEstimate(flops=0, bytes_accessed=moved, transcendentals=0)
    return dict(compiler_params=pltpu.CompilerParams(vmem_limit_bytes=mib * MIB), name=name, cost_estimate=cost)


def run_models(row_blocks, state, levels):
    workers = len(row_blocks)
    _, slots, cells = state.shape
    width = cells // levels
    groups = -(-slots // ROWS)
    padded = groups * ROWS
    vmem = pl.BlockSpec(memory_space=pltpu.VMEM)
    entries = 3 * PHASES * (width // ROWS)
    return pl.pallas_call(
        functools.partial(model_kernel, workers, slots, levels, width),
        out_shape=[
            jax.ShapeDtypeStruct((groups, entries, ROWS, LANES), F32),
            jax.ShapeDtypeStruct((3, padded, cells), F32),
            jax.ShapeDtypeStruct((padded, LANES), F32),
            jax.ShapeDtypeStruct((ROWS, LANES), jnp.int32),
        ],
        in_specs=[vmem] * workers + [pl.BlockSpec(memory_space=pl.ANY)],
        out_specs=[vmem] * 4,
        scratch_shapes=[
            pltpu.VMEM((3 * PHASES * width, LANES), F32),
            pltpu.VMEM((entries, ROWS, LANES), F32),
            pltpu.VMEM((entries, ROWS, LANES), F32),
            pltpu.VMEM((6 + 3 * PHASES, ROWS, LANES), F32),
            pltpu.VMEM((padded, LANES), F32),
            pltpu.SMEM((ROWS, LANES), jnp.int32),
            pltpu.SemaphoreType.DMA,
            pltpu.SemaphoreType.DMA((padded,)),
        ],
        **small("cloud_models", 12, 40 << 20),
    )(*row_blocks, state)


def condensate(cells, levels, meta, fin, tendency):
    padded = fin.shape[0] * ROWS
    width = cells // levels
    vmem = pl.BlockSpec(memory_space=pltpu.VMEM)
    block = -(-(cells // LANES) // ROWS) * ROWS
    return pl.pallas_call(
        functools.partial(cloud_kernel, levels, width),
        out_shape=[jax.ShapeDtypeStruct((padded, cells), F32), jax.ShapeDtypeStruct((padded * block, LANES), F32)],
        in_specs=[pl.BlockSpec(memory_space=pltpu.SMEM), vmem, vmem],
        out_specs=[vmem] * 2,
        scratch_shapes=[pltpu.VMEM((PHASES * width, LANES), F32)],
        **small("condensate", moved=8 << 20),
    )(meta, fin, tendency)


def send_blocks(workers, slots, meta, blocks):
    capacity = slots // workers
    block = blocks.shape[0] // (-(-slots // ROWS) * ROWS)
    vmem = pl.BlockSpec(memory_space=pltpu.VMEM)
    return pl.pallas_call(
        functools.partial(send_kernel, workers, capacity),
        out_shape=[jax.ShapeDtypeStruct((capacity * block, LANES), F32)] * workers,
        in_specs=[pl.BlockSpec(memory_space=pltpu.SMEM), vmem],
        out_specs=[vmem] * workers,
        **small("send_blocks"),
    )(meta, blocks)


def state_rows(slots, levels, meta, fin, tendency, water, start):
    width = fin.shape[1] // (3 * PHASES) * ROWS
    fields, padded, cells = start.shape
    vmem = pl.BlockSpec(memory_space=pltpu.VMEM)
    return pl.pallas_call(
        functools.partial(state_kernel, slots, levels, width),
        out_shape=jax.ShapeDtypeStruct((fields, slots, cells), F32),
        in_specs=[pl.BlockSpec(memory_space=pltpu.SMEM)] + [vmem] * 4,
        out_specs=pl.BlockSpec(memory_space=pl.ANY),
        scratch_shapes=[
            pltpu.VMEM((fields, padded, cells), F32),
            pltpu.VMEM((PHASES * width, LANES), F32),
            pltpu.SemaphoreType.DMA((slots,)),
        ],
        **small("state_rows", moved=12 << 20),
    )(meta, fin, tendency, water, start)


def edge_kernel(levels, columns, workers, *refs):
    t_refs, out = refs[:workers], refs[workers]
    _, _, lane_column, lane_owner = lanes_of(levels)
    me = lax.axis_index("crm")
    wanted = jnp.where(me == 0, workers - 1, 0).astype(F32)
    rows = jnp.concatenate([ref[...] for ref in t_refs], axis=0)
    lane = iota(rows.shape, 1).astype(F32)
    owner = rows[:, lane_owner : lane_owner + 1]
    column = rows[:, lane_column : lane_column + 1]
    select = ((owner == wanted) & (column == lane + 1.0)).astype(F32)
    out[...] = dot_t(select, rows)[:columns]


def share_rows(index, weight):
    rows = weight[...]
    total = jnp.sum(rows, axis=0, keepdims=True)
    return index[...].astype(F32), rows / total


def inner_kernel(levels, columns, workers, *refs):
    t_refs = refs[:workers]
    index, weight, level_map, inner, maps = refs[workers:]
    _, _, lane_column, lane_owner = lanes_of(levels)
    me = lax.axis_index("crm")
    rows = jnp.concatenate([ref[...] for ref in t_refs], axis=0)
    owner = rows[:, lane_owner : lane_owner + 1]
    column = rows[:, lane_column : lane_column + 1]
    block = owner - me.astype(F32) + 1.0
    named = (column > 0.0) & (block >= 0.0) & (block <= 2.0)
    ident = jnp.where(named, block * columns + column - 1.0, -1.0)
    wanted, share = share_rows(index, weight)
    mix = jnp.zeros((rows.shape[0], columns), F32)
    for source in range(index.shape[0]):
        mix = mix + jnp.where(ident == wanted[source : source + 1], share[source : source + 1], 0.0)
    inner[...] = dot_t(mix, rows)
    spread_row = iota((levels, LANES), 0)
    spread_lane = iota((levels, LANES), 1)
    for variable in range(2):
        place = (spread_lane == spread_row + variable * levels).astype(F32)
        maps[variable] = dot_t(place, level_map[...])


def physics_kernel(columns, workers, inner, maps, edge, index, weight, out):
    me = lax.axis_index("crm")
    edge_sub = iota((columns, 1), 0)
    edge_block = jnp.where(me == 0, 0, jnp.where(me == workers - 1, 2, -3))
    ident = (edge_block * columns + edge_sub).astype(F32)
    wanted, share = share_rows(index, weight)
    mix = jnp.zeros((columns, columns), F32)
    for source in range(index.shape[0]):
        mix = mix + jnp.where(ident == wanted[source : source + 1], share[source : source + 1], 0.0)
    mixed = inner[...] + dot_t(mix, jnp.where(edge_block >= 0, edge[...], 0.0))
    for variable in range(2):
        out[:, variable, :] = dot(mixed, maps[variable])


def gather_kernel(columns, capacity, workers, *refs):
    target = refs[0]
    received = refs[1 : workers + 1]
    out, counts, column_of, places = refs[workers + 1 :]
    tiles = out.shape[1] // LANES
    block = -(-tiles // ROWS) * ROWS
    me = lax.axis_index("crm")
    for worker in range(workers):
        counts[worker] = 0
    for entry in range(workers * capacity):
        column_of[entry] = columns
    for column in range(columns):
        worker = target[column]
        rank = counts[worker]
        counts[worker] = rank + 1
        column_of[(worker ^ me) * capacity + rank] = column
    for distance in range(workers):
        for rank in range(capacity):
            place = pl.multiple_of(column_of[distance * capacity + rank] * block, ROWS)
            places[pl.ds(place, block), :] = received[distance][rank * block : (rank + 1) * block, :]
    for base in range(0, columns, ROWS):
        count = min(ROWS, columns - base)
        for tile in range(tiles):
            rows = places[pl.ds(base * block + tile, count, stride=block), :]
            out[base : base + count, tile * LANES : (tile + 1) * LANES] = rows


def exchange(blocks, axis):
    size = lax.axis_size(axis)
    out = [blocks[0]]
    for distance in range(1, size):
        out.append(lax.ppermute(blocks[distance], axis, [(i, i ^ distance) for i in range(size)]))
    return out


def body(crm_state, forcing, target, cost_class, level_map, remap_index, remap_weight):
    workers = lax.axis_size("crm")
    groups = lax.axis_size("grp")
    columns = forcing.shape[0]
    slots, _, cells = crm_state.shape
    capacity = slots // workers
    levels, gcm = level_map.shape
    vmem = pl.BlockSpec(memory_space=pltpu.VMEM)

    rows = pack(target, cost_class, forcing, level_map, workers, capacity)
    row_blocks = exchange([rows] * workers, "crm")
    fin, start, tendency, meta = run_models(row_blocks, in_hbm(crm_state.transpose(1, 0, 2)), levels)
    tendencies = exchange([tendency] * workers, "crm")
    water, blocks = condensate(cells, levels, meta, fin, tendency)
    tendencies, blocks = lax.optimization_barrier((tendencies, blocks))
    clouds = exchange(send_blocks(workers, slots, meta, blocks), "crm")

    edge = pl.pallas_call(
        functools.partial(edge_kernel, levels, columns, workers),
        out_shape=jax.ShapeDtypeStruct((columns, LANES), F32),
        in_specs=[vmem] * workers,
        out_specs=vmem,
        **small("edge_columns"),
    )(*tendencies)
    pairs = []
    for group in range(groups):
        after = (group + 1) % groups
        pairs.append((group * workers, after * workers))
        pairs.append((after * workers + workers - 1, group * workers + workers - 1))
    edge, meta, tendencies = lax.optimization_barrier((edge, meta, tendencies))
    edge = lax.ppermute(edge, ("grp", "crm"), pairs)
    inner, maps = pl.pallas_call(
        functools.partial(inner_kernel, levels, columns, workers),
        out_shape=[jax.ShapeDtypeStruct((columns, LANES), F32), jax.ShapeDtypeStruct((2, LANES, gcm), F32)],
        in_specs=[vmem] * (workers + 3),
        out_specs=[vmem] * 2,
        **small("inner_blocks"),
    )(*tendencies, remap_index.T, remap_weight.T, level_map)
    state = state_rows(slots, levels, meta, fin, tendency, water, start)
    block = clouds[0].shape[0] // capacity
    cloud_water = pl.pallas_call(
        functools.partial(gather_kernel, columns, capacity, workers),
        out_shape=jax.ShapeDtypeStruct((columns, cells), F32),
        in_specs=[pl.BlockSpec(memory_space=pltpu.SMEM)] + [vmem] * workers,
        out_specs=vmem,
        scratch_shapes=[
            pltpu.SMEM((workers,), jnp.int32),
            pltpu.SMEM((slots,), jnp.int32),
            pltpu.VMEM(((columns + 1) * block, LANES), F32),
        ],
        **small("cloud_rows"),
    )(target, *clouds)
    physics = pl.pallas_call(
        functools.partial(physics_kernel, columns, workers),
        out_shape=jax.ShapeDtypeStruct((columns, 2, gcm), F32),
        in_specs=[vmem] * 5,
        out_specs=vmem,
        **small("physics_cells"),
    )(inner, maps, edge, remap_index.T, remap_weight.T)
    return state.transpose(1, 0, 2), cloud_water, physics


def solution(mesh):
    wide = P(("grp", "crm"), None, None)
    flat = P(("grp", "crm"), None)
    line = P(("grp", "crm"))
    in_specs = (wide, wide, line, line, P(), flat, flat)
    out_specs = (wide, flat, wide)
    return jax.shard_map(body, mesh=mesh, in_specs=in_specs, out_specs=out_specs, check_vma=False)
```

```python
import functools

import jax
import jax.numpy as jnp
from jax import lax
from jax.experimental import pallas as pl
from jax.experimental.pallas import tpu as pltpu
from jax.sharding import PartitionSpec as P

CLASSES = 3
SUB = 4
DIFFUSE_HORIZ = 0.2
DIFFUSE_VERT = 0.1
CONDENSE_RATE = 3.0
LINEAR_DRAG = 0.1
MOIST_BUOYANCY = 0.6
HIGHEST = lax.Precision.HIGHEST
F32 = jnp.float32
LANES = 128
ROWS = 8
PHASES = 4
MIB = 1 << 20


def in_hbm(x):
    return pltpu.with_memory_space_constraint(x, pltpu.HBM)


def iota(shape, axis):
    return lax.broadcasted_iota(jnp.int32, shape, axis)


def dot_t(lhs, rhs):
    return lax.dot_general(lhs, rhs, (((0,), (0,)), ((), ())), precision=HIGHEST, preferred_element_type=F32)


def dot(lhs, rhs):
    return jnp.dot(lhs, rhs, precision=HIGHEST, preferred_element_type=F32)


def all_rows(x):
    x = x + pltpu.roll(x, 4, 0)
    x = x + pltpu.roll(x, 2, 0)
    return x + pltpu.roll(x, 1, 0)


def lanes_of(levels):
    base = 2 * levels
    return base, base + 1, base + 2, base + 3


def pack_kernel(capacity, workers, target_hbm, cost_hbm, forcing_hbm, level_hbm, rows, target, cost, forcing, level_map, counts, spread, sems):
    pairs = ((target_hbm, target), (cost_hbm, cost), (forcing_hbm, forcing), (level_hbm, level_map))
    copies = [pltpu.make_async_copy(source, place, sems.at[i]) for i, (source, place) in enumerate(pairs)]
    for copy in copies:
        copy.start()
    for copy in copies:
        copy.wait()
    levels, gcm = level_map.shape
    columns = forcing.shape[0]
    lane_class, lane_slot, lane_column, lane_owner = lanes_of(levels)
    me = lax.axis_index("crm")
    for worker in range(workers):
        counts[worker] = 0
    sub = iota((columns, LANES), 0)
    lane = iota((columns, LANES), 1)
    classes = jnp.zeros((columns, LANES), F32)
    slots = jnp.zeros((columns, LANES), F32)
    for column in range(columns):
        worker = target[column]
        rank = counts[worker]
        counts[worker] = rank + 1
        slot = (worker * workers + me) * capacity + rank
        classes = jnp.where(sub == column, cost[column].astype(F32), classes)
        slots = jnp.where(sub == column, slot.astype(F32), slots)
    spread[...] = jnp.zeros(spread.shape, F32)
    mapped = jnp.zeros((columns, LANES), F32)
    for variable in range(2):
        spread[variable, variable * levels : (variable + 1) * levels, :] = level_map[...]
        mapped = mapped + lax.dot_general(
            forcing[:, variable, :],
            spread[variable],
            (((1,), (1,)), ((), ())),
            precision=HIGHEST,
            preferred_element_type=F32,
        )
    meta = jnp.where(lane == lane_class, classes, 0.0)
    meta = jnp.where(lane == lane_slot, slots, meta)
    meta = jnp.where(lane == lane_column, (sub + 1).astype(F32), meta)
    meta = jnp.where(lane == lane_owner, me.astype(F32), meta)
    rows[...] = jnp.where(lane < lane_class, mapped, meta)


def pack(target, cost, forcing, level_map, workers, capacity):
    columns = forcing.shape[0]
    return pl.pallas_call(
        functools.partial(pack_kernel, capacity, workers),
        out_shape=jax.ShapeDtypeStruct((columns, LANES), F32),
        in_specs=[pl.BlockSpec(memory_space=pl.ANY)] * 4,
        out_specs=pl.BlockSpec(memory_space=pltpu.VMEM),
        scratch_shapes=[
            pltpu.SMEM(target.shape, jnp.int32),
            pltpu.SMEM(cost.shape, jnp.int32),
            pltpu.VMEM(forcing.shape, F32),
            pltpu.VMEM(level_map.shape, F32),
            pltpu.SMEM((workers,), jnp.int32),
            pltpu.VMEM((2, LANES, forcing.shape[2]), F32),
            pltpu.SemaphoreType.DMA((4,)),
        ],
        compiler_params=pltpu.CompilerParams(vmem_limit_bytes=8 * MIB),
        name="pack_forcing",
    )(*(in_hbm(x) for x in (target, cost, forcing, level_map)))


def model_kernel(workers, slots, levels, width, *refs):
    row_refs = refs[:workers]
    x_hbm, fin, xs, t_ref, meta_v, nat, s1, saved, coef, rows_s, meta_s, sem_meta, sem_in = refs[workers:]
    groups = xs.shape[1] // ROWS
    padded = groups * ROWS
    capacity = slots // workers
    tiles = levels * width // LANES
    residues = width // ROWS
    lane_class, lane_slot, lane_column, lane_owner = lanes_of(levels)
    me = lax.axis_index("crm")

    rows = jnp.concatenate([ref[...] for ref in row_refs], axis=0)
    lane_c = iota(rows.shape, 1)
    local = rows[:, lane_slot : lane_slot + 1] - (me * slots).astype(F32)
    member = (local == lane_c.astype(F32)) & (lane_c < slots)
    class_row = jnp.sum(jnp.where(member, rows[:, lane_class : lane_class + 1], 0.0), axis=0, keepdims=True)
    sub_p = iota((padded, LANES), 0)
    lane_p = iota((padded, LANES), 1)
    key_row = class_row * LANES + (LANES - 1 - iota((1, LANES), 1)).astype(F32)
    key_col = jnp.sum(jnp.where(sub_p == lane_p, key_row, 0.0), axis=1, keepdims=True)
    class_col = jnp.sum(jnp.where(sub_p == lane_p, class_row, 0.0), axis=1, keepdims=True)
    ahead_row = ((key_col > key_row) & (sub_p < slots)).astype(F32)
    place_row = jnp.sum(ahead_row, axis=0, keepdims=True)
    ahead_col = ((key_row > key_col) & (lane_p < slots)).astype(F32)
    place_col = jnp.sum(ahead_col, axis=1, keepdims=True)
    here = (place_col == lane_p.astype(F32)) & (sub_p < slots)
    order = jnp.sum(jnp.where(here, sub_p.astype(F32), 0.0), axis=0, keepdims=True)
    class_sorted = jnp.sum(jnp.where(here, class_col, 0.0), axis=0, keepdims=True)
    sub_m = iota((ROWS, LANES), 0)
    lane_m = iota((ROWS, LANES), 1)
    owner_row = jnp.floor((order + 0.5) * (1.0 / capacity))
    rank_row = order - owner_row * capacity
    away_row = owner_row.astype(jnp.int32) ^ me
    table = jnp.where(sub_m == 0, order, jnp.where(sub_m == 1, class_sorted, rank_row)).astype(jnp.int32)
    table = jnp.where(sub_m == 2, away_row, table)
    meta_v[...] = jnp.where(sub_m == 4, place_row.astype(jnp.int32), table)
    fetch = pltpu.make_async_copy(meta_v, meta_s, sem_meta)
    fetch.start()
    fetch.wait()

    def load(index, carry):
        slot = meta_s[0, index]
        pltpu.make_async_copy(x_hbm.at[:, pl.ds(slot, 1), :], xs.at[:, pl.ds(index, 1), :], sem_in.at[index]).start()
        return carry

    lax.fori_loop(0, padded, load, 0, unroll=4)
    place_of = jnp.sum(jnp.where(member, place_row + 1.0, 0.0), axis=1, keepdims=True) - 1.0
    rows_s[...] = dot_t((place_of == lane_c.astype(F32)).astype(F32), rows)[:padded]

    model_of = lax.rem(lane_m, ROWS)
    step_of = lane_m // ROWS
    own = model_of == sub_m

    def coef_index(name, phase=0):
        names = ("a", "bx", "c0", "c1", "aw", "ac")
        return names.index(name) if name in names else len(names) + ("fh", "fq", "fs").index(name) * PHASES + phase

    def at(field, phase, residue):
        return (field * PHASES + phase) * residues + residue

    def substep(src, dst, means, last):
        next_means = []

        def self_at(field, phase, residue):
            return src[at(field, phase, residue)]

        def above(field, phase, residue):
            if phase < PHASES - 1:
                return src[at(field, phase + 1, residue)]
            return pltpu.roll(src[at(field, 0, residue)], LANES - ROWS, 1)

        def below(field, phase, residue):
            if phase > 0:
                return src[at(field, phase - 1, residue)]
            return pltpu.roll(src[at(field, PHASES - 1, residue)], ROWS, 1)

        a, bx, aw, ac = (coef[coef_index(name)] for name in ("a", "bx", "aw", "ac"))
        for phase in range(PHASES):
            c1 = coef[coef_index("c0" if phase < 2 else "c1")]
            fh, fq, fs = (coef[coef_index(name, phase)] for name in ("fh", "fq", "fs"))
            def around(field, residue):
                if residue > 0:
                    left = self_at(field, phase, residue - 1)
                else:
                    left = pltpu.roll(self_at(field, phase, residues - 1), 1, 0)
                if residue < residues - 1:
                    return left + self_at(field, phase, residue + 1)
                return left + pltpu.roll(self_at(field, phase, 0), ROWS - 1, 0)

            pushed = []
            for residue in range(residues):
                wind = self_at(2, phase, residue)
                new_wind = (aw * wind + (self_at(0, phase, residue) - self_at(1, phase, residue))) + bx * around(2, residue)
                new_wind = new_wind + c1 * (above(2, phase, residue) + below(2, phase, residue))
                if not last:
                    dst[at(2, phase, residue)] = new_wind
                pushed.append(new_wind)
            total = pushed
            while len(total) > 1:
                total = [sum(total[i : i + 2]) for i in range(0, len(total), 2)]
            mean = all_rows(total[0]) * (1.0 / width)
            next_means.append(mean)
            if last:
                for residue in range(residues):
                    dst[at(2, phase, residue)] = pushed[residue] - mean
            up_base = c1 if means is None else c1 + means[phase]
            down_base = c1 if means is None else c1 - means[phase]
            for residue in range(residues):
                heat, moist, wind = (self_at(field, phase, residue) for field in range(3))
                up_coef = up_base - wind
                down_coef = down_base + wind
                new_heat = (a * heat + fh) + bx * around(0, residue)
                dst[at(0, phase, residue)] = new_heat + (
                    up_coef * above(0, phase, residue) + down_coef * below(0, phase, residue)
                )
                new_moist = jnp.minimum(a * moist + fq, ac * moist + fs) + bx * around(1, residue)
                dst[at(1, phase, residue)] = new_moist + (
                    up_coef * above(1, phase, residue) + down_coef * below(1, phase, residue)
                )
        return next_means

    def run_group(group, carry):
        base = pl.multiple_of(group * ROWS, ROWS)
        units = meta_s[1, base]
        mixed = meta_s[1, base + ROWS - 1] != units

        for member in range(ROWS):
            index = base + member
            pltpu.make_async_copy(x_hbm.at[:, pl.ds(0, 1), :], xs.at[:, pl.ds(index, 1), :], sem_in.at[index]).wait()

        s0 = fin.at[group]

        @pl.when(units > 0)
        def _():
            mine = rows_s[pl.ds(base, ROWS), :]
            class_m = mine[:, lane_class : lane_class + 1]
            class_l = all_rows(jnp.where(own, class_m, 0.0))
            steps = jnp.maximum(class_l * SUB, 1.0)
            dt = 1.0 / steps
            scale = 0.5 * dt * dt
            moist_weight = 1.0 - MOIST_BUOYANCY
            diffuse = 1.0 - 2.0 * (DIFFUSE_HORIZ + DIFFUSE_VERT) * dt
            coef[coef_index("a")] = diffuse
            coef[coef_index("bx")] = DIFFUSE_HORIZ * dt
            inside = [(PHASES * step_of + phase) < levels for phase in range(PHASES)]
            coef[coef_index("c0")] = jnp.where(inside[1], DIFFUSE_VERT * dt, 0.0)
            coef[coef_index("c1")] = jnp.where(inside[3], DIFFUSE_VERT * dt, 0.0)
            coef[coef_index("aw")] = diffuse - LINEAR_DRAG * dt
            coef[coef_index("ac")] = diffuse - CONDENSE_RATE * dt
            for phase in range(PHASES):
                level = PHASES * step_of + phase
                pick = jnp.minimum(level, levels - 1)
                keep = own & inside[phase]
                force = [
                    all_rows(jnp.where(keep, jnp.take_along_axis(mine, pick + variable * levels, axis=1), 0.0))
                    for variable in range(2)
                ]
                saturated = jnp.where(inside[phase], 1.0 - 2.0 * (level.astype(F32) + 0.5) / levels, 0.0)
                fq = (moist_weight * scale * dt) * force[1]
                coef[coef_index("fh", phase)] = (scale * dt) * (force[0] + force[1])
                coef[coef_index("fq", phase)] = fq
                coef[coef_index("fs", phase)] = fq + (CONDENSE_RATE * moist_weight) * dt * scale * saturated

            zero = jnp.zeros((ROWS, LANES), F32)
            for field in range(3):
                for half in range(2):
                    parts = []
                    for step in range(LANES // ROWS):
                        tile = 2 * step + half
                        parts.append(xs[field, pl.ds(base, ROWS), tile * LANES : (tile + 1) * LANES] if tile < tiles else zero)
                    start = (field * PHASES + 2 * half) * width
                    nat[start : start + LANES, :] = jnp.concatenate(parts, axis=0).T

            def natural(field, phase, residue):
                return pl.ds((field * PHASES + phase) * width + residue, ROWS, stride=residues)

            moist_scale = moist_weight * scale
            wind_scale = 0.5 * dt
            before = []
            for phase in range(PHASES):
                sums = [jnp.zeros((ROWS, LANES), F32)] * 2
                for residue in range(residues):
                    theta, moist, wind = (nat[natural(field, phase, residue), :] for field in range(3))
                    scaled = (scale * (theta + moist), moist_scale * moist, wind_scale * wind)
                    for field in range(3):
                        s0[at(field, phase, residue)] = scaled[field]
                    sums = [sums[variable] + scaled[variable] for variable in range(2)]
                before.append(sums)

            def unit(index, inner):
                means = None
                for step in range(SUB):
                    means = substep(*((s0, s1) if step % 2 == 0 else (s1, s0)), means, step == SUB - 1)

                done = class_l == (index + 1).astype(F32)

                def keep(chunk, kept):
                    for residue in range(residues):
                        entry = chunk * residues + residue
                        saved[entry] = jnp.where(done, s0[entry], saved[entry])
                    return kept

                lax.fori_loop(0, jnp.where(mixed & (index + 1 < units), 3 * PHASES, 0), keep, 0)
                return inner

            lax.fori_loop(0, units, unit, 0)

            last = class_l == units.astype(F32)

            def restore(chunk, kept):
                for residue in range(residues):
                    entry = chunk * residues + residue
                    s0[entry] = jnp.where(last, s0[entry], saved[entry])
                return kept

            lax.fori_loop(0, jnp.where(mixed, 3 * PHASES, 0), restore, 0)
            heat_share = (2.0 / width) * steps * steps
            moist_share = heat_share * (1.0 / moist_weight)
            change = []
            for phase in range(PHASES):
                sums = [-value for value in before[phase]]
                for residue in range(residues):
                    sums = [sums[variable] + s0[at(variable, phase, residue)] for variable in range(2)]
                moist = moist_share * all_rows(sums[1])
                change.append((heat_share * all_rows(sums[0]) - moist, moist))

            active = class_m > 0.0
            second = lane_m >= levels
            level = jnp.where(second, lane_m - levels, lane_m)
            pick = jnp.minimum(level // PHASES * ROWS + sub_m, LANES - 1)
            which = lax.rem(level, PHASES)
            tendency = jnp.zeros((ROWS, LANES), F32)
            for phase in range(PHASES):
                found = [jnp.take_along_axis(change[phase][variable], pick, axis=1) for variable in range(2)]
                tendency = jnp.where(which == phase, jnp.where(second, found[1], found[0]), tendency)
            t_ref[pl.ds(base, ROWS), :] = jnp.where((lane_m < lane_class) & active, tendency, jnp.where(lane_m < lane_class, 0.0, mine))

        @pl.when(units <= 0)
        def _():
            t_ref[pl.ds(base, ROWS), :] = jnp.zeros((ROWS, LANES), F32)

        return carry

    lax.fori_loop(0, groups, run_group, 0)


def turned(fin, nat, group, field, width):
    residues = width // ROWS
    tiles = {}
    for half in range(2):
        for pair in range(2):
            phase = 2 * half + pair
            for residue in range(residues):
                spot = pl.ds(phase * width + residue, ROWS, stride=residues)
                nat[spot, :] = fin[group, (field * PHASES + phase) * residues + residue]
        back = nat[2 * half * width : 2 * half * width + LANES, :].T
        for step in range(LANES // ROWS):
            tiles[2 * step + half] = back[step * ROWS : (step + 1) * ROWS]
    return tiles


def weights_of(t_ref, base, lane_class):
    class_m = t_ref[pl.ds(base, ROWS), lane_class : lane_class + 1]
    steps = jnp.broadcast_to(jnp.maximum(class_m * SUB, 1.0), (ROWS, LANES))
    heat = 2.0 * steps * steps
    return class_m > 0.0, heat, heat * (1.0 / (1.0 - MOIST_BUOYANCY)), 2.0 * steps


def cloud_kernel(levels, width, meta, fin, t_ref, water, cl, nat):
    groups = fin.shape[0]
    tiles = levels * width // LANES
    block = -(-tiles // ROWS) * ROWS
    lane_m = iota((ROWS, LANES), 1)
    lane_class = lanes_of(levels)[0]

    def run_group(group, carry):
        base = pl.multiple_of(group * ROWS, ROWS)

        @pl.when(meta[1, base] > 0)
        def _():
            _, _, moist_weight, _ = weights_of(t_ref, base, lane_class)
            parts = turned(fin, nat, group, 1, width)
            for tile in range(tiles):
                value = moist_weight * parts[tile]
                level = (LANES // width) * tile + lane_m // width
                saturated = 1.0 - 2.0 * (level.astype(F32) + 0.5) / levels
                water[pl.ds(base, ROWS), tile * LANES : (tile + 1) * LANES] = value
                cl[pl.ds(base * block + tile, ROWS, stride=block), :] = jnp.maximum(value - saturated, 0.0)

        return carry

    lax.fori_loop(0, groups, run_group, 0)


def send_kernel(workers, capacity, meta, cl, *outs):
    block = outs[0].shape[0] // capacity
    me = lax.axis_index("crm")
    for distance in range(workers):
        first = (me ^ distance) * capacity
        for rank in range(capacity):
            source = pl.multiple_of(meta[4, first + rank] * block, ROWS)
            outs[distance][rank * block : (rank + 1) * block, :] = cl[pl.ds(source, block), :]


def state_kernel(slots, levels, width, meta, fin, t_ref, water, xs, y_hbm, ys, nat, sems):
    groups = fin.shape[0]
    tiles = levels * width // LANES
    lane_class = lanes_of(levels)[0]

    def run_group(group, carry):
        base = pl.multiple_of(group * ROWS, ROWS)

        @pl.when(meta[1, base] > 0)
        def _():
            active, heat_weight, _, wind_weight = weights_of(t_ref, base, lane_class)
            heats = turned(fin, nat, group, 0, width)
            winds = turned(fin, nat, group, 2, width)
            for tile in range(tiles):
                lanes = slice(tile * LANES, (tile + 1) * LANES)
                moist = water[pl.ds(base, ROWS), lanes]
                values = (heat_weight * heats[tile] - moist, moist, wind_weight * winds[tile])
                for field in range(3):
                    spot = (field, pl.ds(base, ROWS), lanes)
                    ys[spot] = jnp.where(active, values[field], xs[spot])

        def store(source, member, inner):
            index = base + member

            @pl.when(index < slots)
            def _():
                pltpu.make_async_copy(
                    source.at[:, pl.ds(index, 1), :], y_hbm.at[:, pl.ds(meta[0, index], 1), :], sems.at[index]
                ).start()

            return inner

        @pl.when(meta[1, base] > 0)
        def _():
            lax.fori_loop(0, ROWS, functools.partial(store, ys), 0)

        @pl.when(meta[1, base] <= 0)
        def _():
            lax.fori_loop(0, ROWS, functools.partial(store, xs), 0)

        return carry

    lax.fori_loop(0, groups, run_group, 0)
    for index in range(slots):
        pltpu.make_async_copy(ys.at[:, pl.ds(index, 1), :], y_hbm.at[:, pl.ds(0, 1), :], sems.at[index]).wait()


def small(name, mib=8, moved=1 << 20):
    cost = pl.CostEstimate(flops=0, bytes_accessed=moved, transcendentals=0)
    return dict(compiler_params=pltpu.CompilerParams(vmem_limit_bytes=mib * MIB), name=name, cost_estimate=cost)


def run_models(row_blocks, state, levels):
    workers = len(row_blocks)
    _, slots, cells = state.shape
    width = cells // levels
    groups = -(-slots // ROWS)
    padded = groups * ROWS
    vmem = pl.BlockSpec(memory_space=pltpu.VMEM)
    entries = 3 * PHASES * (width // ROWS)
    return pl.pallas_call(
        functools.partial(model_kernel, workers, slots, levels, width),
        out_shape=[
            jax.ShapeDtypeStruct((groups, entries, ROWS, LANES), F32),
            jax.ShapeDtypeStruct((3, padded, cells), F32),
            jax.ShapeDtypeStruct((padded, LANES), F32),
            jax.ShapeDtypeStruct((ROWS, LANES), jnp.int32),
        ],
        in_specs=[vmem] * workers + [pl.BlockSpec(memory_space=pl.ANY)],
        out_specs=[vmem] * 4,
        scratch_shapes=[
            pltpu.VMEM((3 * PHASES * width, LANES), F32),
            pltpu.VMEM((entries, ROWS, LANES), F32),
            pltpu.VMEM((entries, ROWS, LANES), F32),
            pltpu.VMEM((6 + 3 * PHASES, ROWS, LANES), F32),
            pltpu.VMEM((padded, LANES), F32),
            pltpu.SMEM((ROWS, LANES), jnp.int32),
            pltpu.SemaphoreType.DMA,
            pltpu.SemaphoreType.DMA((padded,)),
        ],
        **small("cloud_models", 12, 40 << 20),
    )(*row_blocks, state)


def condensate(cells, levels, meta, fin, tendency):
    padded = fin.shape[0] * ROWS
    width = cells // levels
    vmem = pl.BlockSpec(memory_space=pltpu.VMEM)
    block = -(-(cells // LANES) // ROWS) * ROWS
    return pl.pallas_call(
        functools.partial(cloud_kernel, levels, width),
        out_shape=[jax.ShapeDtypeStruct((padded, cells), F32), jax.ShapeDtypeStruct((padded * block, LANES), F32)],
        in_specs=[pl.BlockSpec(memory_space=pltpu.SMEM), vmem, vmem],
        out_specs=[vmem] * 2,
        scratch_shapes=[pltpu.VMEM((PHASES * width, LANES), F32)],
        **small("condensate", moved=8 << 20),
    )(meta, fin, tendency)


def send_blocks(workers, slots, meta, blocks):
    capacity = slots // workers
    block = blocks.shape[0] // (-(-slots // ROWS) * ROWS)
    vmem = pl.BlockSpec(memory_space=pltpu.VMEM)
    return pl.pallas_call(
        functools.partial(send_kernel, workers, capacity),
        out_shape=[jax.ShapeDtypeStruct((capacity * block, LANES), F32)] * workers,
        in_specs=[pl.BlockSpec(memory_space=pltpu.SMEM), vmem],
        out_specs=[vmem] * workers,
        **small("send_blocks"),
    )(meta, blocks)


def state_rows(slots, levels, meta, fin, tendency, water, start):
    width = fin.shape[1] // (3 * PHASES) * ROWS
    fields, padded, cells = start.shape
    vmem = pl.BlockSpec(memory_space=pltpu.VMEM)
    return pl.pallas_call(
        functools.partial(state_kernel, slots, levels, width),
        out_shape=jax.ShapeDtypeStruct((fields, slots, cells), F32),
        in_specs=[pl.BlockSpec(memory_space=pltpu.SMEM)] + [vmem] * 4,
        out_specs=pl.BlockSpec(memory_space=pl.ANY),
        scratch_shapes=[
            pltpu.VMEM((fields, padded, cells), F32),
            pltpu.VMEM((PHASES * width, LANES), F32),
            pltpu.SemaphoreType.DMA((slots,)),
        ],
        **small("state_rows", moved=12 << 20),
    )(meta, fin, tendency, water, start)


def edge_kernel(levels, columns, workers, *refs):
    t_refs, out = refs[:workers], refs[workers]
    _, _, lane_column, lane_owner = lanes_of(levels)
    me = lax.axis_index("crm")
    wanted = jnp.where(me == 0, workers - 1, 0).astype(F32)
    rows = jnp.concatenate([ref[...] for ref in t_refs], axis=0)
    lane = iota(rows.shape, 1).astype(F32)
    owner = rows[:, lane_owner : lane_owner + 1]
    column = rows[:, lane_column : lane_column + 1]
    select = ((owner == wanted) & (column == lane + 1.0)).astype(F32)
    out[...] = dot_t(select, rows)[:columns]


def share_rows(index, weight):
    rows = weight[...]
    total = jnp.sum(rows, axis=0, keepdims=True)
    return index[...].astype(F32), rows / total


def inner_kernel(levels, columns, workers, *refs):
    t_refs = refs[:workers]
    index, weight, level_map, inner, maps = refs[workers:]
    _, _, lane_column, lane_owner = lanes_of(levels)
    me = lax.axis_index("crm")
    rows = jnp.concatenate([ref[...] for ref in t_refs], axis=0)
    owner = rows[:, lane_owner : lane_owner + 1]
    column = rows[:, lane_column : lane_column + 1]
    block = owner - me.astype(F32) + 1.0
    named = (column > 0.0) & (block >= 0.0) & (block <= 2.0)
    ident = jnp.where(named, block * columns + column - 1.0, -1.0)
    wanted, share = share_rows(index, weight)
    mix = jnp.zeros((rows.shape[0], columns), F32)
    for source in range(index.shape[0]):
        mix = mix + jnp.where(ident == wanted[source : source + 1], share[source : source + 1], 0.0)
    inner[...] = dot_t(mix, rows)
    spread_row = iota((levels, LANES), 0)
    spread_lane = iota((levels, LANES), 1)
    for variable in range(2):
        place = (spread_lane == spread_row + variable * levels).astype(F32)
        maps[variable] = dot_t(place, level_map[...])


def physics_kernel(columns, workers, inner, maps, edge, index, weight, out):
    me = lax.axis_index("crm")
    edge_sub = iota((columns, 1), 0)
    edge_block = jnp.where(me == 0, 0, jnp.where(me == workers - 1, 2, -3))
    ident = (edge_block * columns + edge_sub).astype(F32)
    wanted, share = share_rows(index, weight)
    mix = jnp.zeros((columns, columns), F32)
    for source in range(index.shape[0]):
        mix = mix + jnp.where(ident == wanted[source : source + 1], share[source : source + 1], 0.0)
    mixed = inner[...] + dot_t(mix, jnp.where(edge_block >= 0, edge[...], 0.0))
    for variable in range(2):
        out[:, variable, :] = dot(mixed, maps[variable])


def gather_kernel(columns, capacity, workers, *refs):
    target = refs[0]
    received = refs[1 : workers + 1]
    out, counts, column_of, places = refs[workers + 1 :]
    tiles = out.shape[1] // LANES
    block = -(-tiles // ROWS) * ROWS
    me = lax.axis_index("crm")
    for worker in range(workers):
        counts[worker] = 0
    for entry in range(workers * capacity):
        column_of[entry] = columns
    for column in range(columns):
        worker = target[column]
        rank = counts[worker]
        counts[worker] = rank + 1
        column_of[(worker ^ me) * capacity + rank] = column
    for distance in range(workers):
        for rank in range(capacity):
            place = pl.multiple_of(column_of[distance * capacity + rank] * block, ROWS)
            places[pl.ds(place, block), :] = received[distance][rank * block : (rank + 1) * block, :]
    for base in range(0, columns, ROWS):
        count = min(ROWS, columns - base)
        for tile in range(tiles):
            rows = places[pl.ds(base * block + tile, count, stride=block), :]
            out[base : base + count, tile * LANES : (tile + 1) * LANES] = rows


def exchange(blocks, axis):
    size = lax.axis_size(axis)
    out = [blocks[0]]
    for distance in range(1, size):
        out.append(lax.ppermute(blocks[distance], axis, [(i, i ^ distance) for i in range(size)]))
    return out


def body(crm_state, forcing, target, cost_class, level_map, remap_index, remap_weight):
    workers = lax.axis_size("crm")
    groups = lax.axis_size("grp")
    columns = forcing.shape[0]
    slots, _, cells = crm_state.shape
    capacity = slots // workers
    levels, gcm = level_map.shape
    vmem = pl.BlockSpec(memory_space=pltpu.VMEM)

    rows = pack(target, cost_class, forcing, level_map, workers, capacity)
    row_blocks = exchange([rows] * workers, "crm")
    fin, start, tendency, meta = run_models(row_blocks, in_hbm(crm_state.transpose(1, 0, 2)), levels)
    tendencies = exchange([tendency] * workers, "crm")
    water, blocks = condensate(cells, levels, meta, fin, tendency)
    clouds = send_blocks(workers, slots, meta, blocks)
    tendencies, clouds = lax.optimization_barrier((tendencies, clouds))
    clouds = exchange(clouds, "crm")

    edge = pl.pallas_call(
        functools.partial(edge_kernel, levels, columns, workers),
        out_shape=jax.ShapeDtypeStruct((columns, LANES), F32),
        in_specs=[vmem] * workers,
        out_specs=vmem,
        **small("edge_columns"),
    )(*tendencies)
    pairs = []
    for group in range(groups):
        after = (group + 1) % groups
        pairs.append((group * workers, after * workers))
        pairs.append((after * workers + workers - 1, group * workers + workers - 1))
    edge, meta, tendencies = lax.optimization_barrier((edge, meta, tendencies))
    edge = lax.ppermute(edge, ("grp", "crm"), pairs)
    inner, maps = pl.pallas_call(
        functools.partial(inner_kernel, levels, columns, workers),
        out_shape=[jax.ShapeDtypeStruct((columns, LANES), F32), jax.ShapeDtypeStruct((2, LANES, gcm), F32)],
        in_specs=[vmem] * (workers + 3),
        out_specs=[vmem] * 2,
        **small("inner_blocks"),
    )(*tendencies, remap_index.T, remap_weight.T, level_map)
    state = state_rows(slots, levels, meta, fin, tendency, water, start)
    block = clouds[0].shape[0] // capacity
    cloud_water = pl.pallas_call(
        functools.partial(gather_kernel, columns, capacity, workers),
        out_shape=jax.ShapeDtypeStruct((columns, cells), F32),
        in_specs=[pl.BlockSpec(memory_space=pltpu.SMEM)] + [vmem] * workers,
        out_specs=vmem,
        scratch_shapes=[
            pltpu.SMEM((workers,), jnp.int32),
            pltpu.SMEM((slots,), jnp.int32),
            pltpu.VMEM(((columns + 1) * block, LANES), F32),
        ],
        **small("cloud_rows"),
    )(target, *clouds)
    inner, maps, cloud_water = lax.optimization_barrier((inner, maps, cloud_water))
    physics = pl.pallas_call(
        functools.partial(physics_kernel, columns, workers),
        out_shape=jax.ShapeDtypeStruct((columns, 2, gcm), F32),
        in_specs=[vmem] * 5,
        out_specs=vmem,
        **small("physics_cells"),
    )(inner, maps, edge, remap_index.T, remap_weight.T)
    return state.transpose(1, 0, 2), cloud_water, physics


def solution(mesh):
    wide = P(("grp", "crm"), None, None)
    flat = P(("grp", "crm"), None)
    line = P(("grp", "crm"))
    in_specs = (wide, wide, line, line, P(), flat, flat)
    out_specs = (wide, flat, wide)
    return jax.shard_map(body, mesh=mesh, in_specs=in_specs, out_specs=out_specs, check_vma=False)
```

```python
import functools

import jax
import jax.numpy as jnp
from jax import lax
from jax.experimental import pallas as pl
from jax.experimental.pallas import tpu as pltpu
from jax.sharding import PartitionSpec as P

CLASSES = 3
SUB = 4
DIFFUSE_HORIZ = 0.2
DIFFUSE_VERT = 0.1
CONDENSE_RATE = 3.0
LINEAR_DRAG = 0.1
MOIST_BUOYANCY = 0.6
HIGHEST = lax.Precision.HIGHEST
F32 = jnp.float32
LANES = 128
ROWS = 8
PHASES = 4
MIB = 1 << 20


def in_hbm(x):
    return pltpu.with_memory_space_constraint(x, pltpu.HBM)


def iota(shape, axis):
    return lax.broadcasted_iota(jnp.int32, shape, axis)


def dot_t(lhs, rhs):
    return lax.dot_general(lhs, rhs, (((0,), (0,)), ((), ())), precision=HIGHEST, preferred_element_type=F32)


def dot(lhs, rhs):
    return jnp.dot(lhs, rhs, precision=HIGHEST, preferred_element_type=F32)


def all_rows(x):
    x = x + pltpu.roll(x, 4, 0)
    x = x + pltpu.roll(x, 2, 0)
    return x + pltpu.roll(x, 1, 0)


def lanes_of(levels):
    base = 2 * levels
    return base, base + 1, base + 2, base + 3


def pack_kernel(capacity, workers, target_hbm, cost_hbm, forcing_hbm, level_hbm, rows, target, cost, forcing, level_map, counts, spread, sems):
    pairs = ((target_hbm, target), (cost_hbm, cost), (forcing_hbm, forcing), (level_hbm, level_map))
    copies = [pltpu.make_async_copy(source, place, sems.at[i]) for i, (source, place) in enumerate(pairs)]
    for copy in copies:
        copy.start()
    for copy in copies:
        copy.wait()
    levels, gcm = level_map.shape
    columns = forcing.shape[0]
    lane_class, lane_slot, lane_column, lane_owner = lanes_of(levels)
    me = lax.axis_index("crm")
    for worker in range(workers):
        counts[worker] = 0
    sub = iota((columns, LANES), 0)
    lane = iota((columns, LANES), 1)
    classes = jnp.zeros((columns, LANES), F32)
    slots = jnp.zeros((columns, LANES), F32)
    for column in range(columns):
        worker = target[column]
        rank = counts[worker]
        counts[worker] = rank + 1
        slot = (worker * workers + me) * capacity + rank
        classes = jnp.where(sub == column, cost[column].astype(F32), classes)
        slots = jnp.where(sub == column, slot.astype(F32), slots)
    spread[...] = jnp.zeros(spread.shape, F32)
    mapped = jnp.zeros((columns, LANES), F32)
    for variable in range(2):
        spread[variable, variable * levels : (variable + 1) * levels, :] = level_map[...]
        mapped = mapped + lax.dot_general(
            forcing[:, variable, :],
            spread[variable],
            (((1,), (1,)), ((), ())),
            precision=HIGHEST,
            preferred_element_type=F32,
        )
    meta = jnp.where(lane == lane_class, classes, 0.0)
    meta = jnp.where(lane == lane_slot, slots, meta)
    meta = jnp.where(lane == lane_column, (sub + 1).astype(F32), meta)
    meta = jnp.where(lane == lane_owner, me.astype(F32), meta)
    rows[...] = jnp.where(lane < lane_class, mapped, meta)


def pack(target, cost, forcing, level_map, workers, capacity):
    columns = forcing.shape[0]
    return pl.pallas_call(
        functools.partial(pack_kernel, capacity, workers),
        out_shape=jax.ShapeDtypeStruct((columns, LANES), F32),
        in_specs=[pl.BlockSpec(memory_space=pl.ANY)] * 4,
        out_specs=pl.BlockSpec(memory_space=pltpu.VMEM),
        scratch_shapes=[
            pltpu.SMEM(target.shape, jnp.int32),
            pltpu.SMEM(cost.shape, jnp.int32),
            pltpu.VMEM(forcing.shape, F32),
            pltpu.VMEM(level_map.shape, F32),
            pltpu.SMEM((workers,), jnp.int32),
            pltpu.VMEM((2, LANES, forcing.shape[2]), F32),
            pltpu.SemaphoreType.DMA((4,)),
        ],
        compiler_params=pltpu.CompilerParams(vmem_limit_bytes=8 * MIB),
        name="pack_forcing",
    )(*(in_hbm(x) for x in (target, cost, forcing, level_map)))


def model_kernel(workers, slots, levels, width, *refs):
    row_refs = refs[:workers]
    x_hbm, fin, xs, t_ref, meta_v, nat, s1, saved, coef, rows_s, meta_s, sem_meta, sem_in = refs[workers:]
    groups = xs.shape[1] // ROWS
    padded = groups * ROWS
    capacity = slots // workers
    tiles = levels * width // LANES
    residues = width // ROWS
    lane_class, lane_slot, lane_column, lane_owner = lanes_of(levels)
    me = lax.axis_index("crm")

    rows = jnp.concatenate([ref[...] for ref in row_refs], axis=0)
    lane_c = iota(rows.shape, 1)
    local = rows[:, lane_slot : lane_slot + 1] - (me * slots).astype(F32)
    member = (local == lane_c.astype(F32)) & (lane_c < slots)
    class_row = jnp.sum(jnp.where(member, rows[:, lane_class : lane_class + 1], 0.0), axis=0, keepdims=True)
    sub_p = iota((padded, LANES), 0)
    lane_p = iota((padded, LANES), 1)
    key_row = class_row * LANES + (LANES - 1 - iota((1, LANES), 1)).astype(F32)
    key_col = jnp.sum(jnp.where(sub_p == lane_p, key_row, 0.0), axis=1, keepdims=True)
    class_col = jnp.sum(jnp.where(sub_p == lane_p, class_row, 0.0), axis=1, keepdims=True)
    ahead_row = ((key_col > key_row) & (sub_p < slots)).astype(F32)
    place_row = jnp.sum(ahead_row, axis=0, keepdims=True)
    ahead_col = ((key_row > key_col) & (lane_p < slots)).astype(F32)
    place_col = jnp.sum(ahead_col, axis=1, keepdims=True)
    here = (place_col == lane_p.astype(F32)) & (sub_p < slots)
    order = jnp.sum(jnp.where(here, sub_p.astype(F32), 0.0), axis=0, keepdims=True)
    class_sorted = jnp.sum(jnp.where(here, class_col, 0.0), axis=0, keepdims=True)
    sub_m = iota((ROWS, LANES), 0)
    lane_m = iota((ROWS, LANES), 1)
    owner_row = jnp.floor((order + 0.5) * (1.0 / capacity))
    rank_row = order - owner_row * capacity
    away_row = owner_row.astype(jnp.int32) ^ me
    table = jnp.where(sub_m == 0, order, jnp.where(sub_m == 1, class_sorted, rank_row)).astype(jnp.int32)
    table = jnp.where(sub_m == 2, away_row, table)
    meta_v[...] = jnp.where(sub_m == 4, place_row.astype(jnp.int32), table)
    fetch = pltpu.make_async_copy(meta_v, meta_s, sem_meta)
    fetch.start()
    fetch.wait()

    def load(index, carry):
        slot = meta_s[0, index]
        pltpu.make_async_copy(x_hbm.at[:, pl.ds(slot, 1), :], xs.at[:, pl.ds(index, 1), :], sem_in.at[index]).start()
        return carry

    lax.fori_loop(0, padded, load, 0, unroll=4)
    place_of = jnp.sum(jnp.where(member, place_row + 1.0, 0.0), axis=1, keepdims=True) - 1.0
    rows_s[...] = dot_t((place_of == lane_c.astype(F32)).astype(F32), rows)[:padded]

    model_of = lax.rem(lane_m, ROWS)
    step_of = lane_m // ROWS
    own = model_of == sub_m

    def coef_index(name, phase=0):
        names = ("a", "bx", "c0", "c1", "aw", "ac")
        return names.index(name) if name in names else len(names) + ("fh", "fq", "fs").index(name) * PHASES + phase

    def at(field, phase, residue):
        return (field * PHASES + phase) * residues + residue

    def substep(src, dst, means, last):
        next_means = []

        def self_at(field, phase, residue):
            return src[at(field, phase, residue)]

        def above(field, phase, residue):
            if phase < PHASES - 1:
                return src[at(field, phase + 1, residue)]
            return pltpu.roll(src[at(field, 0, residue)], LANES - ROWS, 1)

        def below(field, phase, residue):
            if phase > 0:
                return src[at(field, phase - 1, residue)]
            return pltpu.roll(src[at(field, PHASES - 1, residue)], ROWS, 1)

        a, bx, aw, ac = (coef[coef_index(name)] for name in ("a", "bx", "aw", "ac"))
        for phase in range(PHASES):
            c1 = coef[coef_index("c0" if phase < 2 else "c1")]
            fh, fq, fs = (coef[coef_index(name, phase)] for name in ("fh", "fq", "fs"))
            def around(field, residue):
                if residue > 0:
                    left = self_at(field, phase, residue - 1)
                else:
                    left = pltpu.roll(self_at(field, phase, residues - 1), 1, 0)
                if residue < residues - 1:
                    return left + self_at(field, phase, residue + 1)
                return left + pltpu.roll(self_at(field, phase, 0), ROWS - 1, 0)

            pushed = []
            for residue in range(residues):
                wind = self_at(2, phase, residue)
                new_wind = (aw * wind + (self_at(0, phase, residue) - self_at(1, phase, residue))) + bx * around(2, residue)
                new_wind = new_wind + c1 * (above(2, phase, residue) + below(2, phase, residue))
                if not last:
                    dst[at(2, phase, residue)] = new_wind
                pushed.append(new_wind)
            total = pushed
            while len(total) > 1:
                total = [sum(total[i : i + 2]) for i in range(0, len(total), 2)]
            mean = all_rows(total[0]) * (1.0 / width)
            next_means.append(mean)
            if last:
                for residue in range(residues):
                    dst[at(2, phase, residue)] = pushed[residue] - mean
            up_base = c1 if means is None else c1 + means[phase]
            down_base = c1 if means is None else c1 - means[phase]
            for residue in range(residues):
                heat, moist, wind = (self_at(field, phase, residue) for field in range(3))
                up_coef = up_base - wind
                down_coef = down_base + wind
                new_heat = (a * heat + fh) + bx * around(0, residue)
                dst[at(0, phase, residue)] = new_heat + (
                    up_coef * above(0, phase, residue) + down_coef * below(0, phase, residue)
                )
                new_moist = jnp.minimum(a * moist + fq, ac * moist + fs) + bx * around(1, residue)
                dst[at(1, phase, residue)] = new_moist + (
                    up_coef * above(1, phase, residue) + down_coef * below(1, phase, residue)
                )
        return next_means

    def run_group(group, carry):
        base = pl.multiple_of(group * ROWS, ROWS)
        units = meta_s[1, base]
        mixed = meta_s[1, base + ROWS - 1] != units

        for member in range(ROWS):
            index = base + member
            pltpu.make_async_copy(x_hbm.at[:, pl.ds(0, 1), :], xs.at[:, pl.ds(index, 1), :], sem_in.at[index]).wait()

        s0 = fin.at[group]

        @pl.when(units > 0)
        def _():
            mine = rows_s[pl.ds(base, ROWS), :]
            class_m = mine[:, lane_class : lane_class + 1]
            class_l = all_rows(jnp.where(own, class_m, 0.0))
            steps = jnp.maximum(class_l * SUB, 1.0)
            dt = 1.0 / steps
            scale = 0.5 * dt * dt
            moist_weight = 1.0 - MOIST_BUOYANCY
            diffuse = 1.0 - 2.0 * (DIFFUSE_HORIZ + DIFFUSE_VERT) * dt
            coef[coef_index("a")] = diffuse
            coef[coef_index("bx")] = DIFFUSE_HORIZ * dt
            inside = [(PHASES * step_of + phase) < levels for phase in range(PHASES)]
            coef[coef_index("c0")] = jnp.where(inside[1], DIFFUSE_VERT * dt, 0.0)
            coef[coef_index("c1")] = jnp.where(inside[3], DIFFUSE_VERT * dt, 0.0)
            coef[coef_index("aw")] = diffuse - LINEAR_DRAG * dt
            coef[coef_index("ac")] = diffuse - CONDENSE_RATE * dt
            for phase in range(PHASES):
                level = PHASES * step_of + phase
                pick = jnp.minimum(level, levels - 1)
                keep = own & inside[phase]
                force = [
                    all_rows(jnp.where(keep, jnp.take_along_axis(mine, pick + variable * levels, axis=1), 0.0))
                    for variable in range(2)
                ]
                saturated = jnp.where(inside[phase], 1.0 - 2.0 * (level.astype(F32) + 0.5) / levels, 0.0)
                fq = (moist_weight * scale * dt) * force[1]
                coef[coef_index("fh", phase)] = (scale * dt) * (force[0] + force[1])
                coef[coef_index("fq", phase)] = fq
                coef[coef_index("fs", phase)] = fq + (CONDENSE_RATE * moist_weight) * dt * scale * saturated

            zero = jnp.zeros((ROWS, LANES), F32)
            for field in range(3):
                for half in range(2):
                    parts = []
                    for step in range(LANES // ROWS):
                        tile = 2 * step + half
                        parts.append(xs[field, pl.ds(base, ROWS), tile * LANES : (tile + 1) * LANES] if tile < tiles else zero)
                    start = (field * PHASES + 2 * half) * width
                    nat[start : start + LANES, :] = jnp.concatenate(parts, axis=0).T

            def natural(field, phase, residue):
                return pl.ds((field * PHASES + phase) * width + residue, ROWS, stride=residues)

            moist_scale = moist_weight * scale
            wind_scale = 0.5 * dt
            before = []
            for phase in range(PHASES):
                sums = [jnp.zeros((ROWS, LANES), F32)] * 2
                for residue in range(residues):
                    theta, moist, wind = (nat[natural(field, phase, residue), :] for field in range(3))
                    scaled = (scale * (theta + moist), moist_scale * moist, wind_scale * wind)
                    for field in range(3):
                        s0[at(field, phase, residue)] = scaled[field]
                    sums = [sums[variable] + scaled[variable] for variable in range(2)]
                before.append(sums)

            def unit(index, inner):
                means = None
                for step in range(SUB):
                    means = substep(*((s0, s1) if step % 2 == 0 else (s1, s0)), means, step == SUB - 1)

                done = class_l == (index + 1).astype(F32)

                def keep(chunk, kept):
                    for residue in range(residues):
                        entry = chunk * residues + residue
                        saved[entry] = jnp.where(done, s0[entry], saved[entry])
                    return kept

                lax.fori_loop(0, jnp.where(mixed & (index + 1 < units), 3 * PHASES, 0), keep, 0)
                return inner

            lax.fori_loop(0, units, unit, 0)

            last = class_l == units.astype(F32)

            def restore(chunk, kept):
                for residue in range(residues):
                    entry = chunk * residues + residue
                    s0[entry] = jnp.where(last, s0[entry], saved[entry])
                return kept

            lax.fori_loop(0, jnp.where(mixed, 3 * PHASES, 0), restore, 0)
            heat_share = (2.0 / width) * steps * steps
            moist_share = heat_share * (1.0 / moist_weight)
            change = []
            for phase in range(PHASES):
                sums = [-value for value in before[phase]]
                for residue in range(residues):
                    sums = [sums[variable] + s0[at(variable, phase, residue)] for variable in range(2)]
                moist = moist_share * all_rows(sums[1])
                change.append((heat_share * all_rows(sums[0]) - moist, moist))

            active = class_m > 0.0
            second = lane_m >= levels
            level = jnp.where(second, lane_m - levels, lane_m)
            pick = jnp.minimum(level // PHASES * ROWS + sub_m, LANES - 1)
            which = lax.rem(level, PHASES)
            tendency = jnp.zeros((ROWS, LANES), F32)
            for phase in range(PHASES):
                found = [jnp.take_along_axis(change[phase][variable], pick, axis=1) for variable in range(2)]
                tendency = jnp.where(which == phase, jnp.where(second, found[1], found[0]), tendency)
            t_ref[pl.ds(base, ROWS), :] = jnp.where((lane_m < lane_class) & active, tendency, jnp.where(lane_m < lane_class, 0.0, mine))

        @pl.when(units <= 0)
        def _():
            t_ref[pl.ds(base, ROWS), :] = jnp.zeros((ROWS, LANES), F32)

        return carry

    lax.fori_loop(0, groups, run_group, 0)


def turned(fin, nat, group, field, width):
    residues = width // ROWS
    tiles = {}
    for half in range(2):
        for pair in range(2):
            phase = 2 * half + pair
            for residue in range(residues):
                spot = pl.ds(phase * width + residue, ROWS, stride=residues)
                nat[spot, :] = fin[group, (field * PHASES + phase) * residues + residue]
        back = nat[2 * half * width : 2 * half * width + LANES, :].T
        for step in range(LANES // ROWS):
            tiles[2 * step + half] = back[step * ROWS : (step + 1) * ROWS]
    return tiles


def weights_of(t_ref, base, lane_class):
    class_m = t_ref[pl.ds(base, ROWS), lane_class : lane_class + 1]
    steps = jnp.broadcast_to(jnp.maximum(class_m * SUB, 1.0), (ROWS, LANES))
    heat = 2.0 * steps * steps
    return class_m > 0.0, heat, heat * (1.0 / (1.0 - MOIST_BUOYANCY)), 2.0 * steps


def cloud_kernel(levels, width, workers, capacity, meta, fin, t_ref, water, *refs):
    outs = refs[:workers]
    cl, nat = refs[workers:]
    tiles = levels * width // LANES
    block = outs[0].shape[0] // capacity
    lane_m = iota((ROWS, LANES), 1)
    lane_class = lanes_of(levels)[0]
    me = lax.axis_index("crm")
    for group in range(fin.shape[0]):
        base = group * ROWS
        _, _, moist_weight, _ = weights_of(t_ref, base, lane_class)
        parts = turned(fin, nat.at[group], group, 1, width)
        for tile in range(tiles):
            value = moist_weight * parts[tile]
            level = (LANES // width) * tile + lane_m // width
            saturated = 1.0 - 2.0 * (level.astype(F32) + 0.5) / levels
            water[base : base + ROWS, tile * LANES : (tile + 1) * LANES] = value
            cl[pl.ds(base * block + tile, ROWS, stride=block), :] = jnp.maximum(value - saturated, 0.0)
    for distance in range(workers):
        first = (me ^ distance) * capacity
        for rank in range(capacity):
            source = pl.multiple_of(meta[4, first + rank] * block, ROWS)
            outs[distance][rank * block : (rank + 1) * block, :] = cl[pl.ds(source, block), :]


def state_kernel(slots, levels, width, columns, workers, meta, fin, t_ref, water, xs, *refs):
    inner_refs = refs[: workers + 3]
    y_hbm, inner, maps, ys, nat, sems = refs[workers + 3 :]
    groups = fin.shape[0]
    tiles = levels * width // LANES
    lane_class = lanes_of(levels)[0]
    copies = []
    for group in range(groups):
        base = group * ROWS
        active, heat_weight, _, wind_weight = weights_of(t_ref, base, lane_class)
        heats = turned(fin, nat.at[2 * group], group, 0, width)
        winds = turned(fin, nat.at[2 * group + 1], group, 2, width)
        for tile in range(tiles):
            lanes = slice(tile * LANES, (tile + 1) * LANES)
            moist = water[base : base + ROWS, lanes]
            values = (heat_weight * heats[tile] - moist, moist, wind_weight * winds[tile])
            for field in range(3):
                ys[field, base : base + ROWS, lanes] = jnp.where(active, values[field], xs[field, base : base + ROWS, lanes])
        for index in range(base, min(base + ROWS, slots)):
            copy = pltpu.make_async_copy(
                ys.at[:, pl.ds(index, 1), :], y_hbm.at[:, pl.ds(meta[0, index], 1), :], sems.at[index]
            )
            copy.start()
            copies.append(copy)
    inner_blocks(levels, columns, workers, *inner_refs, inner, maps)
    for copy in copies:
        copy.wait()


def small(name, mib=8, moved=1 << 20):
    cost = pl.CostEstimate(flops=0, bytes_accessed=moved, transcendentals=0)
    return dict(compiler_params=pltpu.CompilerParams(vmem_limit_bytes=mib * MIB), name=name, cost_estimate=cost)


def run_models(row_blocks, state, levels):
    workers = len(row_blocks)
    _, slots, cells = state.shape
    width = cells // levels
    groups = -(-slots // ROWS)
    padded = groups * ROWS
    vmem = pl.BlockSpec(memory_space=pltpu.VMEM)
    entries = 3 * PHASES * (width // ROWS)
    return pl.pallas_call(
        functools.partial(model_kernel, workers, slots, levels, width),
        out_shape=[
            jax.ShapeDtypeStruct((groups, entries, ROWS, LANES), F32),
            jax.ShapeDtypeStruct((3, padded, cells), F32),
            jax.ShapeDtypeStruct((padded, LANES), F32),
            jax.ShapeDtypeStruct((ROWS, LANES), jnp.int32),
        ],
        in_specs=[vmem] * workers + [pl.BlockSpec(memory_space=pl.ANY)],
        out_specs=[vmem] * 4,
        scratch_shapes=[
            pltpu.VMEM((3 * PHASES * width, LANES), F32),
            pltpu.VMEM((entries, ROWS, LANES), F32),
            pltpu.VMEM((entries, ROWS, LANES), F32),
            pltpu.VMEM((6 + 3 * PHASES, ROWS, LANES), F32),
            pltpu.VMEM((padded, LANES), F32),
            pltpu.SMEM((ROWS, LANES), jnp.int32),
            pltpu.SemaphoreType.DMA,
            pltpu.SemaphoreType.DMA((padded,)),
        ],
        **small("cloud_models", 12, 40 << 20),
    )(*row_blocks, state)


def condensate(workers, slots, cells, levels, meta, fin, tendency):
    groups = fin.shape[0]
    padded = groups * ROWS
    width = cells // levels
    capacity = slots // workers
    vmem = pl.BlockSpec(memory_space=pltpu.VMEM)
    block = -(-(cells // LANES) // ROWS) * ROWS
    outs = pl.pallas_call(
        functools.partial(cloud_kernel, levels, width, workers, capacity),
        out_shape=[jax.ShapeDtypeStruct((padded, cells), F32)]
        + [jax.ShapeDtypeStruct((capacity * block, LANES), F32)] * workers,
        in_specs=[pl.BlockSpec(memory_space=pltpu.SMEM), vmem, vmem],
        out_specs=[vmem] * (workers + 1),
        scratch_shapes=[pltpu.VMEM((padded * block, LANES), F32), pltpu.VMEM((groups, PHASES * width, LANES), F32)],
        **small("condensate", moved=8 << 20),
    )(meta, fin, tendency)
    return outs[0], outs[1:]


def state_rows(slots, levels, columns, meta, fin, tendency, water, start, tendencies, index, weight, level_map):
    width = fin.shape[1] // (3 * PHASES) * ROWS
    fields, padded, cells = start.shape
    vmem = pl.BlockSpec(memory_space=pltpu.VMEM)
    workers = len(tendencies)
    return pl.pallas_call(
        functools.partial(state_kernel, slots, levels, width, columns, workers),
        out_shape=[
            jax.ShapeDtypeStruct((fields, slots, cells), F32),
            jax.ShapeDtypeStruct((columns, LANES), F32),
            jax.ShapeDtypeStruct((2, LANES, level_map.shape[1]), F32),
        ],
        in_specs=[pl.BlockSpec(memory_space=pltpu.SMEM)] + [vmem] * (workers + 7),
        out_specs=[pl.BlockSpec(memory_space=pl.ANY), vmem, vmem],
        scratch_shapes=[
            pltpu.VMEM((fields, padded, cells), F32),
            pltpu.VMEM((2 * fin.shape[0], PHASES * width, LANES), F32),
            pltpu.SemaphoreType.DMA((slots,)),
        ],
        **small("state_rows", 12, moved=12 << 20),
    )(meta, fin, tendency, water, start, *tendencies, index, weight, level_map)


def edge_kernel(levels, columns, workers, *refs):
    t_refs, out = refs[:workers], refs[workers]
    _, _, lane_column, lane_owner = lanes_of(levels)
    me = lax.axis_index("crm")
    wanted = jnp.where(me == 0, workers - 1, 0).astype(F32)
    rows = jnp.concatenate([ref[...] for ref in t_refs], axis=0)
    lane = iota(rows.shape, 1).astype(F32)
    owner = rows[:, lane_owner : lane_owner + 1]
    column = rows[:, lane_column : lane_column + 1]
    select = ((owner == wanted) & (column == lane + 1.0)).astype(F32)
    out[...] = dot_t(select, rows)[:columns]


def share_rows(index, weight):
    rows = weight[...]
    total = jnp.sum(rows, axis=0, keepdims=True)
    return index[...].astype(F32), rows / total


def inner_blocks(levels, columns, workers, *refs):
    t_refs = refs[:workers]
    index, weight, level_map, inner, maps = refs[workers:]
    _, _, lane_column, lane_owner = lanes_of(levels)
    me = lax.axis_index("crm")
    rows = jnp.concatenate([ref[...] for ref in t_refs], axis=0)
    owner = rows[:, lane_owner : lane_owner + 1]
    column = rows[:, lane_column : lane_column + 1]
    block = owner - me.astype(F32) + 1.0
    named = (column > 0.0) & (block >= 0.0) & (block <= 2.0)
    ident = jnp.where(named, block * columns + column - 1.0, -1.0)
    wanted, share = share_rows(index, weight)
    mix = jnp.zeros((rows.shape[0], columns), F32)
    for source in range(index.shape[0]):
        mix = mix + jnp.where(ident == wanted[source : source + 1], share[source : source + 1], 0.0)
    inner[...] = dot_t(mix, rows)
    spread_row = iota((levels, LANES), 0)
    spread_lane = iota((levels, LANES), 1)
    for variable in range(2):
        place = (spread_lane == spread_row + variable * levels).astype(F32)
        maps[variable] = dot_t(place, level_map[...])


def physics_kernel(columns, workers, inner, maps, edge, index, weight, out):
    me = lax.axis_index("crm")
    edge_sub = iota((columns, 1), 0)
    edge_block = jnp.where(me == 0, 0, jnp.where(me == workers - 1, 2, -3))
    ident = (edge_block * columns + edge_sub).astype(F32)
    wanted, share = share_rows(index, weight)
    mix = jnp.zeros((columns, columns), F32)
    for source in range(index.shape[0]):
        mix = mix + jnp.where(ident == wanted[source : source + 1], share[source : source + 1], 0.0)
    mixed = inner[...] + dot_t(mix, jnp.where(edge_block >= 0, edge[...], 0.0))
    for variable in range(2):
        out[:, variable, :] = dot(mixed, maps[variable])


def gather_kernel(columns, capacity, workers, *refs):
    target = refs[0]
    received = refs[1 : workers + 1]
    out, counts, column_of, places = refs[workers + 1 :]
    tiles = out.shape[1] // LANES
    block = -(-tiles // ROWS) * ROWS
    me = lax.axis_index("crm")
    for worker in range(workers):
        counts[worker] = 0
    for entry in range(workers * capacity):
        column_of[entry] = columns
    for column in range(columns):
        worker = target[column]
        rank = counts[worker]
        counts[worker] = rank + 1
        column_of[(worker ^ me) * capacity + rank] = column
    for distance in range(workers):
        for rank in range(capacity):
            place = pl.multiple_of(column_of[distance * capacity + rank] * block, ROWS)
            places[pl.ds(place, block), :] = received[distance][rank * block : (rank + 1) * block, :]
    for base in range(0, columns, ROWS):
        count = min(ROWS, columns - base)
        for tile in range(tiles):
            rows = places[pl.ds(base * block + tile, count, stride=block), :]
            out[base : base + count, tile * LANES : (tile + 1) * LANES] = rows


def exchange(blocks, axis):
    size = lax.axis_size(axis)
    out = [blocks[0]]
    for distance in range(1, size):
        out.append(lax.ppermute(blocks[distance], axis, [(i, i ^ distance) for i in range(size)]))
    return out


def body(crm_state, forcing, target, cost_class, level_map, remap_index, remap_weight):
    workers = lax.axis_size("crm")
    groups = lax.axis_size("grp")
    columns = forcing.shape[0]
    slots, _, cells = crm_state.shape
    capacity = slots // workers
    levels, gcm = level_map.shape
    vmem = pl.BlockSpec(memory_space=pltpu.VMEM)

    rows = pack(target, cost_class, forcing, level_map, workers, capacity)
    row_blocks = exchange([rows] * workers, "crm")
    fin, start, tendency, meta = run_models(row_blocks, in_hbm(crm_state.transpose(1, 0, 2)), levels)
    tendencies = exchange([tendency] * workers, "crm")
    water, clouds = condensate(workers, slots, cells, levels, meta, fin, tendency)
    tendencies, clouds = lax.optimization_barrier((tendencies, clouds))
    clouds = exchange(clouds, "crm")

    edge = pl.pallas_call(
        functools.partial(edge_kernel, levels, columns, workers),
        out_shape=jax.ShapeDtypeStruct((columns, LANES), F32),
        in_specs=[vmem] * workers,
        out_specs=vmem,
        **small("edge_columns"),
    )(*tendencies)
    pairs = []
    for group in range(groups):
        after = (group + 1) % groups
        pairs.append((group * workers, after * workers))
        pairs.append((after * workers + workers - 1, group * workers + workers - 1))
    edge, meta, tendencies = lax.optimization_barrier((edge, meta, tendencies))
    edge = lax.ppermute(edge, ("grp", "crm"), pairs)
    state, inner, maps = state_rows(
        slots, levels, columns, meta, fin, tendency, water, start, tendencies, remap_index.T, remap_weight.T, level_map
    )
    block = clouds[0].shape[0] // capacity
    cloud_water = pl.pallas_call(
        functools.partial(gather_kernel, columns, capacity, workers),
        out_shape=jax.ShapeDtypeStruct((columns, cells), F32),
        in_specs=[pl.BlockSpec(memory_space=pltpu.SMEM)] + [vmem] * workers,
        out_specs=vmem,
        scratch_shapes=[
            pltpu.SMEM((workers,), jnp.int32),
            pltpu.SMEM((slots,), jnp.int32),
            pltpu.VMEM(((columns + 1) * block, LANES), F32),
        ],
        **small("cloud_rows"),
    )(target, *clouds)
    inner, maps, cloud_water = lax.optimization_barrier((inner, maps, cloud_water))
    physics = pl.pallas_call(
        functools.partial(physics_kernel, columns, workers),
        out_shape=jax.ShapeDtypeStruct((columns, 2, gcm), F32),
        in_specs=[vmem] * 5,
        out_specs=vmem,
        **small("physics_cells"),
    )(inner, maps, edge, remap_index.T, remap_weight.T)
    return state.transpose(1, 0, 2), cloud_water, physics


def solution(mesh):
    wide = P(("grp", "crm"), None, None)
    flat = P(("grp", "crm"), None)
    line = P(("grp", "crm"))
    in_specs = (wide, wide, line, line, P(), flat, flat)
    out_specs = (wide, flat, wide)
    return jax.shard_map(body, mesh=mesh, in_specs=in_specs, out_specs=out_specs, check_vma=False)
```

```python
import functools

import jax
import jax.numpy as jnp
from jax import lax
from jax.experimental import pallas as pl
from jax.experimental.pallas import tpu as pltpu
from jax.sharding import PartitionSpec as P

CLASSES = 3
SUB = 4
DIFFUSE_HORIZ = 0.2
DIFFUSE_VERT = 0.1
CONDENSE_RATE = 3.0
LINEAR_DRAG = 0.1
MOIST_BUOYANCY = 0.6
HIGHEST = lax.Precision.HIGHEST
F32 = jnp.float32
LANES = 128
ROWS = 8
PHASES = 4
MIB = 1 << 20


def in_hbm(x):
    return pltpu.with_memory_space_constraint(x, pltpu.HBM)


def iota(shape, axis):
    return lax.broadcasted_iota(jnp.int32, shape, axis)


def dot_t(lhs, rhs):
    return lax.dot_general(lhs, rhs, (((0,), (0,)), ((), ())), precision=HIGHEST, preferred_element_type=F32)


def dot(lhs, rhs):
    return jnp.dot(lhs, rhs, precision=HIGHEST, preferred_element_type=F32)


def all_rows(x):
    x = x + pltpu.roll(x, 4, 0)
    x = x + pltpu.roll(x, 2, 0)
    return x + pltpu.roll(x, 1, 0)


def lanes_of(levels):
    base = 2 * levels
    return base, base + 1, base + 2, base + 3


def pack_kernel(capacity, workers, target_hbm, cost_hbm, forcing_hbm, level_hbm, rows, target, cost, forcing, level_map, counts, spread, sems):
    pairs = ((target_hbm, target), (cost_hbm, cost), (forcing_hbm, forcing), (level_hbm, level_map))
    copies = [pltpu.make_async_copy(source, place, sems.at[i]) for i, (source, place) in enumerate(pairs)]
    for copy in copies:
        copy.start()
    for copy in copies:
        copy.wait()
    levels, gcm = level_map.shape
    columns = forcing.shape[0]
    lane_class, lane_slot, lane_column, lane_owner = lanes_of(levels)
    me = lax.axis_index("crm")
    for worker in range(workers):
        counts[worker] = 0
    sub = iota((columns, LANES), 0)
    lane = iota((columns, LANES), 1)
    classes = jnp.zeros((columns, LANES), F32)
    slots = jnp.zeros((columns, LANES), F32)
    for column in range(columns):
        worker = target[column]
        rank = counts[worker]
        counts[worker] = rank + 1
        slot = (worker * workers + me) * capacity + rank
        classes = jnp.where(sub == column, cost[column].astype(F32), classes)
        slots = jnp.where(sub == column, slot.astype(F32), slots)
    spread[...] = jnp.zeros(spread.shape, F32)
    mapped = jnp.zeros((columns, LANES), F32)
    for variable in range(2):
        spread[variable, variable * levels : (variable + 1) * levels, :] = level_map[...]
        mapped = mapped + lax.dot_general(
            forcing[:, variable, :],
            spread[variable],
            (((1,), (1,)), ((), ())),
            precision=HIGHEST,
            preferred_element_type=F32,
        )
    meta = jnp.where(lane == lane_class, classes, 0.0)
    meta = jnp.where(lane == lane_slot, slots, meta)
    meta = jnp.where(lane == lane_column, (sub + 1).astype(F32), meta)
    meta = jnp.where(lane == lane_owner, me.astype(F32), meta)
    rows[...] = jnp.where(lane < lane_class, mapped, meta)


def pack(target, cost, forcing, level_map, workers, capacity):
    columns = forcing.shape[0]
    return pl.pallas_call(
        functools.partial(pack_kernel, capacity, workers),
        out_shape=jax.ShapeDtypeStruct((columns, LANES), F32),
        in_specs=[pl.BlockSpec(memory_space=pl.ANY)] * 4,
        out_specs=pl.BlockSpec(memory_space=pltpu.VMEM),
        scratch_shapes=[
            pltpu.SMEM(target.shape, jnp.int32),
            pltpu.SMEM(cost.shape, jnp.int32),
            pltpu.VMEM(forcing.shape, F32),
            pltpu.VMEM(level_map.shape, F32),
            pltpu.SMEM((workers,), jnp.int32),
            pltpu.VMEM((2, LANES, forcing.shape[2]), F32),
            pltpu.SemaphoreType.DMA((4,)),
        ],
        compiler_params=pltpu.CompilerParams(vmem_limit_bytes=8 * MIB),
        name="pack_forcing",
    )(*(in_hbm(x) for x in (target, cost, forcing, level_map)))


def model_kernel(workers, slots, levels, width, *refs):
    row_refs = refs[:workers]
    x_hbm, fin, xs, t_ref, meta_v, nat, s1, saved, coef, rows_s, meta_s, sem_meta, sem_in = refs[workers:]
    groups = xs.shape[1] // ROWS
    padded = groups * ROWS
    capacity = slots // workers
    tiles = levels * width // LANES
    residues = width // ROWS
    lane_class, lane_slot, lane_column, lane_owner = lanes_of(levels)
    me = lax.axis_index("crm")

    rows = jnp.concatenate([ref[...] for ref in row_refs], axis=0)
    lane_c = iota(rows.shape, 1)
    local = rows[:, lane_slot : lane_slot + 1] - (me * slots).astype(F32)
    member = (local == lane_c.astype(F32)) & (lane_c < slots)
    class_row = jnp.sum(jnp.where(member, rows[:, lane_class : lane_class + 1], 0.0), axis=0, keepdims=True)
    sub_p = iota((padded, LANES), 0)
    lane_p = iota((padded, LANES), 1)
    key_row = class_row * LANES + (LANES - 1 - iota((1, LANES), 1)).astype(F32)
    key_col = jnp.sum(jnp.where(sub_p == lane_p, key_row, 0.0), axis=1, keepdims=True)
    class_col = jnp.sum(jnp.where(sub_p == lane_p, class_row, 0.0), axis=1, keepdims=True)
    ahead_row = ((key_col > key_row) & (sub_p < slots)).astype(F32)
    place_row = jnp.sum(ahead_row, axis=0, keepdims=True)
    ahead_col = ((key_row > key_col) & (lane_p < slots)).astype(F32)
    place_col = jnp.sum(ahead_col, axis=1, keepdims=True)
    here = (place_col == lane_p.astype(F32)) & (sub_p < slots)
    order = jnp.sum(jnp.where(here, sub_p.astype(F32), 0.0), axis=0, keepdims=True)
    class_sorted = jnp.sum(jnp.where(here, class_col, 0.0), axis=0, keepdims=True)
    sub_m = iota((ROWS, LANES), 0)
    lane_m = iota((ROWS, LANES), 1)
    owner_row = jnp.floor((order + 0.5) * (1.0 / capacity))
    rank_row = order - owner_row * capacity
    away_row = owner_row.astype(jnp.int32) ^ me
    table = jnp.where(sub_m == 0, order, jnp.where(sub_m == 1, class_sorted, rank_row)).astype(jnp.int32)
    table = jnp.where(sub_m == 2, away_row, table)
    meta_v[...] = jnp.where(sub_m == 4, place_row.astype(jnp.int32), table)
    fetch = pltpu.make_async_copy(meta_v, meta_s, sem_meta)
    fetch.start()
    fetch.wait()

    def load(index, carry):
        slot = meta_s[0, index]
        pltpu.make_async_copy(x_hbm.at[:, pl.ds(slot, 1), :], xs.at[:, pl.ds(index, 1), :], sem_in.at[index]).start()
        return carry

    lax.fori_loop(0, padded, load, 0, unroll=4)
    place_of = jnp.sum(jnp.where(member, place_row + 1.0, 0.0), axis=1, keepdims=True) - 1.0
    rows_s[...] = dot_t((place_of == lane_c.astype(F32)).astype(F32), rows)[:padded]

    model_of = lax.rem(lane_m, ROWS)
    step_of = lane_m // ROWS
    own = model_of == sub_m

    def coef_index(name, phase=0):
        names = ("a", "bx", "c0", "c1", "aw", "ac")
        return names.index(name) if name in names else len(names) + ("fh", "fq", "fs").index(name) * PHASES + phase

    def at(field, phase, residue):
        return (field * PHASES + phase) * residues + residue

    def substep(src, dst, means, last):
        next_means = []

        def self_at(field, phase, residue):
            return src[at(field, phase, residue)]

        def above(field, phase, residue):
            if phase < PHASES - 1:
                return src[at(field, phase + 1, residue)]
            return pltpu.roll(src[at(field, 0, residue)], LANES - ROWS, 1)

        def below(field, phase, residue):
            if phase > 0:
                return src[at(field, phase - 1, residue)]
            return pltpu.roll(src[at(field, PHASES - 1, residue)], ROWS, 1)

        a, bx, aw, ac = (coef[coef_index(name)] for name in ("a", "bx", "aw", "ac"))
        for phase in range(PHASES):
            c1 = coef[coef_index("c0" if phase < 2 else "c1")]
            fh, fq, fs = (coef[coef_index(name, phase)] for name in ("fh", "fq", "fs"))
            def around(field, residue):
                if residue > 0:
                    left = self_at(field, phase, residue - 1)
                else:
                    left = pltpu.roll(self_at(field, phase, residues - 1), 1, 0)
                if residue < residues - 1:
                    return left + self_at(field, phase, residue + 1)
                return left + pltpu.roll(self_at(field, phase, 0), ROWS - 1, 0)

            pushed = []
            for residue in range(residues):
                wind = self_at(2, phase, residue)
                new_wind = (aw * wind + (self_at(0, phase, residue) - self_at(1, phase, residue))) + bx * around(2, residue)
                new_wind = new_wind + c1 * (above(2, phase, residue) + below(2, phase, residue))
                if not last:
                    dst[at(2, phase, residue)] = new_wind
                pushed.append(new_wind)
            total = pushed
            while len(total) > 1:
                total = [sum(total[i : i + 2]) for i in range(0, len(total), 2)]
            mean = all_rows(total[0]) * (1.0 / width)
            next_means.append(mean)
            if last:
                for residue in range(residues):
                    dst[at(2, phase, residue)] = pushed[residue] - mean
            up_base = c1 if means is None else c1 + means[phase]
            down_base = c1 if means is None else c1 - means[phase]
            for residue in range(residues):
                heat, moist, wind = (self_at(field, phase, residue) for field in range(3))
                up_coef = up_base - wind
                down_coef = down_base + wind
                new_heat = (a * heat + fh) + bx * around(0, residue)
                dst[at(0, phase, residue)] = new_heat + (
                    up_coef * above(0, phase, residue) + down_coef * below(0, phase, residue)
                )
                new_moist = jnp.minimum(a * moist + fq, ac * moist + fs) + bx * around(1, residue)
                dst[at(1, phase, residue)] = new_moist + (
                    up_coef * above(1, phase, residue) + down_coef * below(1, phase, residue)
                )
        return next_means

    def run_group(group, carry):
        base = pl.multiple_of(group * ROWS, ROWS)
        units = meta_s[1, base]
        mixed = meta_s[1, base + ROWS - 1] != units

        for member in range(ROWS):
            index = base + member
            pltpu.make_async_copy(x_hbm.at[:, pl.ds(0, 1), :], xs.at[:, pl.ds(index, 1), :], sem_in.at[index]).wait()

        s0 = fin.at[group]

        @pl.when(units > 0)
        def _():
            mine = rows_s[pl.ds(base, ROWS), :]
            class_m = mine[:, lane_class : lane_class + 1]
            class_l = all_rows(jnp.where(own, class_m, 0.0))
            steps = jnp.maximum(class_l * SUB, 1.0)
            dt = 1.0 / steps
            scale = 0.5 * dt * dt
            moist_weight = 1.0 - MOIST_BUOYANCY
            diffuse = 1.0 - 2.0 * (DIFFUSE_HORIZ + DIFFUSE_VERT) * dt
            coef[coef_index("a")] = diffuse
            coef[coef_index("bx")] = DIFFUSE_HORIZ * dt
            inside = [(PHASES * step_of + phase) < levels for phase in range(PHASES)]
            coef[coef_index("c0")] = jnp.where(inside[1], DIFFUSE_VERT * dt, 0.0)
            coef[coef_index("c1")] = jnp.where(inside[3], DIFFUSE_VERT * dt, 0.0)
            coef[coef_index("aw")] = diffuse - LINEAR_DRAG * dt
            coef[coef_index("ac")] = diffuse - CONDENSE_RATE * dt
            for phase in range(PHASES):
                level = PHASES * step_of + phase
                pick = jnp.minimum(level, levels - 1)
                keep = own & inside[phase]
                force = [
                    all_rows(jnp.where(keep, jnp.take_along_axis(mine, pick + variable * levels, axis=1), 0.0))
                    for variable in range(2)
                ]
                saturated = jnp.where(inside[phase], 1.0 - 2.0 * (level.astype(F32) + 0.5) / levels, 0.0)
                fq = (moist_weight * scale * dt) * force[1]
                coef[coef_index("fh", phase)] = (scale * dt) * (force[0] + force[1])
                coef[coef_index("fq", phase)] = fq
                coef[coef_index("fs", phase)] = fq + (CONDENSE_RATE * moist_weight) * dt * scale * saturated

            zero = jnp.zeros((ROWS, LANES), F32)
            for field in range(3):
                for half in range(2):
                    parts = []
                    for step in range(LANES // ROWS):
                        tile = 2 * step + half
                        parts.append(xs[field, pl.ds(base, ROWS), tile * LANES : (tile + 1) * LANES] if tile < tiles else zero)
                    start = (field * PHASES + 2 * half) * width
                    nat[start : start + LANES, :] = jnp.concatenate(parts, axis=0).T

            def natural(field, phase, residue):
                return pl.ds((field * PHASES + phase) * width + residue, ROWS, stride=residues)

            moist_scale = moist_weight * scale
            wind_scale = 0.5 * dt
            before = []
            for phase in range(PHASES):
                sums = [jnp.zeros((ROWS, LANES), F32)] * 2
                for residue in range(residues):
                    theta, moist, wind = (nat[natural(field, phase, residue), :] for field in range(3))
                    scaled = (scale * (theta + moist), moist_scale * moist, wind_scale * wind)
                    for field in range(3):
                        s0[at(field, phase, residue)] = scaled[field]
                    sums = [sums[variable] + scaled[variable] for variable in range(2)]
                before.append(sums)

            def unit(index, inner):
                means = None
                for step in range(SUB):
                    means = substep(*((s0, s1) if step % 2 == 0 else (s1, s0)), means, step == SUB - 1)

                done = class_l == (index + 1).astype(F32)

                def keep(chunk, kept):
                    for residue in range(residues):
                        entry = chunk * residues + residue
                        saved[entry] = jnp.where(done, s0[entry], saved[entry])
                    return kept

                lax.fori_loop(0, jnp.where(mixed & (index + 1 < units), 3 * PHASES, 0), keep, 0)
                return inner

            lax.fori_loop(0, units, unit, 0)

            last = class_l == units.astype(F32)

            def restore(chunk, kept):
                for residue in range(residues):
                    entry = chunk * residues + residue
                    s0[entry] = jnp.where(last, s0[entry], saved[entry])
                return kept

            lax.fori_loop(0, jnp.where(mixed, 3 * PHASES, 0), restore, 0)
            heat_share = (2.0 / width) * steps * steps
            moist_share = heat_share * (1.0 / moist_weight)
            change = []
            for phase in range(PHASES):
                sums = [-value for value in before[phase]]
                for residue in range(residues):
                    sums = [sums[variable] + s0[at(variable, phase, residue)] for variable in range(2)]
                moist = moist_share * all_rows(sums[1])
                change.append((heat_share * all_rows(sums[0]) - moist, moist))

            active = class_m > 0.0
            second = lane_m >= levels
            level = jnp.where(second, lane_m - levels, lane_m)
            pick = jnp.minimum(level // PHASES * ROWS + sub_m, LANES - 1)
            which = lax.rem(level, PHASES)
            tendency = jnp.zeros((ROWS, LANES), F32)
            for phase in range(PHASES):
                found = [jnp.take_along_axis(change[phase][variable], pick, axis=1) for variable in range(2)]
                tendency = jnp.where(which == phase, jnp.where(second, found[1], found[0]), tendency)
            t_ref[pl.ds(base, ROWS), :] = jnp.where((lane_m < lane_class) & active, tendency, jnp.where(lane_m < lane_class, 0.0, mine))

        @pl.when(units <= 0)
        def _():
            t_ref[pl.ds(base, ROWS), :] = jnp.zeros((ROWS, LANES), F32)

        return carry

    lax.fori_loop(0, groups, run_group, 0)


def turned(fin, nat, group, field, width):
    residues = width // ROWS
    tiles = {}
    for half in range(2):
        for pair in range(2):
            phase = 2 * half + pair
            for residue in range(residues):
                spot = pl.ds(phase * width + residue, ROWS, stride=residues)
                nat[spot, :] = fin[group, (field * PHASES + phase) * residues + residue]
        back = nat[2 * half * width : 2 * half * width + LANES, :].T
        for step in range(LANES // ROWS):
            tiles[2 * step + half] = back[step * ROWS : (step + 1) * ROWS]
    return tiles


def weights_of(t_ref, base, lane_class):
    class_m = t_ref[pl.ds(base, ROWS), lane_class : lane_class + 1]
    steps = jnp.broadcast_to(jnp.maximum(class_m * SUB, 1.0), (ROWS, LANES))
    heat = 2.0 * steps * steps
    return class_m > 0.0, heat, heat * (1.0 / (1.0 - MOIST_BUOYANCY)), 2.0 * steps


def cloud_kernel(levels, width, workers, capacity, meta, fin, t_ref, water, *refs):
    outs = refs[:workers]
    cl, nat = refs[workers:]
    tiles = levels * width // LANES
    block = outs[0].shape[0] // capacity
    lane_m = iota((ROWS, LANES), 1)
    lane_class = lanes_of(levels)[0]
    me = lax.axis_index("crm")
    for group in range(fin.shape[0]):
        base = group * ROWS
        _, _, moist_weight, _ = weights_of(t_ref, base, lane_class)
        parts = turned(fin, nat.at[group], group, 1, width)
        for tile in range(tiles):
            value = moist_weight * parts[tile]
            level = (LANES // width) * tile + lane_m // width
            saturated = 1.0 - 2.0 * (level.astype(F32) + 0.5) / levels
            water[base : base + ROWS, tile * LANES : (tile + 1) * LANES] = value
            cl[pl.ds(base * block + tile, ROWS, stride=block), :] = jnp.maximum(value - saturated, 0.0)
    for distance in range(workers):
        first = (me ^ distance) * capacity
        for rank in range(capacity):
            source = pl.multiple_of(meta[4, first + rank] * block, ROWS)
            outs[distance][rank * block : (rank + 1) * block, :] = cl[pl.ds(source, block), :]


def state_kernel(slots, levels, width, columns, workers, meta, fin, t_ref, water, xs, *refs):
    inner_refs = refs[: workers + 3]
    y_hbm, inner, maps, ys, nat, sems = refs[workers + 3 :]
    groups = fin.shape[0]
    tiles = levels * width // LANES
    lane_class = lanes_of(levels)[0]
    copies = []
    for group in range(groups):
        base = group * ROWS
        active, heat_weight, _, wind_weight = weights_of(t_ref, base, lane_class)
        heats = turned(fin, nat.at[2 * group], group, 0, width)
        winds = turned(fin, nat.at[2 * group + 1], group, 2, width)
        for tile in range(tiles):
            lanes = slice(tile * LANES, (tile + 1) * LANES)
            moist = water[base : base + ROWS, lanes]
            values = (heat_weight * heats[tile] - moist, moist, wind_weight * winds[tile])
            for field in range(3):
                ys[field, base : base + ROWS, lanes] = jnp.where(active, values[field], xs[field, base : base + ROWS, lanes])
        for index in range(base, min(base + ROWS, slots)):
            copy = pltpu.make_async_copy(
                ys.at[:, pl.ds(index, 1), :], y_hbm.at[:, pl.ds(meta[0, index], 1), :], sems.at[index]
            )
            copy.start()
            copies.append(copy)
    inner_blocks(levels, columns, workers, *inner_refs, inner, maps)
    for copy in copies:
        copy.wait()


def small(name, mib=8, moved=1 << 20):
    cost = pl.CostEstimate(flops=0, bytes_accessed=moved, transcendentals=0)
    return dict(compiler_params=pltpu.CompilerParams(vmem_limit_bytes=mib * MIB), name=name, cost_estimate=cost)


def run_models(row_blocks, state, levels):
    workers = len(row_blocks)
    _, slots, cells = state.shape
    width = cells // levels
    groups = -(-slots // ROWS)
    padded = groups * ROWS
    vmem = pl.BlockSpec(memory_space=pltpu.VMEM)
    entries = 3 * PHASES * (width // ROWS)
    return pl.pallas_call(
        functools.partial(model_kernel, workers, slots, levels, width),
        out_shape=[
            jax.ShapeDtypeStruct((groups, entries, ROWS, LANES), F32),
            jax.ShapeDtypeStruct((3, padded, cells), F32),
            jax.ShapeDtypeStruct((padded, LANES), F32),
            jax.ShapeDtypeStruct((ROWS, LANES), jnp.int32),
        ],
        in_specs=[vmem] * workers + [pl.BlockSpec(memory_space=pl.ANY)],
        out_specs=[vmem] * 4,
        scratch_shapes=[
            pltpu.VMEM((3 * PHASES * width, LANES), F32),
            pltpu.VMEM((entries, ROWS, LANES), F32),
            pltpu.VMEM((entries, ROWS, LANES), F32),
            pltpu.VMEM((6 + 3 * PHASES, ROWS, LANES), F32),
            pltpu.VMEM((padded, LANES), F32),
            pltpu.SMEM((ROWS, LANES), jnp.int32),
            pltpu.SemaphoreType.DMA,
            pltpu.SemaphoreType.DMA((padded,)),
        ],
        **small("cloud_models", 12, 40 << 20),
    )(*row_blocks, state)


def condensate(workers, slots, cells, levels, meta, fin, tendency):
    groups = fin.shape[0]
    padded = groups * ROWS
    width = cells // levels
    capacity = slots // workers
    vmem = pl.BlockSpec(memory_space=pltpu.VMEM)
    block = -(-(cells // LANES) // ROWS) * ROWS
    outs = pl.pallas_call(
        functools.partial(cloud_kernel, levels, width, workers, capacity),
        out_shape=[jax.ShapeDtypeStruct((padded, cells), F32)]
        + [jax.ShapeDtypeStruct((capacity * block, LANES), F32)] * workers,
        in_specs=[pl.BlockSpec(memory_space=pltpu.SMEM), vmem, vmem],
        out_specs=[vmem] * (workers + 1),
        scratch_shapes=[pltpu.VMEM((padded * block, LANES), F32), pltpu.VMEM((groups, PHASES * width, LANES), F32)],
        **small("condensate", moved=8 << 20),
    )(meta, fin, tendency)
    return outs[0], outs[1:]


def state_rows(slots, levels, columns, meta, fin, tendency, water, start, tendencies, index, weight, level_map):
    width = fin.shape[1] // (3 * PHASES) * ROWS
    fields, padded, cells = start.shape
    vmem = pl.BlockSpec(memory_space=pltpu.VMEM)
    workers = len(tendencies)
    return pl.pallas_call(
        functools.partial(state_kernel, slots, levels, width, columns, workers),
        out_shape=[
            jax.ShapeDtypeStruct((fields, slots, cells), F32),
            jax.ShapeDtypeStruct((columns, LANES), F32),
            jax.ShapeDtypeStruct((2, LANES, level_map.shape[1]), F32),
        ],
        in_specs=[pl.BlockSpec(memory_space=pltpu.SMEM)] + [vmem] * (workers + 7),
        out_specs=[pl.BlockSpec(memory_space=pl.ANY), vmem, vmem],
        scratch_shapes=[
            pltpu.VMEM((fields, padded, cells), F32),
            pltpu.VMEM((2 * fin.shape[0], PHASES * width, LANES), F32),
            pltpu.SemaphoreType.DMA((slots,)),
        ],
        **small("state_rows", 12, moved=12 << 20),
    )(meta, fin, tendency, water, start, *tendencies, index, weight, level_map)


def edge_kernel(levels, columns, workers, *refs):
    t_refs, out = refs[:workers], refs[workers]
    _, _, lane_column, lane_owner = lanes_of(levels)
    me = lax.axis_index("crm")
    wanted = jnp.where(me == 0, workers - 1, 0).astype(F32)
    rows = jnp.concatenate([ref[...] for ref in t_refs], axis=0)
    lane = iota(rows.shape, 1).astype(F32)
    owner = rows[:, lane_owner : lane_owner + 1]
    column = rows[:, lane_column : lane_column + 1]
    select = ((owner == wanted) & (column == lane + 1.0)).astype(F32)
    out[...] = dot_t(select, rows)[:columns]


def share_rows(index, weight):
    rows = weight[...]
    total = jnp.sum(rows, axis=0, keepdims=True)
    return index[...].astype(F32), rows / total


def inner_blocks(levels, columns, workers, *refs):
    t_refs = refs[:workers]
    index, weight, level_map, inner, maps = refs[workers:]
    _, _, lane_column, lane_owner = lanes_of(levels)
    me = lax.axis_index("crm")
    rows = jnp.concatenate([ref[...] for ref in t_refs], axis=0)
    owner = rows[:, lane_owner : lane_owner + 1]
    column = rows[:, lane_column : lane_column + 1]
    block = owner - me.astype(F32) + 1.0
    named = (column > 0.0) & (block >= 0.0) & (block <= 2.0)
    ident = jnp.where(named, block * columns + column - 1.0, -1.0)
    wanted, share = share_rows(index, weight)
    mix = jnp.zeros((rows.shape[0], columns), F32)
    for source in range(index.shape[0]):
        mix = mix + jnp.where(ident == wanted[source : source + 1], share[source : source + 1], 0.0)
    inner[...] = dot_t(mix, rows)
    spread_row = iota((levels, LANES), 0)
    spread_lane = iota((levels, LANES), 1)
    for variable in range(2):
        place = (spread_lane == spread_row + variable * levels).astype(F32)
        maps[variable] = dot_t(place, level_map[...])


def finish_kernel(columns, capacity, workers, *refs):
    target = refs[0]
    received = refs[1 : workers + 1]
    inner, maps, edge, index, weight, cloud_hbm, physics_hbm, counts, column_of, places, cloud, physics, sems = refs[workers + 1 :]
    tiles = cloud.shape[1] // LANES
    block = -(-tiles // ROWS) * ROWS
    me = lax.axis_index("crm")
    for worker in range(workers):
        counts[worker] = 0
    for entry in range(workers * capacity):
        column_of[entry] = columns
    for column in range(columns):
        worker = target[column]
        rank = counts[worker]
        counts[worker] = rank + 1
        column_of[(worker ^ me) * capacity + rank] = column
    for distance in range(workers):
        for rank in range(capacity):
            place = pl.multiple_of(column_of[distance * capacity + rank] * block, ROWS)
            places[pl.ds(place, block), :] = received[distance][rank * block : (rank + 1) * block, :]
    chunk = ROWS if columns % ROWS == 0 else columns
    copies = []
    for base in range(0, columns, chunk):
        for tile in range(tiles):
            rows = places[pl.ds(base * block + tile, chunk, stride=block), :]
            cloud[base : base + chunk, tile * LANES : (tile + 1) * LANES] = rows
        copies.append(
            pltpu.make_async_copy(cloud.at[pl.ds(base, chunk), :], cloud_hbm.at[pl.ds(base, chunk), :], sems.at[len(copies)])
        )
        copies[-1].start()

    edge_sub = iota((columns, 1), 0)
    edge_block = jnp.where(me == 0, 0, jnp.where(me == workers - 1, 2, -3))
    ident = (edge_block * columns + edge_sub).astype(F32)
    wanted, share = share_rows(index, weight)
    mix = jnp.zeros((columns, columns), F32)
    for source in range(index.shape[0]):
        mix = mix + jnp.where(ident == wanted[source : source + 1], share[source : source + 1], 0.0)
    mixed = inner[...] + dot_t(mix, jnp.where(edge_block >= 0, edge[...], 0.0))
    for variable in range(2):
        physics[:, variable, :] = dot(mixed, maps[variable])
    copies.append(pltpu.make_async_copy(physics, physics_hbm, sems.at[len(copies)]))
    copies[-1].start()
    for copy in copies:
        copy.wait()


def exchange(blocks, axis):
    size = lax.axis_size(axis)
    out = [blocks[0]]
    for distance in range(1, size):
        out.append(lax.ppermute(blocks[distance], axis, [(i, i ^ distance) for i in range(size)]))
    return out


def body(crm_state, forcing, target, cost_class, level_map, remap_index, remap_weight):
    workers = lax.axis_size("crm")
    groups = lax.axis_size("grp")
    columns = forcing.shape[0]
    slots, _, cells = crm_state.shape
    capacity = slots // workers
    levels, gcm = level_map.shape
    vmem = pl.BlockSpec(memory_space=pltpu.VMEM)

    rows = pack(target, cost_class, forcing, level_map, workers, capacity)
    row_blocks = exchange([rows] * workers, "crm")
    fin, start, tendency, meta = run_models(row_blocks, in_hbm(crm_state.transpose(1, 0, 2)), levels)
    tendencies = exchange([tendency] * workers, "crm")
    water, clouds = condensate(workers, slots, cells, levels, meta, fin, tendency)
    tendencies, clouds = lax.optimization_barrier((tendencies, clouds))
    clouds = exchange(clouds, "crm")

    edge = pl.pallas_call(
        functools.partial(edge_kernel, levels, columns, workers),
        out_shape=jax.ShapeDtypeStruct((columns, LANES), F32),
        in_specs=[vmem] * workers,
        out_specs=vmem,
        **small("edge_columns"),
    )(*tendencies)
    pairs = []
    for group in range(groups):
        after = (group + 1) % groups
        for worker in range(workers):
            ends = (group * workers + worker, after * workers + worker)
            pairs.append(ends if 2 * worker < workers else ends[::-1])
    edge, meta, tendencies = lax.optimization_barrier((edge, meta, tendencies))
    edge = lax.ppermute(edge, ("grp", "crm"), pairs)
    state, inner, maps = state_rows(
        slots, levels, columns, meta, fin, tendency, water, start, tendencies, remap_index.T, remap_weight.T, level_map
    )
    block = clouds[0].shape[0] // capacity
    cloud_water, physics = pl.pallas_call(
        functools.partial(finish_kernel, columns, capacity, workers),
        out_shape=[jax.ShapeDtypeStruct((columns, cells), F32), jax.ShapeDtypeStruct((columns, 2, gcm), F32)],
        in_specs=[pl.BlockSpec(memory_space=pltpu.SMEM)] + [vmem] * (workers + 5),
        out_specs=[pl.BlockSpec(memory_space=pl.ANY)] * 2,
        scratch_shapes=[
            pltpu.SMEM((workers,), jnp.int32),
            pltpu.SMEM((slots,), jnp.int32),
            pltpu.VMEM(((columns + 1) * block, LANES), F32),
            pltpu.VMEM((columns, cells), F32),
            pltpu.VMEM((columns, 2, gcm), F32),
            pltpu.SemaphoreType.DMA((-(-columns // ROWS) + 1,)),
        ],
        **small("columns_out"),
    )(target, *clouds, inner, maps, edge, remap_index.T, remap_weight.T)
    return state.transpose(1, 0, 2), cloud_water, physics


def solution(mesh):
    wide = P(("grp", "crm"), None, None)
    flat = P(("grp", "crm"), None)
    line = P(("grp", "crm"))
    in_specs = (wide, wide, line, line, P(), flat, flat)
    out_specs = (wide, flat, wide)
    return jax.shard_map(body, mesh=mesh, in_specs=in_specs, out_specs=out_specs, check_vma=False)
```

```python
import functools

import jax
import jax.numpy as jnp
from jax import lax
from jax.experimental import pallas as pl
from jax.experimental.pallas import tpu as pltpu
from jax.sharding import PartitionSpec as P

CLASSES = 3
SUB = 4
DIFFUSE_HORIZ = 0.2
DIFFUSE_VERT = 0.1
CONDENSE_RATE = 3.0
LINEAR_DRAG = 0.1
MOIST_BUOYANCY = 0.6
HIGHEST = lax.Precision.HIGHEST
F32 = jnp.float32
LANES = 128
ROWS = 8
PHASES = 4
MIB = 1 << 20


def in_hbm(x):
    return pltpu.with_memory_space_constraint(x, pltpu.HBM)


def iota(shape, axis):
    return lax.broadcasted_iota(jnp.int32, shape, axis)


def dot_t(lhs, rhs):
    return lax.dot_general(lhs, rhs, (((0,), (0,)), ((), ())), precision=HIGHEST, preferred_element_type=F32)


def dot(lhs, rhs):
    return jnp.dot(lhs, rhs, precision=HIGHEST, preferred_element_type=F32)


def all_rows(x):
    x = x + pltpu.roll(x, 4, 0)
    x = x + pltpu.roll(x, 2, 0)
    return x + pltpu.roll(x, 1, 0)


def lanes_of(levels):
    base = 2 * levels
    return base, base + 1, base + 2, base + 3


def pack_kernel(capacity, workers, target_hbm, cost_hbm, forcing_hbm, level_hbm, rows, target, cost, forcing, level_map, counts, spread, sems):
    pairs = ((target_hbm, target), (cost_hbm, cost), (forcing_hbm, forcing), (level_hbm, level_map))
    copies = [pltpu.make_async_copy(source, place, sems.at[i]) for i, (source, place) in enumerate(pairs)]
    for copy in copies:
        copy.start()
    for copy in copies:
        copy.wait()
    levels, gcm = level_map.shape
    columns = forcing.shape[0]
    lane_class, lane_slot, lane_column, lane_owner = lanes_of(levels)
    me = lax.axis_index("crm")
    for worker in range(workers):
        counts[worker] = 0
    sub = iota((columns, LANES), 0)
    lane = iota((columns, LANES), 1)
    classes = jnp.zeros((columns, LANES), F32)
    slots = jnp.zeros((columns, LANES), F32)
    for column in range(columns):
        worker = target[column]
        rank = counts[worker]
        counts[worker] = rank + 1
        slot = (worker * workers + me) * capacity + rank
        classes = jnp.where(sub == column, cost[column].astype(F32), classes)
        slots = jnp.where(sub == column, slot.astype(F32), slots)
    spread[...] = jnp.zeros(spread.shape, F32)
    mapped = jnp.zeros((columns, LANES), F32)
    for variable in range(2):
        spread[variable, variable * levels : (variable + 1) * levels, :] = level_map[...]
        mapped = mapped + lax.dot_general(
            forcing[:, variable, :],
            spread[variable],
            (((1,), (1,)), ((), ())),
            precision=HIGHEST,
            preferred_element_type=F32,
        )
    meta = jnp.where(lane == lane_class, classes, 0.0)
    meta = jnp.where(lane == lane_slot, slots, meta)
    meta = jnp.where(lane == lane_column, (sub + 1).astype(F32), meta)
    meta = jnp.where(lane == lane_owner, me.astype(F32), meta)
    rows[...] = jnp.where(lane < lane_class, mapped, meta)


def pack(target, cost, forcing, level_map, workers, capacity):
    columns = forcing.shape[0]
    return pl.pallas_call(
        functools.partial(pack_kernel, capacity, workers),
        out_shape=jax.ShapeDtypeStruct((columns, LANES), F32),
        in_specs=[pl.BlockSpec(memory_space=pl.ANY)] * 4,
        out_specs=pl.BlockSpec(memory_space=pltpu.VMEM),
        scratch_shapes=[
            pltpu.SMEM(target.shape, jnp.int32),
            pltpu.SMEM(cost.shape, jnp.int32),
            pltpu.VMEM(forcing.shape, F32),
            pltpu.VMEM(level_map.shape, F32),
            pltpu.SMEM((workers,), jnp.int32),
            pltpu.VMEM((2, LANES, forcing.shape[2]), F32),
            pltpu.SemaphoreType.DMA((4,)),
        ],
        compiler_params=pltpu.CompilerParams(vmem_limit_bytes=8 * MIB),
        name="pack_forcing",
    )(*(in_hbm(x) for x in (target, cost, forcing, level_map)))


def model_kernel(workers, slots, levels, width, *refs):
    row_refs = refs[:workers]
    x_hbm, fin, xs, t_ref, meta_v, nat, s1, saved, coef, rows_s, meta_s, sem_meta, sem_in = refs[workers:]
    groups = xs.shape[1] // ROWS
    padded = groups * ROWS
    capacity = slots // workers
    tiles = levels * width // LANES
    residues = width // ROWS
    lane_class, lane_slot, lane_column, lane_owner = lanes_of(levels)
    me = lax.axis_index("crm")

    rows = jnp.concatenate([ref[...] for ref in row_refs], axis=0)
    lane_c = iota(rows.shape, 1)
    local = rows[:, lane_slot : lane_slot + 1] - (me * slots).astype(F32)
    member = (local == lane_c.astype(F32)) & (lane_c < slots)
    class_row = jnp.sum(jnp.where(member, rows[:, lane_class : lane_class + 1], 0.0), axis=0, keepdims=True)
    sub_p = iota((padded, LANES), 0)
    lane_p = iota((padded, LANES), 1)
    key_row = class_row * LANES + (LANES - 1 - iota((1, LANES), 1)).astype(F32)
    key_col = jnp.sum(jnp.where(sub_p == lane_p, key_row, 0.0), axis=1, keepdims=True)
    class_col = jnp.sum(jnp.where(sub_p == lane_p, class_row, 0.0), axis=1, keepdims=True)
    ahead_row = ((key_col > key_row) & (sub_p < slots)).astype(F32)
    place_row = jnp.sum(ahead_row, axis=0, keepdims=True)
    ahead_col = ((key_row > key_col) & (lane_p < slots)).astype(F32)
    place_col = jnp.sum(ahead_col, axis=1, keepdims=True)
    here = (place_col == lane_p.astype(F32)) & (sub_p < slots)
    order = jnp.sum(jnp.where(here, sub_p.astype(F32), 0.0), axis=0, keepdims=True)
    class_sorted = jnp.sum(jnp.where(here, class_col, 0.0), axis=0, keepdims=True)
    sub_m = iota((ROWS, LANES), 0)
    lane_m = iota((ROWS, LANES), 1)
    owner_row = jnp.floor((order + 0.5) * (1.0 / capacity))
    rank_row = order - owner_row * capacity
    away_row = owner_row.astype(jnp.int32) ^ me
    table = jnp.where(sub_m == 0, order, jnp.where(sub_m == 1, class_sorted, rank_row)).astype(jnp.int32)
    table = jnp.where(sub_m == 2, away_row, table)
    meta_v[...] = jnp.where(sub_m == 4, place_row.astype(jnp.int32), table)
    fetch = pltpu.make_async_copy(meta_v, meta_s, sem_meta)
    fetch.start()
    fetch.wait()

    for index in range(padded):
        slot = meta_s[0, index]
        pltpu.make_async_copy(x_hbm.at[:, pl.ds(slot, 1), :], xs.at[:, pl.ds(index, 1), :], sem_in.at[index]).start()
    place_of = jnp.sum(jnp.where(member, place_row + 1.0, 0.0), axis=1, keepdims=True) - 1.0
    rows_s[...] = dot_t((place_of == lane_c.astype(F32)).astype(F32), rows)[:padded]

    model_of = lax.rem(lane_m, ROWS)
    step_of = lane_m // ROWS
    own = model_of == sub_m

    def coef_index(name, phase=0):
        names = ("a", "bx", "c0", "c1", "aw", "ac")
        return names.index(name) if name in names else len(names) + ("fh", "fq", "fs").index(name) * PHASES + phase

    def at(field, phase, residue):
        return (field * PHASES + phase) * residues + residue

    def substep(src, dst, means, last):
        next_means = []

        def self_at(field, phase, residue):
            return src[at(field, phase, residue)]

        def above(field, phase, residue):
            if phase < PHASES - 1:
                return src[at(field, phase + 1, residue)]
            return pltpu.roll(src[at(field, 0, residue)], LANES - ROWS, 1)

        def below(field, phase, residue):
            if phase > 0:
                return src[at(field, phase - 1, residue)]
            return pltpu.roll(src[at(field, PHASES - 1, residue)], ROWS, 1)

        a, bx, aw, ac = (coef[coef_index(name)] for name in ("a", "bx", "aw", "ac"))
        for phase in range(PHASES):
            c1 = coef[coef_index("c0" if phase < 2 else "c1")]
            fh, fq, fs = (coef[coef_index(name, phase)] for name in ("fh", "fq", "fs"))
            def around(field, residue):
                if residue > 0:
                    left = self_at(field, phase, residue - 1)
                else:
                    left = pltpu.roll(self_at(field, phase, residues - 1), 1, 0)
                if residue < residues - 1:
                    return left + self_at(field, phase, residue + 1)
                return left + pltpu.roll(self_at(field, phase, 0), ROWS - 1, 0)

            pushed = []
            for residue in range(residues):
                wind = self_at(2, phase, residue)
                new_wind = (aw * wind + (self_at(0, phase, residue) - self_at(1, phase, residue))) + bx * around(2, residue)
                new_wind = new_wind + c1 * (above(2, phase, residue) + below(2, phase, residue))
                if not last:
                    dst[at(2, phase, residue)] = new_wind
                pushed.append(new_wind)
            total = pushed
            while len(total) > 1:
                total = [sum(total[i : i + 2]) for i in range(0, len(total), 2)]
            mean = all_rows(total[0]) * (1.0 / width)
            next_means.append(mean)
            if last:
                for residue in range(residues):
                    dst[at(2, phase, residue)] = pushed[residue] - mean
            up_base = c1 if means is None else c1 + means[phase]
            down_base = c1 if means is None else c1 - means[phase]
            for residue in range(residues):
                heat, moist, wind = (self_at(field, phase, residue) for field in range(3))
                up_coef = up_base - wind
                down_coef = down_base + wind
                new_heat = (a * heat + fh) + bx * around(0, residue)
                dst[at(0, phase, residue)] = new_heat + (
                    up_coef * above(0, phase, residue) + down_coef * below(0, phase, residue)
                )
                new_moist = jnp.minimum(a * moist + fq, ac * moist + fs) + bx * around(1, residue)
                dst[at(1, phase, residue)] = new_moist + (
                    up_coef * above(1, phase, residue) + down_coef * below(1, phase, residue)
                )
        return next_means

    def run_group(group, carry):
        base = pl.multiple_of(group * ROWS, ROWS)
        units = meta_s[1, base]
        mixed = meta_s[1, base + ROWS - 1] != units

        for member in range(ROWS):
            index = base + member
            pltpu.make_async_copy(x_hbm.at[:, pl.ds(0, 1), :], xs.at[:, pl.ds(index, 1), :], sem_in.at[index]).wait()

        s0 = fin.at[group]

        @pl.when(units > 0)
        def _():
            mine = rows_s[pl.ds(base, ROWS), :]
            class_m = mine[:, lane_class : lane_class + 1]
            class_l = all_rows(jnp.where(own, class_m, 0.0))
            steps = jnp.maximum(class_l * SUB, 1.0)
            dt = 1.0 / steps
            scale = 0.5 * dt * dt
            moist_weight = 1.0 - MOIST_BUOYANCY
            diffuse = 1.0 - 2.0 * (DIFFUSE_HORIZ + DIFFUSE_VERT) * dt
            coef[coef_index("a")] = diffuse
            coef[coef_index("bx")] = DIFFUSE_HORIZ * dt
            inside = [(PHASES * step_of + phase) < levels for phase in range(PHASES)]
            coef[coef_index("c0")] = jnp.where(inside[1], DIFFUSE_VERT * dt, 0.0)
            coef[coef_index("c1")] = jnp.where(inside[3], DIFFUSE_VERT * dt, 0.0)
            coef[coef_index("aw")] = diffuse - LINEAR_DRAG * dt
            coef[coef_index("ac")] = diffuse - CONDENSE_RATE * dt
            for phase in range(PHASES):
                level = PHASES * step_of + phase
                pick = jnp.minimum(level, levels - 1)
                keep = own & inside[phase]
                force = [
                    all_rows(jnp.where(keep, jnp.take_along_axis(mine, pick + variable * levels, axis=1), 0.0))
                    for variable in range(2)
                ]
                saturated = jnp.where(inside[phase], 1.0 - 2.0 * (level.astype(F32) + 0.5) / levels, 0.0)
                fq = (moist_weight * scale * dt) * force[1]
                coef[coef_index("fh", phase)] = (scale * dt) * (force[0] + force[1])
                coef[coef_index("fq", phase)] = fq
                coef[coef_index("fs", phase)] = fq + (CONDENSE_RATE * moist_weight) * dt * scale * saturated

            zero = jnp.zeros((ROWS, LANES), F32)
            for field in range(3):
                for half in range(2):
                    parts = []
                    for step in range(LANES // ROWS):
                        tile = 2 * step + half
                        parts.append(xs[field, pl.ds(base, ROWS), tile * LANES : (tile + 1) * LANES] if tile < tiles else zero)
                    start = (field * PHASES + 2 * half) * width
                    nat[start : start + LANES, :] = jnp.concatenate(parts, axis=0).T

            def natural(field, phase, residue):
                return pl.ds((field * PHASES + phase) * width + residue, ROWS, stride=residues)

            moist_scale = moist_weight * scale
            wind_scale = 0.5 * dt
            before = []
            for phase in range(PHASES):
                sums = [jnp.zeros((ROWS, LANES), F32)] * 2
                for residue in range(residues):
                    theta, moist, wind = (nat[natural(field, phase, residue), :] for field in range(3))
                    scaled = (scale * (theta + moist), moist_scale * moist, wind_scale * wind)
                    for field in range(3):
                        s0[at(field, phase, residue)] = scaled[field]
                    sums = [sums[variable] + scaled[variable] for variable in range(2)]
                before.append(sums)

            def unit(index, inner):
                means = None
                for step in range(SUB):
                    means = substep(*((s0, s1) if step % 2 == 0 else (s1, s0)), means, step == SUB - 1)

                done = class_l == (index + 1).astype(F32)

                def keep(chunk, kept):
                    for residue in range(residues):
                        entry = chunk * residues + residue
                        saved[entry] = jnp.where(done, s0[entry], saved[entry])
                    return kept

                lax.fori_loop(0, jnp.where(mixed & (index + 1 < units), 3 * PHASES, 0), keep, 0)
                return inner

            lax.fori_loop(0, units, unit, 0)

            last = class_l == units.astype(F32)

            def restore(chunk, kept):
                for residue in range(residues):
                    entry = chunk * residues + residue
                    s0[entry] = jnp.where(last, s0[entry], saved[entry])
                return kept

            lax.fori_loop(0, jnp.where(mixed, 3 * PHASES, 0), restore, 0)
            heat_share = (2.0 / width) * steps * steps
            moist_share = heat_share * (1.0 / moist_weight)
            change = []
            for phase in range(PHASES):
                sums = [-value for value in before[phase]]
                for residue in range(residues):
                    sums = [sums[variable] + s0[at(variable, phase, residue)] for variable in range(2)]
                moist = moist_share * all_rows(sums[1])
                change.append((heat_share * all_rows(sums[0]) - moist, moist))

            active = class_m > 0.0
            second = lane_m >= levels
            level = jnp.where(second, lane_m - levels, lane_m)
            pick = jnp.minimum(level // PHASES * ROWS + sub_m, LANES - 1)
            which = lax.rem(level, PHASES)
            tendency = jnp.zeros((ROWS, LANES), F32)
            for phase in range(PHASES):
                found = [jnp.take_along_axis(change[phase][variable], pick, axis=1) for variable in range(2)]
                tendency = jnp.where(which == phase, jnp.where(second, found[1], found[0]), tendency)
            t_ref[pl.ds(base, ROWS), :] = jnp.where((lane_m < lane_class) & active, tendency, jnp.where(lane_m < lane_class, 0.0, mine))

        @pl.when(units <= 0)
        def _():
            t_ref[pl.ds(base, ROWS), :] = jnp.zeros((ROWS, LANES), F32)

        return carry

    lax.fori_loop(0, groups, run_group, 0)


def turned(fin, nat, group, field, width):
    residues = width // ROWS
    tiles = {}
    for half in range(2):
        for pair in range(2):
            phase = 2 * half + pair
            for residue in range(residues):
                spot = pl.ds(phase * width + residue, ROWS, stride=residues)
                nat[spot, :] = fin[group, (field * PHASES + phase) * residues + residue]
        back = nat[2 * half * width : 2 * half * width + LANES, :].T
        for step in range(LANES // ROWS):
            tiles[2 * step + half] = back[step * ROWS : (step + 1) * ROWS]
    return tiles


def weights_of(t_ref, base, lane_class):
    class_m = t_ref[pl.ds(base, ROWS), lane_class : lane_class + 1]
    steps = jnp.broadcast_to(jnp.maximum(class_m * SUB, 1.0), (ROWS, LANES))
    heat = 2.0 * steps * steps
    return class_m > 0.0, heat, heat * (1.0 / (1.0 - MOIST_BUOYANCY)), 2.0 * steps


def cloud_kernel(levels, width, workers, capacity, meta, fin, t_ref, water, *refs):
    outs = refs[:workers]
    cl, nat = refs[workers:]
    tiles = levels * width // LANES
    block = outs[0].shape[0] // capacity
    lane_m = iota((ROWS, LANES), 1)
    lane_class = lanes_of(levels)[0]
    me = lax.axis_index("crm")
    for group in range(fin.shape[0]):
        base = group * ROWS
        _, _, moist_weight, _ = weights_of(t_ref, base, lane_class)
        parts = turned(fin, nat.at[group], group, 1, width)
        for tile in range(tiles):
            value = moist_weight * parts[tile]
            level = (LANES // width) * tile + lane_m // width
            saturated = 1.0 - 2.0 * (level.astype(F32) + 0.5) / levels
            water[base : base + ROWS, tile * LANES : (tile + 1) * LANES] = value
            cl[pl.ds(base * block + tile, ROWS, stride=block), :] = jnp.maximum(value - saturated, 0.0)
    for distance in range(workers):
        first = (me ^ distance) * capacity
        for rank in range(capacity):
            source = pl.multiple_of(meta[4, first + rank] * block, ROWS)
            outs[distance][rank * block : (rank + 1) * block, :] = cl[pl.ds(source, block), :]


def state_kernel(slots, levels, width, columns, workers, meta, fin, t_ref, water, xs, *refs):
    inner_refs = refs[: workers + 3]
    y_hbm, inner, maps, ys, nat, sems = refs[workers + 3 :]
    groups = fin.shape[0]
    tiles = levels * width // LANES
    lane_class = lanes_of(levels)[0]
    copies = []
    for group in range(groups):
        base = group * ROWS
        active, heat_weight, _, wind_weight = weights_of(t_ref, base, lane_class)
        heats = turned(fin, nat.at[2 * group], group, 0, width)
        winds = turned(fin, nat.at[2 * group + 1], group, 2, width)
        for tile in range(tiles):
            lanes = slice(tile * LANES, (tile + 1) * LANES)
            moist = water[base : base + ROWS, lanes]
            values = (heat_weight * heats[tile] - moist, moist, wind_weight * winds[tile])
            for field in range(3):
                ys[field, base : base + ROWS, lanes] = jnp.where(active, values[field], xs[field, base : base + ROWS, lanes])
        for index in range(base, min(base + ROWS, slots)):
            copy = pltpu.make_async_copy(
                ys.at[:, pl.ds(index, 1), :], y_hbm.at[:, pl.ds(meta[0, index], 1), :], sems.at[index]
            )
            copy.start()
            copies.append(copy)
    inner_blocks(levels, columns, workers, *inner_refs, inner, maps)
    for copy in copies:
        copy.wait()


def small(name, mib=8, moved=1 << 20):
    cost = pl.CostEstimate(flops=0, bytes_accessed=moved, transcendentals=0)
    return dict(compiler_params=pltpu.CompilerParams(vmem_limit_bytes=mib * MIB), name=name, cost_estimate=cost)


def run_models(row_blocks, state, levels):
    workers = len(row_blocks)
    _, slots, cells = state.shape
    width = cells // levels
    groups = -(-slots // ROWS)
    padded = groups * ROWS
    vmem = pl.BlockSpec(memory_space=pltpu.VMEM)
    entries = 3 * PHASES * (width // ROWS)
    return pl.pallas_call(
        functools.partial(model_kernel, workers, slots, levels, width),
        out_shape=[
            jax.ShapeDtypeStruct((groups, entries, ROWS, LANES), F32),
            jax.ShapeDtypeStruct((3, padded, cells), F32),
            jax.ShapeDtypeStruct((padded, LANES), F32),
            jax.ShapeDtypeStruct((ROWS, LANES), jnp.int32),
        ],
        in_specs=[vmem] * workers + [pl.BlockSpec(memory_space=pl.ANY)],
        out_specs=[vmem] * 4,
        scratch_shapes=[
            pltpu.VMEM((3 * PHASES * width, LANES), F32),
            pltpu.VMEM((entries, ROWS, LANES), F32),
            pltpu.VMEM((entries, ROWS, LANES), F32),
            pltpu.VMEM((6 + 3 * PHASES, ROWS, LANES), F32),
            pltpu.VMEM((padded, LANES), F32),
            pltpu.SMEM((ROWS, LANES), jnp.int32),
            pltpu.SemaphoreType.DMA,
            pltpu.SemaphoreType.DMA((padded,)),
        ],
        **small("cloud_models", 12, 40 << 20),
    )(*row_blocks, state)


def condensate(workers, slots, cells, levels, meta, fin, tendency):
    groups = fin.shape[0]
    padded = groups * ROWS
    width = cells // levels
    capacity = slots // workers
    vmem = pl.BlockSpec(memory_space=pltpu.VMEM)
    block = -(-(cells // LANES) // ROWS) * ROWS
    outs = pl.pallas_call(
        functools.partial(cloud_kernel, levels, width, workers, capacity),
        out_shape=[jax.ShapeDtypeStruct((padded, cells), F32)]
        + [jax.ShapeDtypeStruct((capacity * block, LANES), F32)] * workers,
        in_specs=[pl.BlockSpec(memory_space=pltpu.SMEM), vmem, vmem],
        out_specs=[vmem] * (workers + 1),
        scratch_shapes=[pltpu.VMEM((padded * block, LANES), F32), pltpu.VMEM((groups, PHASES * width, LANES), F32)],
        **small("condensate", moved=8 << 20),
    )(meta, fin, tendency)
    return outs[0], outs[1:]


def state_rows(slots, levels, columns, meta, fin, tendency, water, start, tendencies, index, weight, level_map):
    width = fin.shape[1] // (3 * PHASES) * ROWS
    fields, padded, cells = start.shape
    vmem = pl.BlockSpec(memory_space=pltpu.VMEM)
    workers = len(tendencies)
    return pl.pallas_call(
        functools.partial(state_kernel, slots, levels, width, columns, workers),
        out_shape=[
            jax.ShapeDtypeStruct((fields, slots, cells), F32),
            jax.ShapeDtypeStruct((columns, LANES), F32),
            jax.ShapeDtypeStruct((2, LANES, level_map.shape[1]), F32),
        ],
        in_specs=[pl.BlockSpec(memory_space=pltpu.SMEM)] + [vmem] * (workers + 7),
        out_specs=[pl.BlockSpec(memory_space=pl.ANY), vmem, vmem],
        scratch_shapes=[
            pltpu.VMEM((fields, padded, cells), F32),
            pltpu.VMEM((2 * fin.shape[0], PHASES * width, LANES), F32),
            pltpu.SemaphoreType.DMA((slots,)),
        ],
        **small("state_rows", 12, moved=12 << 20),
    )(meta, fin, tendency, water, start, *tendencies, index, weight, level_map)


def edge_kernel(levels, columns, workers, *refs):
    t_refs, out = refs[:workers], refs[workers]
    _, _, lane_column, lane_owner = lanes_of(levels)
    me = lax.axis_index("crm")
    wanted = jnp.where(me == 0, workers - 1, 0).astype(F32)
    rows = jnp.concatenate([ref[...] for ref in t_refs], axis=0)
    lane = iota(rows.shape, 1).astype(F32)
    owner = rows[:, lane_owner : lane_owner + 1]
    column = rows[:, lane_column : lane_column + 1]
    select = ((owner == wanted) & (column == lane + 1.0)).astype(F32)
    out[...] = dot_t(select, rows)[:columns]


def share_rows(index, weight):
    rows = weight[...]
    total = jnp.sum(rows, axis=0, keepdims=True)
    return index[...].astype(F32), rows / total


def inner_blocks(levels, columns, workers, *refs):
    t_refs = refs[:workers]
    index, weight, level_map, inner, maps = refs[workers:]
    _, _, lane_column, lane_owner = lanes_of(levels)
    me = lax.axis_index("crm")
    rows = jnp.concatenate([ref[...] for ref in t_refs], axis=0)
    owner = rows[:, lane_owner : lane_owner + 1]
    column = rows[:, lane_column : lane_column + 1]
    block = owner - me.astype(F32) + 1.0
    named = (column > 0.0) & (block >= 0.0) & (block <= 2.0)
    ident = jnp.where(named, block * columns + column - 1.0, -1.0)
    wanted, share = share_rows(index, weight)
    mix = jnp.zeros((rows.shape[0], columns), F32)
    for source in range(index.shape[0]):
        mix = mix + jnp.where(ident == wanted[source : source + 1], share[source : source + 1], 0.0)
    inner[...] = dot_t(mix, rows)
    spread_row = iota((levels, LANES), 0)
    spread_lane = iota((levels, LANES), 1)
    for variable in range(2):
        place = (spread_lane == spread_row + variable * levels).astype(F32)
        maps[variable] = dot_t(place, level_map[...])


def finish_kernel(columns, capacity, workers, *refs):
    target = refs[0]
    received = refs[1 : workers + 1]
    inner, maps, edge, index, weight, cloud_hbm, physics_hbm, counts, column_of, places, cloud, physics, sems = refs[workers + 1 :]
    tiles = cloud.shape[1] // LANES
    block = -(-tiles // ROWS) * ROWS
    me = lax.axis_index("crm")
    for worker in range(workers):
        counts[worker] = 0
    for entry in range(workers * capacity):
        column_of[entry] = columns
    for column in range(columns):
        worker = target[column]
        rank = counts[worker]
        counts[worker] = rank + 1
        column_of[(worker ^ me) * capacity + rank] = column
    for distance in range(workers):
        for rank in range(capacity):
            place = pl.multiple_of(column_of[distance * capacity + rank] * block, ROWS)
            places[pl.ds(place, block), :] = received[distance][rank * block : (rank + 1) * block, :]
    chunk = ROWS if columns % ROWS == 0 else columns
    copies = []
    for base in range(0, columns, chunk):
        for tile in range(tiles):
            rows = places[pl.ds(base * block + tile, chunk, stride=block), :]
            cloud[base : base + chunk, tile * LANES : (tile + 1) * LANES] = rows
        copies.append(
            pltpu.make_async_copy(cloud.at[pl.ds(base, chunk), :], cloud_hbm.at[pl.ds(base, chunk), :], sems.at[len(copies)])
        )
        copies[-1].start()

    edge_sub = iota((columns, 1), 0)
    edge_block = jnp.where(me == 0, 0, jnp.where(me == workers - 1, 2, -3))
    ident = (edge_block * columns + edge_sub).astype(F32)
    wanted, share = share_rows(index, weight)
    mix = jnp.zeros((columns, columns), F32)
    for source in range(index.shape[0]):
        mix = mix + jnp.where(ident == wanted[source : source + 1], share[source : source + 1], 0.0)
    mixed = inner[...] + dot_t(mix, jnp.where(edge_block >= 0, edge[...], 0.0))
    for variable in range(2):
        physics[:, variable, :] = dot(mixed, maps[variable])
    copies.append(pltpu.make_async_copy(physics, physics_hbm, sems.at[len(copies)]))
    copies[-1].start()
    for copy in copies:
        copy.wait()


def exchange(blocks, axis):
    size = lax.axis_size(axis)
    out = [blocks[0]]
    for distance in range(1, size):
        out.append(lax.ppermute(blocks[distance], axis, [(i, i ^ distance) for i in range(size)]))
    return out


def spread(block, axis):
    bit = lax.axis_size(axis) // 2
    out = {0: block}
    while bit:
        pairs = [(i, i ^ bit) for i in range(lax.axis_size(axis))]
        out.update({known | bit: lax.ppermute(out[known], axis, pairs) for known in sorted(out)})
        bit //= 2
    return [out[distance] for distance in sorted(out)]


def body(crm_state, forcing, target, cost_class, level_map, remap_index, remap_weight):
    workers = lax.axis_size("crm")
    groups = lax.axis_size("grp")
    columns = forcing.shape[0]
    slots, _, cells = crm_state.shape
    capacity = slots // workers
    levels, gcm = level_map.shape
    vmem = pl.BlockSpec(memory_space=pltpu.VMEM)

    rows = pack(target, cost_class, forcing, level_map, workers, capacity)
    row_blocks = exchange([rows] * workers, "crm")
    fin, start, tendency, meta = run_models(row_blocks, in_hbm(crm_state.transpose(1, 0, 2)), levels)
    tendencies = spread(tendency, "crm")
    water, clouds = condensate(workers, slots, cells, levels, meta, fin, tendency)
    tendencies[2::2], clouds = lax.optimization_barrier((tendencies[2::2], clouds))
    clouds = exchange(clouds, "crm")

    edge = pl.pallas_call(
        functools.partial(edge_kernel, levels, columns, workers),
        out_shape=jax.ShapeDtypeStruct((columns, LANES), F32),
        in_specs=[vmem] * workers,
        out_specs=vmem,
        **small("edge_columns"),
    )(*tendencies)
    pairs = []
    for group in range(groups):
        after = (group + 1) % groups
        for worker in range(workers):
            ends = (group * workers + worker, after * workers + worker)
            pairs.append(ends if 2 * worker < workers else ends[::-1])
    edge, meta, tendencies = lax.optimization_barrier((edge, meta, tendencies))
    edge = lax.ppermute(edge, ("grp", "crm"), pairs)
    state, inner, maps = state_rows(
        slots, levels, columns, meta, fin, tendency, water, start, tendencies, remap_index.T, remap_weight.T, level_map
    )
    block = clouds[0].shape[0] // capacity
    cloud_water, physics = pl.pallas_call(
        functools.partial(finish_kernel, columns, capacity, workers),
        out_shape=[jax.ShapeDtypeStruct((columns, cells), F32), jax.ShapeDtypeStruct((columns, 2, gcm), F32)],
        in_specs=[pl.BlockSpec(memory_space=pltpu.SMEM)] + [vmem] * (workers + 5),
        out_specs=[pl.BlockSpec(memory_space=pl.ANY)] * 2,
        scratch_shapes=[
            pltpu.SMEM((workers,), jnp.int32),
            pltpu.SMEM((slots,), jnp.int32),
            pltpu.VMEM(((columns + 1) * block, LANES), F32),
            pltpu.VMEM((columns, cells), F32),
            pltpu.VMEM((columns, 2, gcm), F32),
            pltpu.SemaphoreType.DMA((-(-columns // ROWS) + 1,)),
        ],
        **small("columns_out"),
    )(target, *clouds, inner, maps, edge, remap_index.T, remap_weight.T)
    return state.transpose(1, 0, 2), cloud_water, physics


def solution(mesh):
    wide = P(("grp", "crm"), None, None)
    flat = P(("grp", "crm"), None)
    line = P(("grp", "crm"))
    in_specs = (wide, wide, line, line, P(), flat, flat)
    out_specs = (wide, flat, wide)
    return jax.shard_map(body, mesh=mesh, in_specs=in_specs, out_specs=out_specs, check_vma=False)
```
